128 devices in a mesh: section: 2 (over x_lo), dp: 16 (over z, y), ctx: 4 (over x_hi, core).
Axes of the slice: x: 4 (x_hi: 2, x_lo: 2; x = x_hi * 2 + x_lo), y: 4, z: 4, core: 2. Of those that a mesh axis runs over, the one named last changes fastest.
Arguments:
- ends_in: bfloat16 [2, 2, 16, 256, 1024], P('section', None, 'dp', 'ctx'), may hold values from -6 to 6
- lengths: int32 [2, 16, 3], P(None, 'dp'), may hold values from 1 to 224, 256 in all within a row
- qkv_w: float32 [2, 1024, 3072], P('section', 'dp'), may hold values from -0.1875 to 0.1875
- out_w: float32 [2, 1024, 1024], P('section', 'dp'), may hold values from -1.5 to 1.5
- gate_w: float32 [2, 1024, 2816], P('section', 'dp'), may hold values from -0.1875 to 0.1875
- up_w: float32 [2, 1024, 2816], P('section', 'dp'), may hold values from -0.1875 to 0.1875
- down_w: float32 [2, 2816, 1024], P('section', 'dp'), may hold values from -0.109375 to 0.109375
- gains: float32 [2, 2, 1024], P('section', None, 'dp'), may hold values from 0.5 to 1.5
Outputs:
- edges: bfloat16 [2, 2, 16, 256, 1024], P('section', None, 'dp', 'ctx')
- qkv_grad: float32 [2, 1024, 3072], P('section', 'dp')
- out_grad: float32 [2, 1024, 1024], P('section', 'dp')
- gate_grad: float32 [2, 1024, 2816], P('section', 'dp')
- up_grad: float32 [2, 1024, 2816], P('section', 'dp')
- down_grad: float32 [2, 2816, 1024], P('section', 'dp')
- gains_grad: float32 [2, 2, 1024], P('section', None, 'dp')
The draws below stay inside these ranges and needn't reach their ends.
Inputs may be any that keep to these rules, and one draw needn't show every extreme that they name: Each row of lengths holds 3 positive document lengths that sum to 256; the longest is exactly 224.
All inputs are finite; a program needn't handle non-finite values.
Results may differ from the reference program's by a relative error of at most 0.025.
Values may be sent and summed in bfloat16 or wider, within the bound.
A program may use at most 576 MiB of HBM per device.

```python
import math
import jax
import jax.numpy as jnp
import numpy as np
from jax import lax

D = 1024
FF = 2816
HEADS = 16
HEAD_DIM = 64
MB = 2
DOCS = 3
SEQ_LEN = 256
SEQS = 16
LONGEST = 224


def level_of(own_key, dims, pieces, smallest, top_value):
    loudness = 1.0
    for position, shards_of in pieces:
        steps = jax.random.uniform(jax.random.fold_in(jax.random.fold_in(own_key, 6), position), (shards_of,), jnp.float32, smallest / len(pieces), top_value / len(pieces))
        loudness = loudness * jnp.repeat(jnp.exp(steps), dims[position] // shards_of).reshape((-1,) + (1,) * (len(dims) - 1 - position))
    return loudness


def length_profile(number_of, total, limit, skew):
    loads = [(1 << 20) // math.isqrt(rank ** skew) + 1 for rank in range(2, number_of + 1)]
    spare, holding = total - limit - (number_of - 1), [1] * (number_of - 1)
    while spare > 0:
        movable = [i for i in range(number_of - 1) if holding[i] < limit]
        whole, remaining = sum([loads[i] for i in movable]), spare
        for i in movable:
            more = min(limit - holding[i], max(1, remaining * loads[i] // whole), spare)
            holding[i] = holding[i] + more
            spare = spare - more
    return np.array([limit] + holding)


def uneven(rng, number_of, total, bound, lean):
    if number_of == 2:
        one = jax.random.randint(rng, (), max(1, total - bound), min(bound, total - 1) + 1)
        return jnp.stack([one, total - one])
    tallies = jnp.asarray(length_profile(number_of, total, bound, lean), jnp.int32)
    pairs = (number_of - 1) // 2
    source_of, receiver = tallies[1:1 + 2 * pairs:2], tallies[2:2 + 2 * pairs:2]
    room = jnp.minimum(source_of - 1, bound - receiver)
    moved = jax.random.randint(jax.random.fold_in(rng, 1), (pairs,), 0, 1 << 20) % (room + 1)
    tallies = tallies.at[1:1 + 2 * pairs:2].set(source_of - moved).at[2:2 + 2 * pairs:2].set(receiver + moved)
    return tallies[jax.random.permutation(jax.random.fold_in(rng, 2), number_of)]


def scatter_about(rng, shape, width, limit, pieces=(), kind=jnp.bfloat16):
    gain = level_of(rng, shape, pieces, -0.22, 0.18) if pieces else 1.0
    entries = jax.random.normal(rng, shape, jnp.float32) * width * gain
    return jnp.minimum(jnp.maximum(entries, -limit), limit).astype(kind)


def setup_inputs(seed: int = 0) -> dict:
    arg_keys = jax.random.split(jax.random.key(seed), 9)
    ends_in = scatter_about(arg_keys[0], (2, MB, SEQS, SEQ_LEN, D), 1.0, 6.0, ((0, 2), (2, 16), (3, 4)))
    lengths = jax.vmap(lambda own: uneven(own, DOCS, SEQ_LEN, LONGEST, 2))(jax.random.split(arg_keys[1], MB * SEQS)).reshape((MB, SEQS, DOCS)).astype(jnp.int32)
    qkv_w = scatter_about(arg_keys[2], (2, D, 3 * D), D ** -0.5, 0.1875, ((0, 2), (1, 16)), jnp.float32)
    out_w = scatter_about(arg_keys[3], (2, D, D), 16 ** -0.5, 1.5, ((0, 2), (1, 16)), jnp.float32)
    gate_w = scatter_about(arg_keys[4], (2, D, FF), D ** -0.5, 0.1875, ((0, 2), (1, 16)), jnp.float32)
    up_w = scatter_about(arg_keys[5], (2, D, FF), D ** -0.5, 0.1875, ((0, 2), (1, 16)), jnp.float32)
    down_w = scatter_about(arg_keys[6], (2, FF, D), FF ** -0.5, 0.109375, ((0, 2), (1, 16)), jnp.float32)
    gains = jnp.clip(1.0 + 0.1 * jax.random.normal(arg_keys[7], (2, 2, D), jnp.float32), 0.5, 1.5)
    return {"ends_in": ends_in, "lengths": lengths, "qkv_w": qkv_w, "out_w": out_w, "gate_w": gate_w, "up_w": up_w, "down_w": down_w, "gains": gains}


epsilon = 1e-05
heads_per_block = 4

@jax.custom_vjp
def low(v):
    return lax.optimization_barrier(v.astype(jnp.bfloat16)).astype(jnp.float32)

@jax.custom_vjp
def low_back(v):
    return v

def low_keep(v):
    return (low(v), None)

def low_pass(kept, grad):
    return (grad,)

def back_keep(v):
    return (v, None)

def back_low(kept, grad):
    return (low(grad),)
low.defvjp(low_keep, low_pass)
low_back.defvjp(back_keep, back_low)

def matmul(left, right):
    return jnp.dot(left, right, precision=lax.Precision.HIGHEST, preferred_element_type=jnp.float32)

def rotary_tables(offsets):
    half_dim = HEAD_DIM // 2
    frequency = 10000.0 ** (-jnp.arange(half_dim, dtype=jnp.float32) / half_dim)
    phases = offsets.astype(jnp.float32)[:, None] * frequency[None, :]
    return (jnp.cos(phases)[:, None, :], jnp.sin(phases)[:, None, :])

def rotate(heads_in, cosine, sine_table):
    half_dim = heads_in.shape[-1] // 2
    front_half = heads_in[..., :half_dim]
    back_half = heads_in[..., half_dim:]
    return jnp.concatenate([front_half * cosine - back_half * sine_table, back_half * cosine + front_half * sine_table], axis=-1)

def layout(doc_lengths, token_index):
    doc_ends = jnp.cumsum(doc_lengths).astype(jnp.int32)
    doc_starts = doc_ends - doc_lengths
    inside = (token_index[:, None] >= doc_starts[None, :]) & (token_index[:, None] < doc_ends[None, :])
    doc_ids = lax.optimization_barrier(jnp.sum((token_index[:, None] >= doc_ends[None, :]).astype(jnp.int32), axis=1))
    offsets = token_index - lax.optimization_barrier(jnp.sum(jnp.where(inside, doc_starts[None, :], 0), axis=1)).astype(jnp.int32)
    return (doc_ids, offsets)

def attend_block(q_part, k_part, v_part, allowed):
    scores = low_back(jnp.einsum('qhd,khd->hqk', q_part, k_part, precision=lax.Precision.HIGHEST) * HEAD_DIM ** (-0.5))
    scores = jnp.where(allowed[None], scores, -1e+30)
    row_max = lax.optimization_barrier(jnp.max(scores, axis=-1, keepdims=True))
    shifted = jnp.exp(scores - row_max)
    weights = shifted / lax.optimization_barrier(jnp.sum(shifted, axis=-1, keepdims=True))
    return jnp.einsum('hqk,khd->qhd', low(weights), v_part, precision=lax.Precision.HIGHEST)

def attention(queries, key_rows, value_rows, allowed):
    row_count = queries.shape[0]
    blocks = HEADS // heads_per_block

    def split_heads(tensor):
        return tensor.reshape(row_count, blocks, heads_per_block, HEAD_DIM).transpose(1, 0, 2, 3)

    def one_block(operands):
        return attend_block(operands[0], operands[1], operands[2], allowed)
    attended = lax.map(jax.checkpoint(one_block), (split_heads(queries), split_heads(key_rows), split_heads(value_rows)))
    return attended.transpose(1, 0, 2, 3).reshape(row_count, D)

def layer_pass(weights, tokens_in, mixed_in, mix, allowed, cosine, sine_table):
    qkv_w, out_w, gate_w, up_w, down_w, gains = weights
    row_count = tokens_in.shape[0]
    inv_one = lax.rsqrt(lax.optimization_barrier(jnp.mean(tokens_in * tokens_in, axis=-1, keepdims=True)) + epsilon)
    normed = low(tokens_in * inv_one * gains[0])
    packed = low_back(matmul(normed, qkv_w))
    queries = rotate(packed[:, :D].reshape(row_count, HEADS, HEAD_DIM), cosine, sine_table).reshape(row_count, D)
    key_rows = rotate(packed[:, D:2 * D].reshape(row_count, HEADS, HEAD_DIM), cosine, sine_table).reshape(row_count, D)
    queries = low(low_back(queries))
    key_rows = low(low_back(key_rows))
    value_rows = low(low_back((1.0 - mix) * packed[:, 2 * D:] + mix * mixed_in))
    attended = low(low_back(attention(queries, key_rows, value_rows, allowed)))
    hidden = tokens_in + low_back(matmul(attended, out_w))
    inv_two = lax.rsqrt(lax.optimization_barrier(jnp.mean(hidden * hidden, axis=-1, keepdims=True)) + epsilon)
    normed_two = low(hidden * inv_two * gains[1])
    gate_act = low_back(matmul(normed_two, gate_w))
    up_act = low_back(matmul(normed_two, up_w))
    product = low(jax.nn.silu(gate_act) * up_act)
    return (hidden + low_back(matmul(product, down_w)), value_rows)

def network(masters, inputs, lengths):
    weights = tuple((low(master) for master in masters))
    front_weights = tuple((weight[0] for weight in weights))
    back_weights = tuple((weight[1] for weight in weights))
    token_index = jnp.arange(SEQ_LEN, dtype=jnp.int32)
    flat_inputs = inputs.reshape(MB * SEQS, SEQ_LEN, D)
    flat_lengths = lengths.reshape(MB * SEQS, DOCS)

    def one_buffer(unused_carry, buffer_item):
        tokens_in, doc_lengths = buffer_item
        doc_ids, offsets = layout(doc_lengths, token_index)
        allowed = (doc_ids[:, None] == doc_ids[None, :]) & (token_index[None, :] <= token_index[:, None])
        cosine, sine_table = rotary_tables(offsets)
        front_out, value_one = layer_pass(front_weights, tokens_in, jnp.zeros_like(tokens_in), 0.0, allowed, cosine, sine_table)
        front_out = low(low_back(front_out))
        back_out, unused_value = layer_pass(back_weights, front_out, low_back(value_one), 0.5, allowed, cosine, sine_table)
        return (unused_carry, back_out)
    unused_carry, outputs = lax.scan(one_buffer, jnp.zeros((), jnp.float32), (flat_inputs, flat_lengths))
    return outputs.reshape(MB, SEQS, SEQ_LEN, D)

def reference(ends_in, lengths, qkv_w, out_w, gate_w, up_w, down_w, gains):
    masters = (qkv_w, out_w, gate_w, up_w, down_w, gains)
    inputs = ends_in[0].astype(jnp.float32)
    cotangent = ends_in[1].astype(jnp.float32)

    def forward(master_set, input_set):
        return network(master_set, input_set, lengths)
    outputs, pullback = jax.vjp(forward, masters, inputs)
    grads, input_grad = pullback(cotangent)
    edges = jnp.stack([input_grad, outputs]).astype(jnp.bfloat16)
    return (edges, grads[0], grads[1], grads[2], grads[3], grads[4], grads[5])
```

```python
import jax
import jax.numpy as jnp
from jax import lax
from jax.experimental import pallas as pl
from jax.experimental.pallas import tpu as pltpu
from jax.sharding import PartitionSpec as P

T = 256
D = 1024
FF = 2816
FX = FF // 4
FP = 768
HX = 256
SH = 64
DR = 176
BT = 64
EPS = 1e-5
MESH = pl.DeviceIdType.MESH
BF = jnp.bfloat16
F32 = jnp.float32


def dot(a, b):
    return jnp.dot(a, b, preferred_element_type=F32)


def dot_nt(a, b):
    return lax.dot_general(a, b, (((1,), (1,)), ((), ())), preferred_element_type=F32)


def dot_tn(a, b):
    return lax.dot_general(a, b, (((0,), (0,)), ((), ())), preferred_element_type=F32)


N_SEM = 400
N_LOC = 24


def kernel(
    lengths, ends, q_src, o_src, gu_src, d_src, gain_src, cos_ref, sa_ref, sb_ref,
    oq_hbm, oo_hbm, ogu_hbm, od_hbm, edge_hbm, gsum_hbm,
    Wq, Wo, Wgu, Wd, Gn,
    E, X1, DY0, N1, N1s, N2, N2s, H, QKV, PR, O, Os, GU, M, Ms, DGU, DGUs, DP, DPs, DHB, DHBs, DYs, DH,
    PS, PRV,
    Gq, Go, Ggu, Gd, R1q, R1o, R1gu, R1d, R2q, R2o, R2gu, R2d, Sq, So, Sgu, Sd, OUTq, OUTo, OUTgu, OUTd,
    FSq, FSo, FSgu, FSd, GS, GR, TT, EO,
    ssem, rsem, lsem,
):
    s = lax.axis_index("section")
    dp = lax.axis_index("dp")
    c = lax.axis_index("ctx")
    xh = lax.div(c, 2)
    k = lax.rem(c, 2)
    x = xh * 2 + s
    z = lax.div(dp, 4)
    y = lax.rem(dp, 4)

    def dev(x_, y_, z_, k_):
        return (lax.rem(x_, 2), z_ * 4 + y_, lax.div(x_, 2) * 2 + k_)

    def ring(v):
        return [lax.rem(v + 1, 4), lax.rem(v + 3, 4), lax.rem(v + 2, 4)]

    X3, Y3, Z3 = ring(x), ring(y), ring(z)
    PX = [dev(v, y, z, k) for v in X3]
    PY = [dev(x, v, z, k) for v in Y3]
    PZ = [dev(x, y, v, k) for v in Z3]
    SIB = dev(x, y, z, 1 - k)

    bar = pltpu.get_barrier_semaphore()
    partners = PX + PY + PZ + [SIB]
    for p in partners:
        pl.semaphore_signal(bar, inc=1, device_id=p, device_id_type=MESH)
    pl.semaphore_wait(bar, len(partners))

    counter = [0, 0]
    sent = []

    def rc(src, dst, to, recv=None, cond=None, keep=True):
        i = counter[0]
        counter[0] += 1
        desc = pltpu.make_async_remote_copy(
            src_ref=src, dst_ref=dst, send_sem=ssem.at[i], recv_sem=rsem.at[i if recv is None else recv],
            device_id=to, device_id_type=MESH,
        )
        if keep:
            sent.append((cond, desc))
        return desc

    def push(src, dst, to):
        desc = rc(src, dst, to)
        desc.start()
        return desc

    def push3(srcs, dsts, to):
        return [push(a, b, t) for a, b, t in zip(srcs, dsts, to)]

    def wait_recv(descs):
        for desc in descs:
            desc.wait_recv()

    def flush():
        for cond, desc in sent:
            if cond is None:
                desc.wait_send()
            else:
                @pl.when(cond)
                def _(desc=desc):
                    desc.wait_send()
        sent.clear()

    def local(src, dst):
        i = counter[1]
        counter[1] += 1
        return pltpu.make_async_copy(src, dst, lsem.at[i])

    def half(width):
        return pl.ds(pl.multiple_of(k * (width // 2), 128), width // 2)

    def other_half(width):
        return pl.ds(pl.multiple_of((1 - k) * (width // 2), 128), width // 2)

    own = pl.ds(pl.multiple_of(x * BT, BT), BT)

    tx = lax.rem(x + 3 - 2 * k, 4)
    TO = dev(tx, y, z, k)
    REG = {"q": (Wq, 768), "o": (Wo, 1024), "gu": (Wgu, 2 * FP)}
    pre, loc = {}, {}

    def src_of(name, sl):
        if name == "q":
            return q_src.at[sl, :, half(768)]
        if name == "gu":
            return gu_src.at[sl, :, half(2 * FP)]
        return o_src.at[:, half(1024)]

    loc["g"] = local(gain_src, Gn.at[s, z, y])
    pre["g"] = rc(gain_src, Gn.at[s, z, y], TO)
    loc["g"].start()
    pre["g"].start()
    for name, (W, width) in REG.items():
        pre[name] = rc(src_of(name, tx), W.at[s, z, y, :, half(width)], TO)
        pre[name].start()
        loc[name] = local(src_of(name, x), W.at[s, z, y, :, half(width)])
        loc[name].start()
    down_rows = pl.ds(pl.multiple_of(y * DR, 16), DR)
    pre["d"] = rc(d_src.at[:, half(D)], Wd.at[s, down_rows, half(D)], TO, cond=(z == tx))
    loc["d"] = local(d_src.at[:, half(D)], Wd.at[s, down_rows, half(D)])

    @pl.when(z == tx)
    def _():
        pre["d"].start()

    @pl.when(z == x)
    def _():
        loc["d"].start()

    mine = pl.ds(pl.multiple_of(xh * 128 + k * 64, 64), 64)
    e_loc = local(ends.at[k], E.at[s, mine])
    e_loc.start()
    e_sib = push(ends.at[1 - k], E.at[s, mine], SIB)

    ag = {}

    def ready(l, name):
        @pl.when(s == l)
        def _():
            loc[name].wait()

        @pl.when(s != l)
        def _():
            pre[name].wait_recv()

    def ag1(l, name):
        if name == "d":
            descs = []
            for j in range(3):
                desc = rc(Wd.at[l, down_rows, half(D)], Wd.at[l, down_rows, half(D)], PZ[j],
                          recv=None if j == 0 else ag[l, "dz", "i"], cond=(z == x))
                if j == 0:
                    ag[l, "dz", "i"] = counter[0] - 1
                descs.append(desc)
            ag[l, "dz"] = descs

            @pl.when(z == x)
            def _():
                ready(l, "d")
                for desc in descs:
                    desc.start()
            return
        ready(l, name)
        if name == "g":
            ref = Gn.at[l, z, y]
            ag[l, name, 1] = (push3([ref] * 3, [ref] * 3, PY), [])
            return
        W, width = REG[name]
        a = W.at[l, z, y, pl.ds(0, 32), half(width)]
        b = W.at[l, z, y, pl.ds(32, 32), half(width)]
        ag[l, name, 1] = (push3([a] * 3, [a] * 3, PY), push3([b] * 3, [b] * 3, PZ))

    def ag2(l, name):
        if name == "d":
            @pl.when(z != x)
            def _():
                ag[l, "dz"][0].wait_recv()

            ref = Wd.at[l, down_rows, half(D)]
            ag[l, name, 2] = push3([ref] * 3, [ref] * 3, PY)
            return
        first = ag[l, name, 1]
        wait_recv(first[0])
        if name == "g":
            ref = Gn.at[l, z]
            ag[l, name, 2] = push3([ref] * 3, [ref] * 3, PZ)
            return
        W, width = REG[name]
        a = W.at[l, z, :, pl.ds(0, 32), half(width)]
        sent_a = push3([a] * 3, [a] * 3, PZ)
        wait_recv(first[1])
        b = W.at[l, :, y, pl.ds(32, 32), half(width)]
        ag[l, name, 2] = sent_a + push3([b] * 3, [b] * 3, PY)

    def ag3(l, name):
        wait_recv(ag[l, name, 2])
        if name == "g":
            return
        if name == "d":
            ref = Wd.at[l, pl.ds(0, FX), half(D)]
        else:
            W, width = REG[name]
            ref = W.at[l, :, :, :, half(width)]
        ag[l, name, 3] = push(ref, ref, SIB)

    def ag_done(l, name):
        wait_recv([ag[l, name, 3]])

    def gather_blocks(ref):
        return push3([ref] * 3, [ref] * 3, PX)

    def scatter_sums(i, value_of):
        for b in range(4):
            PS[i, b] = value_of(b)
        return push3([PS.at[i, v] for v in X3], [PRV.at[i, j] for j in range(3)], PX)

    def summed(i, descs):
        total = PS[i, x].astype(F32)
        for j, desc in enumerate(descs):
            desc.wait_recv()
            total = total + PRV[i, j].astype(F32)
        return total

    GRAD = {"q": (Gq, R1q, R2q, Sq, OUTq, FSq, 384), "o": (Go, R1o, R2o, So, OUTo, FSo, 128),
            "gu": (Ggu, R1gu, R2gu, Sgu, OUTgu, FSgu, FP)}
    rs = {}

    def rs1(l, name):
        if name == "d":
            rs[l, name, 1] = push3(
                [Gd.at[l, pl.ds(pl.multiple_of(v * DR, 16), DR)] for v in Y3], [R1d.at[l, j] for j in range(3)], PY)
            return
        G, R1, R2, S, OUT, FS, width = GRAD[name]
        a = push3([G.at[l, v, :, pl.ds(0, 32)] for v in Z3], [R1.at[l, 0, j] for j in range(3)], PZ)
        b = push3([G.at[l, :, v, pl.ds(32, 32)] for v in Y3], [R1.at[l, 1, j] for j in range(3)], PY)
        rs[l, name, 1] = (a, b)

    def rs2(l, name):
        first = rs[l, name, 1]
        if name == "d":
            wait_recv(first)
            Sd[l] = (Gd[l, down_rows].astype(F32) + R1d[l, 0].astype(F32) + R1d[l, 1].astype(F32)
                     + R1d[l, 2].astype(F32)).astype(BF)
            j_of = [lax.rem(x + 4 - z, 4) == 1, lax.rem(x + 4 - z, 4) == 3, lax.rem(x + 4 - z, 4) == 2]
            descs = []
            for j in range(3):
                desc = rc(Sd.at[l], R2d.at[l, j], PZ[j], cond=j_of[j])

                @pl.when(j_of[j])
                def _(desc=desc):
                    desc.start()
                descs.append(desc)
            rs[l, name, 2] = descs
            return
        G, R1, R2, S, OUT, FS, width = GRAD[name]
        wait_recv(first[0])
        S[l, 0] = (G[l, z, :, pl.ds(0, 32)].astype(F32) + R1[l, 0, 0].astype(F32) + R1[l, 0, 1].astype(F32)
                   + R1[l, 0, 2].astype(F32)).astype(BF)
        a = push3([S.at[l, 0, v] for v in Y3], [R2.at[l, 0, j] for j in range(3)], PY)
        wait_recv(first[1])
        S[l, 1] = (G[l, :, y, pl.ds(32, 32)].astype(F32) + R1[l, 1, 0].astype(F32) + R1[l, 1, 1].astype(F32)
                   + R1[l, 1, 2].astype(F32)).astype(BF)
        b = push3([S.at[l, 1, v] for v in Z3], [R2.at[l, 1, j] for j in range(3)], PZ)
        rs[l, name, 2] = (a, b)

    def rs3(l, name):
        second = rs[l, name, 2]
        if name == "d":
            idx = counter[0]
            far = rc(OUTd.at[k], OUTd.at[k], PX[2], cond=(z == x) & (s == l))
            near = [rc(FSd, OUTd.at[k], PX[j], recv=idx, cond=(z == x) & (s != l)) for j in range(2)]

            @pl.when(z == x)
            def _():
                wait_recv(second)
                total = (Sd[l].astype(F32) + R2d[l, 0].astype(F32) + R2d[l, 1].astype(F32)
                         + R2d[l, 2].astype(F32)).astype(BF)

                @pl.when(s == l)
                def _():
                    OUTd[k] = total
                    far.start()

                @pl.when(s != l)
                def _():
                    FSd[...] = total
                    for desc in near:
                        desc.start()
            rs[l, name, 3] = far
            return
        G, R1, R2, S, OUT, FS, width = GRAD[name]
        wait_recv(second[0])
        wait_recv(second[1])
        top = (S[l, 0, y].astype(F32) + R2[l, 0, 0].astype(F32) + R2[l, 0, 1].astype(F32)
               + R2[l, 0, 2].astype(F32)).astype(BF)
        low = (S[l, 1, z].astype(F32) + R2[l, 1, 0].astype(F32) + R2[l, 1, 1].astype(F32)
               + R2[l, 1, 2].astype(F32)).astype(BF)
        slot = OUT.at[k, x]
        far = rc(slot, slot, PX[2], cond=(s == l))
        near = [rc(FS, slot, PX[j], cond=(s != l)) for j in range(2)]

        @pl.when(s == l)
        def _():
            OUT[k, x, 0:32] = top
            OUT[k, x, 32:64] = low
            far.start()

        @pl.when(s != l)
        def _():
            FS[0:32] = top
            FS[32:64] = low
            for desc in near:
                desc.start()
        rs[l, name, 3] = [far] + near

    def rs4(l, name):
        third = rs[l, name, 3]
        if name == "d":
            ref = OUTd.at[k]
            fin = rc(ref, ref, SIB, cond=(s == l))

            @pl.when(s == l)
            def _():
                @pl.when(z != x)
                def _():
                    third.wait_recv()
                fin.start()
        else:
            ref = GRAD[name][4].at[k]
            fin = rc(ref, ref, SIB, cond=(s == l))

            @pl.when(s == l)
            def _():
                wait_recv(third)
                fin.start()
        rs[l, name, 4] = fin

    def rs5(l, name):
        @pl.when(s == l)
        def _():
            rs[l, name, 4].wait_recv()

    def edge(l, value):
        moved = rc(TT.at[l, s], TT.at[l, s], PX[0] if l == 1 else PX[1], cond=(s != l))
        TT[l, s] = value
        swap = rc(TT.at[l, 1 - k], EO.at[k], SIB, cond=(s == l))

        @pl.when(s != l)
        def _():
            moved.start()

        def finish():
            @pl.when(s == l)
            def _():
                moved.wait_recv()
                swap.start()
                EO[k] = TT[l, k]

        def done():
            @pl.when(s == l)
            def _():
                swap.wait_recv()
        return finish, done

    e0 = lengths[k, 0]
    e1 = e0 + lengths[k, 1]
    qi = lax.broadcasted_iota(jnp.int32, (T, T), 0)
    ki = lax.broadcasted_iota(jnp.int32, (T, T), 1)

    def doc(i):
        return jnp.where(i >= e0, 1, 0) + jnp.where(i >= e1, 1, 0)

    def allowed():
        return (doc(qi) == doc(ki)) & (ki <= qi)

    lane = lax.broadcasted_iota(jnp.int32, (T, 128), 1)

    def head(value, hh):
        return jnp.where((lane < 64) if hh == 0 else (lane >= 64), value, jnp.zeros_like(value))

    def rope(v):
        return v * cos_ref[...] + pltpu.roll(v, HX - 32, 1) * sa_ref[...] + pltpu.roll(v, 32, 1) * sb_ref[...]

    def rope_t(v):
        return v * cos_ref[...] - pltpu.roll(v, HX - 32, 1) * sa_ref[...] - pltpu.roll(v, 32, 1) * sb_ref[...]

    def gain(l, i):
        tiles = []
        for t in range(8):
            a = Gn[l, t // 2, 2 * (t % 2)].astype(F32) + Gn[l, t // 2, 2 * (t % 2) + 1].astype(F32)
            tiles.append(a[i : i + 1])
        return jnp.concatenate(tiles, axis=1)

    def mix(l):
        return 0.5 * l

    def norm_one(l, XR):
        g = gain(l, 0)
        for b in range(4):
            r = pl.ds(b * 64, 64)
            xf = XR[r, :].astype(F32)
            inv = lax.rsqrt(jnp.mean(xf * xf, axis=-1, keepdims=True) + EPS)
            N1[l, r, :] = (xf * inv * g).astype(BF)
        return push(N1.at[l], N1s.at[l], SIB)

    def wq(l):
        return Wq[l].reshape(D, 768)

    def project(l):
        n = N1[l]
        w = wq(l)
        QKV[l, 0] = rope(dot(n, w[:, 0:256])).astype(BF)
        QKV[l, 1] = rope(dot(n, w[:, 256:512])).astype(BF)
        v = dot(n, w[:, 512:768])
        if l == 1:
            v = 0.5 * v + 0.5 * QKV[0, 2].astype(F32)
        QKV[l, 2] = v.astype(BF)

    def attend(l):
        ok = allowed()
        for t in range(2):
            cols = pl.ds(128 * t, 128)
            qt, kt, vt = QKV[l, 0, :, cols], QKV[l, 1, :, cols], QKV[l, 2, :, cols]
            acc = jnp.zeros((T, 128), F32)
            for hh in range(2):
                sc = jnp.where(ok, dot_nt(head(qt, hh), kt) * 0.125, -1e30)
                ex = jnp.exp(sc - jnp.max(sc, axis=-1, keepdims=True))
                pr = (ex / jnp.sum(ex, axis=-1, keepdims=True)).astype(BF)
                PR[l, 2 * t + hh] = pr
                acc = acc + dot(pr, head(vt, hh))
            O[l, x, :, cols] = acc.astype(BF)
        got = gather_blocks(O.at[l, x])
        return got

    def hidden(l, XR, got):
        wait_recv(got)
        osib = push(O.at[l], Os.at[l], SIB)
        g = gain(l, 1)
        w = Wo[l].reshape(D, D)
        o = jnp.concatenate([O[l, b] for b in range(4)], axis=1)
        H[l] = XR[...].astype(F32) + dot(o, w)
        for b in range(4):
            r = pl.ds(b * 64, 64)
            hf = H[l, r, :]
            inv = lax.rsqrt(jnp.mean(hf * hf, axis=-1, keepdims=True) + EPS)
            N2[l, r, :] = (hf * inv * g).astype(BF)
        nsib = push(N2.at[l], N2s.at[l], SIB)
        return osib, nsib

    def gate_up(l):
        n = N2[l]
        GU[l, 0] = dot(n, Wgu[l, :, :, :, 0:FP].reshape(D, FP))
        GU[l, 1] = dot(n, Wgu[l, :, :, :, FP : 2 * FP].reshape(D, FP))
        for b in range(4):
            r = pl.ds(b * 64, 64)
            ga, up = GU[l, 0, r, :], GU[l, 1, r, :]
            M[l, r, :] = (ga * jax.nn.sigmoid(ga) * up).astype(BF)
        return push(M.at[l], Ms.at[l], SIB)

    def down(l, i):
        part = dot(M[l], Wd[l]).astype(BF)
        return scatter_sums(i, lambda b: part[b * 64 : (b + 1) * 64])

    def back_ff(l, DY, i):
        dy = DY[...]
        dm = dot_nt(dy, Wd[l])
        ga, up = GU[l, 0], GU[l, 1]
        sg = jax.nn.sigmoid(ga)
        DGU[l, 0] = (dm * up * sg * (1.0 + ga * (1.0 - sg))).astype(BF)
        DGU[l, 1] = (dm * ga * sg).astype(BF)
        sib = push(DGU.at[l, 1 - k], DGUs.at[l], SIB)
        part = (dot_nt(DGU[l, 0], Wgu[l, :, :, :, 0:FP].reshape(D, FP))
                + dot_nt(DGU[l, 1], Wgu[l, :, :, :, FP : 2 * FP].reshape(D, FP))).astype(BF)
        got = scatter_sums(i, lambda b: part[b * 64 : (b + 1) * 64])
        return sib, got

    def grads_ff(l, DY, msib, dysib, nsib, gsib):
        cols = half(D)
        wait_recv([msib, dysib])
        Gd[l] = (dot_tn(M[l], DY[:, cols]) + dot_tn(Ms[l], DYs[l])).astype(BF)
        rs1(l, "d")
        wait_recv([nsib, gsib])
        Ggu[l] = (dot_tn(N2[l], DGU[l, k]) + dot_tn(N2s[l], DGUs[l])).astype(BF).reshape(4, 4, SH, FP)
        rs1(l, "gu")

    def back_hidden(l, DY, i, got):
        dn = summed(i, got)
        hf = H[l, own, :]
        g = gain(l, 1)
        inv = lax.rsqrt(jnp.mean(hf * hf, axis=-1, keepdims=True) + EPS)
        GS[2 * l + 1 : 2 * l + 2] = jnp.sum(dn * hf * inv, axis=0, keepdims=True)
        e = dn * g
        dh = DY[own, :].astype(F32) + inv * e - hf * (inv * inv * inv) * jnp.mean(e * hf, axis=-1, keepdims=True)
        DH[l] = dh
        DHB[l, own, :] = dh.astype(BF)
        return gather_blocks(DHB.at[l, own])

    def back_attend(l, got, i):
        wait_recv(got)
        hs = pl.ds(pl.multiple_of(x * HX + (1 - k) * 128, 128), 128)
        hsib = push(DHB.at[l, :, hs], DHBs.at[l], SIB)
        do = dot_nt(DHB[l], Wo[l, x].reshape(HX, D)).astype(BF)
        dqs, dks, dvs = [], [], []
        for t in range(2):
            cols = pl.ds(128 * t, 128)
            qt, kt, vt = QKV[l, 0, :, cols], QKV[l, 1, :, cols], QKV[l, 2, :, cols]
            dot_ = do[:, 128 * t : 128 * (t + 1)]
            dq = dk = dv = jnp.zeros((T, 128), F32)
            for hh in range(2):
                pr = PR[l, 2 * t + hh]
                pf = pr.astype(F32)
                dom = head(dot_, hh)
                dpp = dot_nt(dom, vt)
                ds = (pf * (dpp - jnp.sum(pf * dpp, axis=-1, keepdims=True))).astype(BF)
                dq = dq + dot(ds, head(kt, hh))
                dk = dk + dot_tn(ds, head(qt, hh))
                dv = dv + dot_tn(pr, dom)
            dqs.append(dq)
            dks.append(dk)
            dvs.append(dv)
        dq = (jnp.concatenate(dqs, axis=1) * 0.125).astype(BF).astype(F32)
        dk = (jnp.concatenate(dks, axis=1) * 0.125).astype(BF).astype(F32)
        dv = jnp.concatenate(dvs, axis=1)
        DP[l, :, 0:256] = rope_t(dq).astype(BF)
        DP[l, :, 256:512] = rope_t(dk).astype(BF)
        if l == 1:
            dvt = dv.astype(BF)
            DP[l, :, 512:768] = (0.5 * dvt.astype(F32)).astype(BF)
        else:
            dvt = (dv + DP[1, :, 512:768].astype(F32)).astype(BF)
            DP[l, :, 512:768] = dvt
        psib = push(DP.at[l, :, other_half(768)], DPs.at[l], SIB)
        part = dot_nt(DP[l], wq(l)).astype(BF)
        got = scatter_sums(i, lambda b: part[b * 64 : (b + 1) * 64])
        return hsib, psib, got

    def grads_att(l, n1sib, osib, hsib, psib):
        wait_recv([n1sib, psib])
        Gq[l] = (dot_tn(N1[l], DP[l, :, half(768)]) + dot_tn(N1s[l], DPs[l])).astype(BF).reshape(4, 4, SH, 384)
        rs1(l, "q")
        wait_recv([osib, hsib])
        hs = pl.ds(pl.multiple_of(x * HX + k * 128, 128), 128)
        for b in range(4):
            Go[l, b] = (dot_tn(O[l, b], DHB[l, :, hs]) + dot_tn(Os[l, b], DHBs[l])).astype(BF).reshape(4, SH, 128)
        rs1(l, "o")

    def back_input(l, XR, i, got):
        dn = summed(i, got)
        xf = XR[own, :].astype(F32)
        g = gain(l, 0)
        inv = lax.rsqrt(jnp.mean(xf * xf, axis=-1, keepdims=True) + EPS)
        GS[2 * l : 2 * l + 1] = jnp.sum(dn * xf * inv, axis=0, keepdims=True)
        e = dn * g
        dx = DH[l] + inv * e - xf * (inv * inv * inv) * jnp.mean(e * xf, axis=-1, keepdims=True)
        return dx.astype(BF)

    X0 = E.at[0]
    DY1 = E.at[1]
    GS[...] = jnp.zeros_like(GS)
    for l in range(2):
        Wd[l, FX:FP, :] = jnp.zeros((FP - FX, D), BF)
    for name in ("g", "q", "o", "gu", "d"):
        ag1(0, name)
    e_loc.wait()
    e_sib.wait_recv()
    mine2 = pl.ds(pl.multiple_of(xh * 128, 128), 128)
    e_got = push3([E.at[s, mine2]] * 3, [E.at[s, mine2]] * 3, PX)
    ag2(0, "g")
    ag2(0, "q")
    ag2(0, "o")
    ag2(0, "gu")
    ag2(0, "d")
    ag3(0, "g")
    wait_recv(e_got)
    dysib = [None, push(DY1.at[:, other_half(D)], DYs.at[1], SIB)]
    n1sib = [norm_one(0, X0), None]
    ag3(0, "q")
    ag_done(0, "q")
    project(0)
    got = attend(0)
    for name in ("g", "q", "o", "gu", "d"):
        ag1(1, name)
    ag3(0, "o")
    ag3(0, "gu")
    ag3(0, "d")
    ag_done(0, "o")
    osib, nsib, msib = [None, None], [None, None], [None, None]
    osib[0], nsib[0] = hidden(0, X0, got)
    ag_done(0, "gu")
    msib[0] = gate_up(0)
    ag_done(0, "d")
    got = down(0, 0)
    for name in ("g", "q", "o", "gu", "d"):
        ag2(1, name)
    X1[own, :] = (summed(0, got) + H[0, own, :]).astype(BF)
    got = gather_blocks(X1.at[own])
    for name in ("g", "q", "o", "gu", "d"):
        ag3(1, name)
    wait_recv(got)
    n1sib[1] = norm_one(1, X1)
    ag_done(1, "q")
    project(1)
    got = attend(1)
    ag_done(1, "o")
    osib[1], nsib[1] = hidden(1, X1, got)
    ag_done(1, "gu")
    msib[1] = gate_up(1)
    ag_done(1, "d")
    y_got = down(1, 1)

    gsib, got = back_ff(1, DY1, 2)
    y_fin, y_done = edge(1, (summed(1, y_got) + H[1, own, :]).astype(BF))
    grads_ff(1, DY1, msib[1], dysib[1], nsib[1], gsib)
    got = back_hidden(1, DY1, 2, got)
    y_fin()
    hsib, psib, got = back_attend(1, got, 3)
    grads_att(1, n1sib[1], osib[1], hsib, psib)
    DY0[own, :] = back_input(1, X1, 3, got)
    got = gather_blocks(DY0.at[own])
    rs2(1, "d")
    rs2(1, "gu")
    wait_recv(got)
    dysib[0] = push(DY0.at[:, other_half(D)], DYs.at[0], SIB)

    gsib, got = back_ff(0, DY0, 4)
    rs2(1, "q")
    rs2(1, "o")
    grads_ff(0, DY0, msib[0], dysib[0], nsib[0], gsib)
    rs3(1, "d")
    rs3(1, "gu")
    got = back_hidden(0, DY0, 4, got)
    rs3(1, "q")
    rs3(1, "o")
    hsib, psib, got = back_attend(0, got, 5)
    rs2(0, "d")
    rs2(0, "gu")
    grads_att(0, n1sib[0], osib[0], hsib, psib)
    for name in ("d", "gu", "q", "o"):
        rs4(1, name)
    dx = back_input(0, X0, 5, got)
    x_fin, x_done = edge(0, dx)

    def gsum(i, to):
        descs = push3([GS] * len(to), [GR.at[i, j] for j in range(len(to))], to)
        for desc in descs:
            desc.wait()
        del sent[len(sent) - len(descs):]
        total = GS[...]
        for j in range(len(to)):
            total = total + GR[i, j]
        GS[...] = total

    gsum(0, PX)
    rs2(0, "q")
    rs2(0, "o")
    rs3(0, "d")
    rs3(0, "gu")
    gsum(1, PY)
    x_fin()
    gsum(2, PZ)
    rs3(0, "q")
    rs3(0, "o")
    gsum(3, [SIB])
    for name in ("d", "gu", "q", "o"):
        rs4(0, name)
    for name in ("d", "gu", "q", "o"):
        rs5(1, name)
        rs5(0, name)
    x_done()
    y_done()
    outs = [local(a, b) for a, b in
            ((OUTq, oq_hbm), (OUTo, oo_hbm), (OUTgu, ogu_hbm), (OUTd, od_hbm), (EO, edge_hbm), (GS, gsum_hbm))]
    for o in outs:
        o.start()
    flush()
    for o in outs:
        o.wait()


def run_kernel(lengths, ends, q_src, o_src, gu_src, d_src, gain_src, cos, sa, sb):
    V = pltpu.VMEM
    sh = jax.ShapeDtypeStruct
    any_ = pl.BlockSpec(memory_space=pl.ANY)
    vm = pl.BlockSpec(memory_space=pltpu.VMEM)
    out_shape = [
        sh((2, 4, SH, 384), BF), sh((2, 4, SH, 128), BF), sh((2, 4, SH, FP), BF), sh((2, DR, 512), BF),
        sh((2, BT, D), BF), sh((8, D), F32),
    ]
    scratch = [
        V((2, 4, 4, SH, 768), BF), V((2, 4, 4, SH, D), BF), V((2, 4, 4, SH, 2 * FP), BF), V((2, FP, D), BF),
        V((2, 4, 4, 16, 128), BF),
        V((2, T, D), BF), V((T, D), BF), V((T, D), BF),
        V((2, T, D), BF), V((2, T, D), BF), V((2, T, D), BF), V((2, T, D), BF),
        V((2, T, D), F32), V((2, 3, T, HX), BF), V((2, 4, T, T), BF),
        V((2, 4, T, HX), BF), V((2, 4, T, HX), BF),
        V((2, 2, T, FP), F32), V((2, T, FP), BF), V((2, T, FP), BF),
        V((2, 2, T, FP), BF), V((2, T, FP), BF),
        V((2, T, 768), BF), V((2, T, 384), BF),
        V((2, T, D), BF), V((2, T, 128), BF), V((2, T, 512), BF), V((2, BT, D), F32),
        V((6, 4, BT, D), BF), V((6, 3, BT, D), BF),
        V((2, 4, 4, SH, 384), BF), V((2, 4, 4, SH, 128), BF), V((2, 4, 4, SH, FP), BF), V((2, FP, 512), BF),
        V((2, 2, 3, 4, 32, 384), BF), V((2, 2, 3, 4, 32, 128), BF), V((2, 2, 3, 4, 32, FP), BF),
        V((2, 3, DR, 512), BF),
        V((2, 2, 3, 32, 384), BF), V((2, 2, 3, 32, 128), BF), V((2, 2, 3, 32, FP), BF), V((2, 3, DR, 512), BF),
        V((2, 2, 4, 32, 384), BF), V((2, 2, 4, 32, 128), BF), V((2, 2, 4, 32, FP), BF), V((2, DR, 512), BF),
        V((2, 4, SH, 384), BF), V((2, 4, SH, 128), BF), V((2, 4, SH, FP), BF), V((2, DR, 512), BF),
        V((SH, 384), BF), V((SH, 128), BF), V((SH, FP), BF), V((DR, 512), BF),
        V((8, D), F32), V((4, 3, 8, D), F32), V((2, 2, BT, D), BF), V((2, BT, D), BF),
        pltpu.SemaphoreType.DMA((N_SEM,)), pltpu.SemaphoreType.DMA((N_SEM,)), pltpu.SemaphoreType.DMA((N_LOC,)),
    ]
    return pl.pallas_call(
        kernel,
        out_shape=out_shape,
        in_specs=[pl.BlockSpec(memory_space=pltpu.SMEM)] + [any_] * 6 + [vm] * 3,
        out_specs=[any_] * 6,
        scratch_shapes=scratch,
        name="two_layers",
        compiler_params=pltpu.CompilerParams(
            collective_id=0, has_side_effects=True, vmem_limit_bytes=64 * 1024 * 1024 - 65536
        ),
    )(lengths, ends, q_src, o_src, gu_src, d_src, gain_src, cos, sa, sb)


def tables(doc_lengths):
    ends = jnp.cumsum(doc_lengths)
    i = jnp.arange(T, dtype=jnp.int32)
    start = jnp.where(i >= ends[1], ends[1], jnp.where(i >= ends[0], ends[0], 0))
    pos = (i - start).astype(F32)
    lane = jnp.arange(HX, dtype=jnp.int32) % 64
    freq = 10000.0 ** (-(lane % 32).astype(F32) / 32.0)
    phase = pos[:, None] * freq[None, :]
    cos, sin = jnp.cos(phase), jnp.sin(phase)
    first = (lane < 32)[None, :]
    return cos, jnp.where(first, -sin, 0.0), jnp.where(first, 0.0, sin)


def per_device(ends_in, lengths, qkv_w, out_w, gate_w, up_w, down_w, gains):
    s = lax.axis_index("section")
    d = lax.axis_index("dp")
    k = lax.rem(lax.axis_index("ctx"), 2)
    ends = ends_in[0, :, 0]
    doc = lengths[:, 0]
    q_src = qkv_w[0].astype(BF).reshape(SH, 3, 4, HX).transpose(2, 0, 1, 3).reshape(4, SH, 768)

    def ff_slices(w):
        return jnp.pad(w.astype(BF).reshape(SH, 4, FX), ((0, 0), (0, 0), (0, FP - FX))).transpose(1, 0, 2)

    gu_src = jnp.concatenate([ff_slices(gate_w[0]), ff_slices(up_w[0])], axis=2)
    o_src = out_w[0].astype(BF)
    d_src = down_w[0].astype(BF)
    gb = gains[0].astype(BF)
    odd = lax.rem(d, 2) == 1
    gain_src = jnp.where(odd, jnp.pad(gb, ((0, 14), (64, 0))), jnp.pad(gb, ((0, 14), (0, 64))))
    cos, sa, sb = tables(lax.dynamic_index_in_dim(doc, k, 0, keepdims=False))
    oq, oo, ogu, od, edge, gsum = run_kernel(doc, ends, q_src, o_src, gu_src, d_src, gain_src, cos, sa, sb)
    qkv = oq.transpose(2, 1, 0, 3).reshape(SH, 4, 3, HX).transpose(0, 2, 1, 3).reshape(SH, 3 * D).astype(F32)
    out = oo.transpose(2, 1, 0, 3).reshape(SH, D).astype(F32)
    gate = ogu[0].transpose(1, 0, 2)[:, :, :FX].reshape(SH, FF).astype(F32)
    up = ogu[1].transpose(1, 0, 2)[:, :, :FX].reshape(SH, FF).astype(F32)
    down = od.transpose(1, 0, 2).reshape(DR, D).astype(F32)
    gg = lax.dynamic_slice(gsum, (2 * s, d * SH), (2, SH))
    return edge[None, :, None], qkv[None], out[None], gate[None], up[None], down[None], gg[None]


def solution(mesh):
    in_specs = (
        P("section", None, "dp", "ctx", None),
        P(None, "dp", None),
        P("section", "dp", None),
        P("section", "dp", None),
        P("section", "dp", None),
        P("section", "dp", None),
        P("section", "dp", None),
        P("section", None, "dp"),
    )
    out_specs = (
        P("section", None, "dp", "ctx", None),
        P("section", "dp", None),
        P("section", "dp", None),
        P("section", "dp", None),
        P("section", "dp", None),
        P("section", "dp", None),
        P("section", None, "dp"),
    )
    return jax.shard_map(per_device, mesh=mesh, in_specs=in_specs, out_specs=out_specs, check_vma=False)
```

```python
import jax
import jax.numpy as jnp
from jax import lax
from jax.experimental import pallas as pl
from jax.experimental.pallas import tpu as pltpu
from jax.sharding import PartitionSpec as P

T = 256
D = 1024
FF = 2816
FX = FF // 4
FP = 768
HX = 256
SH = 64
DR = 176
BT = 64
EPS = 1e-5
MESH = pl.DeviceIdType.MESH
BF = jnp.bfloat16
F32 = jnp.float32


def dot(a, b):
    return jnp.dot(a, b, preferred_element_type=F32)


def dot_nt(a, b):
    return lax.dot_general(a, b, (((1,), (1,)), ((), ())), preferred_element_type=F32)


def dot_tn(a, b):
    return lax.dot_general(a, b, (((0,), (0,)), ((), ())), preferred_element_type=F32)


N_SEND = 64
N_RECV = 264
N_LOC = 12
GROUP_BYTES = 4 * 1024 * 1024


def kernel(
    lengths, ends, q_src, o_src, gu_src, d_src, gain_src, cos_ref, sa_ref, sb_ref,
    oq_hbm, oo_hbm, ogu_hbm, od_hbm, edge_hbm, gsum_hbm, dummy,
    Wq, Wo, Wgu, Wd, Gn,
    E, X1, DY0, N1, N1s, N2, N2s, H, QKV, PR, O, Os, GU, M, Ms, DGU, DGUs, DP, DPs, DHB, DHBs, DYs, DH,
    PS, PRV,
    Gq, Go, Ggu, Gd, R1q, R1o, R1gu, R1d, R2q, R2o, R2gu, R2d, Sq, So, Sgu, Sd, OUTq, OUTo, OUTgu, OUTd,
    FSq, FSo, FSgu, FSd, GS, GR, TT, EO,
    ssem, rsem, lsem,
):
    s = lax.axis_index("section")
    dp = lax.axis_index("dp")
    c = lax.axis_index("ctx")
    xh = lax.div(c, 2)
    k = lax.rem(c, 2)
    x = xh * 2 + s
    z = lax.div(dp, 4)
    y = lax.rem(dp, 4)

    def dev(x_, y_, z_, k_):
        return (lax.rem(x_, 2), z_ * 4 + y_, lax.div(x_, 2) * 2 + k_)

    def ring(v):
        return [lax.rem(v + 1, 4), lax.rem(v + 3, 4), lax.rem(v + 2, 4)]

    X3, Y3, Z3 = ring(x), ring(y), ring(z)
    PX = [dev(v, y, z, k) for v in X3]
    PY = [dev(x, v, z, k) for v in Y3]
    PZ = [dev(x, y, v, k) for v in Z3]
    SIB = dev(x, y, z, 1 - k)

    bar = pltpu.get_barrier_semaphore()
    partners = PX + PY + PZ + [SIB]
    for p in partners:
        pl.semaphore_signal(bar, inc=1, device_id=p, device_id_type=MESH)
    pl.semaphore_wait(bar, len(partners))

    counter = [0, 0, 0]
    sent = []
    groups = []

    def size(ref):
        n = 2 if ref.dtype == BF else 4
        for v in ref.shape:
            n *= v
        return n

    def new_recv():
        counter[0] += 1
        return counter[0] - 1

    def rc(src, dst, to, recv=None, cond=None):
        recv = new_recv() if recv is None else recv
        if cond is None:
            if not groups or groups[-1][1] + size(src) > GROUP_BYTES:
                groups.append([counter[2], 0])
                counter[2] += 1
            groups[-1][1] += size(src)
            i = groups[-1][0]
        else:
            i = counter[2]
            counter[2] += 1
        desc = pltpu.make_async_remote_copy(
            src_ref=src, dst_ref=dst, send_sem=ssem.at[i], recv_sem=rsem.at[recv],
            device_id=to, device_id_type=MESH,
        )
        if cond is not None:
            sent.append((cond, desc))
        return desc

    def push(src, dst, to, recv=None):
        desc = rc(src, dst, to, recv)
        desc.start()
        return desc

    def push3(srcs, dsts, to):
        return [push(a, b, t) for a, b, t in zip(srcs, dsts, to)]

    def wait_recv(descs):
        for desc in descs:
            desc.wait_recv()

    def wait_bytes(ref, recv):
        pltpu.make_async_remote_copy(
            src_ref=ref, dst_ref=ref, send_sem=ssem.at[0], recv_sem=rsem.at[recv], device_id=SIB, device_id_type=MESH,
        ).wait_recv()

    def flush():
        for i, total in groups:
            ref = dummy.at[pl.ds(0, total // 4096)]
            pltpu.make_async_copy(ref, ref, ssem.at[i]).wait()
        for cond, desc in sent:
            @pl.when(cond)
            def _(desc=desc):
                desc.wait_send()

    class Gather:
        def __init__(self, ring, blk, both):
            (self.p, self.m, self.o), self.me, self.P, self.M = ring
            self.blk, self.both = blk, both

        def a(self):
            self.r = [new_recv() for _ in range(3)]
            h0, h1 = self.blk(self.me, 0), self.blk(self.me, 1)
            push(h0, h0, self.P, self.r[0])
            push(h1, h1, self.M, self.r[1])
            push(h1, h1, self.P, self.r[2])
            push(h0, h0, self.M, self.r[2])
            return self

        def b(self):
            left, right = self.blk(self.m, 0), self.blk(self.p, 1)
            wait_bytes(left, self.r[0])
            push(left, left, self.P, self.r[2])
            wait_bytes(right, self.r[1])
            push(right, right, self.M, self.r[2])
            return self

        def c(self):
            wait_bytes(self.both, self.r[2])

    class Reduce:
        def __init__(self, ring, part, buf, both):
            (self.p, self.m, self.o), self.me, self.P, self.M = ring
            self.part, self.buf, self.both = part, buf, both

        def a(self):
            self.r = [new_recv() for _ in range(3)]
            part, buf = self.part, self.buf
            push(part(self.o, 0), buf(0, 0), self.P, self.r[0])
            push(part(self.o, 1), buf(0, 1), self.M, self.r[1])
            push(part(self.p, 1), buf(1, 1), self.P, self.r[2])
            push(part(self.m, 0), buf(2, 0), self.M, self.r[2])
            return self

        def b(self):
            part, buf = self.part, self.buf
            for h, j, to in ((0, self.p, self.P), (1, self.m, self.M)):
                ref, got = part(j, h), buf(0, h)
                wait_bytes(got, self.r[h])
                ref[...] = (ref[...].astype(F32) + got[...].astype(F32)).astype(BF)
                push(ref, buf(1 + h, h), to, self.r[2])
            return self

        def c(self):
            wait_bytes(self.both, self.r[2])

    RX = ((X3[0], X3[1], X3[2]), x, PX[0], PX[1])
    RY = ((Y3[0], Y3[1], Y3[2]), y, PY[0], PY[1])
    RZ = ((Z3[0], Z3[1], Z3[2]), z, PZ[0], PZ[1])

    def local(src, dst):
        i = counter[1]
        counter[1] += 1
        return pltpu.make_async_copy(src, dst, lsem.at[i])

    def half(width):
        return pl.ds(pl.multiple_of(k * (width // 2), 128), width // 2)

    def other_half(width):
        return pl.ds(pl.multiple_of((1 - k) * (width // 2), 128), width // 2)

    own = pl.ds(pl.multiple_of(x * BT, BT), BT)

    tx = lax.rem(x + 3 - 2 * k, 4)
    TO = dev(tx, y, z, k)
    REG = {"q": (Wq, 768), "o": (Wo, 1024), "gu": (Wgu, 2 * FP)}
    pre, loc = {}, {}

    def src_of(name, sl):
        if name == "q":
            return q_src.at[sl, :, half(768)]
        if name == "gu":
            return gu_src.at[sl, :, half(2 * FP)]
        return o_src.at[:, half(1024)]

    loc["g"] = local(gain_src, Gn.at[s, z, y])
    pre["g"] = rc(gain_src, Gn.at[s, z, y], TO)
    loc["g"].start()
    pre["g"].start()
    for name, (W, width) in REG.items():
        pre[name] = rc(src_of(name, tx), W.at[s, z, y, :, half(width)], TO)
        pre[name].start()
        loc[name] = local(src_of(name, x), W.at[s, z, y, :, half(width)])
        loc[name].start()
    down_rows = pl.ds(pl.multiple_of(y * DR, 16), DR)
    pre["d"] = rc(d_src.at[:, half(D)], Wd.at[s, down_rows, half(D)], TO, cond=(z == tx))
    loc["d"] = local(d_src.at[:, half(D)], Wd.at[s, down_rows, half(D)])

    @pl.when(z == tx)
    def _():
        pre["d"].start()

    @pl.when(z == x)
    def _():
        loc["d"].start()

    mine = pl.ds(pl.multiple_of(xh * 128 + k * 64, 64), 64)
    e_loc = local(ends.at[k], E.at[s, mine])
    e_loc.start()
    e_sib = push(ends.at[1 - k], E.at[s, mine], SIB)

    ag = {}

    def ready(l, name):
        @pl.when(s == l)
        def _():
            loc[name].wait()

        @pl.when(s != l)
        def _():
            pre[name].wait_recv()

    def rows16(base, h):
        return pl.ds(base + 16 * h, 16)

    def quarter(h):
        return pl.ds(pl.multiple_of(k * 512 + h * 256, 128), 256)

    is_src, is_p, is_m, is_f = z == x, z == X3[0], z == X3[1], z == X3[2]

    def s1a(l, name):
        if name == "d":
            ref = Wd.at[l, down_rows, half(D)]
            idx = new_recv()
            up = rc(ref, ref, PZ[0], recv=idx, cond=is_src)
            dn = rc(ref, ref, PZ[1], recv=idx, cond=is_src)

            @pl.when(is_src)
            def _():
                ready(l, "d")
                up.start()
                dn.start()
            ag[l, "d", 1] = up, idx
            return
        ready(l, name)
        if name == "g":
            ref = Gn.at[l, z, y]
            ag[l, name, 1] = new_recv()
            for to in PY:
                push(ref, ref, to, ag[l, name, 1])
            return
        W, width = REG[name]
        cols = half(width)
        ag[l, name, 1] = (
            Gather(RY, lambda j, h: W.at[l, z, j, rows16(0, h), cols], W.at[l, z, pl.ds(0, 2), pl.ds(0, 32), cols]).a(),
            Gather(RZ, lambda j, h: W.at[l, j, y, rows16(32, h), cols], W.at[l, pl.ds(0, 2), y, pl.ds(0, 32), cols]).a(),
        )

    def s1b(l, name):
        if name == "g":
            return
        first = ag[l, name, 1]
        if name == "d":
            got, idx = first
            h0, h1 = Wd.at[l, down_rows, quarter(0)], Wd.at[l, down_rows, quarter(1)]
            to_f = [rc(h0, h0, PZ[0], recv=idx, cond=is_p), rc(h1, h1, PZ[1], recv=idx, cond=is_m)]
            for cond, desc in zip((is_p, is_m), to_f):
                @pl.when(cond)
                def _(desc=desc):
                    got.wait_recv()
                    desc.start()
            return
        first[0].b()
        first[1].b()

    def s2a(l, name):
        first = ag[l, name, 1]
        if name == "g":
            wait_bytes(Gn.at[l, z, pl.ds(0, 3)], first)
            ref = Gn.at[l, z]
            ag[l, name, 2] = new_recv()
            for to in PZ:
                push(ref, ref, to, ag[l, name, 2])
            return
        if name == "d":
            @pl.when(is_f)
            def _():
                first[0].wait_recv()

            def blk(j, h):
                return Wd.at[l, pl.ds(pl.multiple_of(j * DR, 16), DR), quarter(h)]
            ag[l, name, 2] = (Gather(RY, blk, Wd.at[l, pl.ds(0, 2 * DR), half(D)]).a(),)
            return
        W, width = REG[name]
        cols = half(width)
        first[0].c()
        ga = Gather(RZ, lambda j, h: W.at[l, j, :, rows16(0, h), cols], W.at[l, pl.ds(0, 2), :, pl.ds(0, 32), cols]).a()
        first[1].c()
        gb = Gather(RY, lambda j, h: W.at[l, :, j, rows16(32, h), cols], W.at[l, :, pl.ds(0, 2), pl.ds(0, 32), cols]).a()
        ag[l, name, 2] = (ga, gb)

    def s2b(l, name):
        if name != "g":
            for g in ag[l, name, 2]:
                g.b()

    def s3(l, name):
        if name == "g":
            wait_bytes(Gn.at[l, pl.ds(0, 3)], ag[l, name, 2])
            return
        for g in ag[l, name, 2]:
            g.c()
        if name == "d":
            ref = Wd.at[l, pl.ds(0, FX), half(D)]
        else:
            W, width = REG[name]
            ref = W.at[l, :, :, :, half(width)]
        ag[l, name, 3] = push(ref, ref, SIB)

    def ag_done(l, name):
        wait_recv([ag[l, name, 3]])

    def gather_rows(ref):
        return Gather(RX, lambda j, h: ref.at[pl.ds(pl.multiple_of(j * BT + h * 32, 32), 32)], ref.at[pl.ds(0, 128)]).a()

    def gather_heads(l):
        return Gather(RX, lambda j, h: O.at[l, j, pl.ds(h * 128, 128)], O.at[l, pl.ds(0, 2)]).a()

    def scatter_sums(i, value_of):
        for b in range(4):
            PS[i, b] = value_of(b)
        return Reduce(RX, lambda j, h: PS.at[i, j, pl.ds(h * 32, 32)], lambda n, h: PRV.at[i, n, pl.ds(h * 32, 32)],
                      PRV.at[i, pl.ds(1, 2)]).a()

    def summed(i, red):
        red.c()
        return PS[i, x].astype(F32) + PRV[i, 1].astype(F32) + PRV[i, 2].astype(F32)

    GRAD = {"q": (Gq, R1q, R2q, Sq, OUTq, FSq, 384), "o": (Go, R1o, R2o, So, OUTo, FSo, 128),
            "gu": (Ggu, R1gu, R2gu, Sgu, OUTgu, FSgu, FP)}
    rs = {}

    def r1a(l, name):
        if name == "d":
            def part(j, h):
                return Gd.at[l, pl.ds(pl.multiple_of(j * DR, 16), DR), pl.ds(h * 256, 256)]
            rs[l, name, 1] = Reduce(RY, part, lambda n, h: R1d.at[l, n, :, pl.ds(h * 256, 256)], R1d.at[l, pl.ds(1, 2)]).a()
            return
        G, R1, R2, S, OUT, FS, width = GRAD[name]
        rs[l, name, 1] = (
            Reduce(RZ, lambda j, h: G.at[l, j, :, rows16(0, h)], lambda n, h: R1.at[l, 0, n, :, rows16(0, h)],
                   R1.at[l, 0, pl.ds(1, 2)]).a(),
            Reduce(RY, lambda j, h: G.at[l, :, j, rows16(32, h)], lambda n, h: R1.at[l, 1, n, :, rows16(0, h)],
                   R1.at[l, 1, pl.ds(1, 2)]).a(),
        )

    def r1b(l, name):
        first = rs[l, name, 1]
        if name == "d":
            first.b()
            return
        first[0].b()
        first[1].b()

    def r2a(l, name):
        first = rs[l, name, 1]
        if name == "d":
            first.c()
            Sd[l] = (Gd[l, down_rows].astype(F32) + R1d[l, 1].astype(F32) + R1d[l, 2].astype(F32)).astype(BF)
            idx = new_recv()
            to = [rc(Sd.at[l, :, pl.ds(0, 256)], R2d.at[l, 0, :, pl.ds(0, 256)], PZ[1], recv=idx, cond=is_f),
                  rc(Sd.at[l, :, pl.ds(256, 256)], R2d.at[l, 0, :, pl.ds(256, 256)], PZ[0], recv=idx, cond=is_f)]

            @pl.when(is_f)
            def _():
                to[0].start()
                to[1].start()
            rs[l, name, 2] = to
            return
        G, R1, R2, S, OUT, FS, width = GRAD[name]
        first[0].c()
        S[l, 0] = (G[l, z, :, pl.ds(0, 32)].astype(F32) + R1[l, 0, 1].astype(F32) + R1[l, 0, 2].astype(F32)).astype(BF)
        a = Reduce(RY, lambda j, h: S.at[l, 0, j, rows16(0, h)], lambda n, h: R2.at[l, 0, n, rows16(0, h)],
                   R2.at[l, 0, pl.ds(1, 2)]).a()
        first[1].c()
        S[l, 1] = (G[l, :, y, pl.ds(32, 32)].astype(F32) + R1[l, 1, 1].astype(F32) + R1[l, 1, 2].astype(F32)).astype(BF)
        b = Reduce(RZ, lambda j, h: S.at[l, 1, j, rows16(0, h)], lambda n, h: R2.at[l, 1, n, rows16(0, h)],
                   R2.at[l, 1, pl.ds(1, 2)]).a()
        rs[l, name, 2] = (a, b)

    def r2b(l, name):
        second = rs[l, name, 2]
        if name == "d":
            idx = [new_recv(), new_recv()]
            fin = [rc(Sd.at[l], R2d.at[l, 1], PZ[1], recv=idx[0], cond=is_p),
                   rc(Sd.at[l], R2d.at[l, 2], PZ[0], recv=idx[1], cond=is_m)]
            for cond, got, h, desc in ((is_p, second[0], 0, fin[0]), (is_m, second[1], 1, fin[1])):
                @pl.when(cond)
                def _(got=got, h=h, desc=desc):
                    got.wait_recv()
                    cols = pl.ds(256 * h, 256)
                    Sd[l, :, cols] = (Sd[l, :, cols].astype(F32) + R2d[l, 0, :, cols].astype(F32)).astype(BF)
                    desc.start()
            rs[l, name, 3] = fin
            return
        second[0].b()
        second[1].b()

    def rs3(l, name):
        idx = new_recv()
        if name == "d":
            fin = rs[l, name, 3]
            far = rc(OUTd.at[k], OUTd.at[k], PX[2], recv=idx, cond=is_src & (s == l))
            near = [rc(FSd, OUTd.at[k], PX[j], recv=idx, cond=is_src & (s != l)) for j in range(2)]

            @pl.when(is_src)
            def _():
                wait_recv(fin)
                total = (Sd[l].astype(F32) + R2d[l, 1].astype(F32) + R2d[l, 2].astype(F32)).astype(BF)

                @pl.when(s == l)
                def _():
                    OUTd[k] = total
                    far.start()

                @pl.when(s != l)
                def _():
                    FSd[...] = total
                    for desc in near:
                        desc.start()
            rs[l, name, 4] = far
            return
        G, R1, R2, S, OUT, FS, width = GRAD[name]
        second = rs[l, name, 2]
        second[0].c()
        second[1].c()
        top = (S[l, 0, y].astype(F32) + R2[l, 0, 1].astype(F32) + R2[l, 0, 2].astype(F32)).astype(BF)
        low = (S[l, 1, z].astype(F32) + R2[l, 1, 1].astype(F32) + R2[l, 1, 2].astype(F32)).astype(BF)
        slot = OUT.at[k, x]
        far = rc(slot, slot, PX[2], recv=idx, cond=(s == l))
        near = [rc(FS, slot, PX[j], recv=idx, cond=(s != l)) for j in range(2)]

        @pl.when(s == l)
        def _():
            OUT[k, x, 0:32] = top
            OUT[k, x, 32:64] = low
            far.start()

        @pl.when(s != l)
        def _():
            FS[0:32] = top
            FS[32:64] = low
            for desc in near:
                desc.start()
        rs[l, name, 4] = idx

    def rs4(l, name):
        got = rs[l, name, 4]
        ref = OUTd.at[k] if name == "d" else GRAD[name][4].at[k]
        fin = rc(ref, ref, SIB, cond=(s == l))

        @pl.when(s == l)
        def _():
            if name == "d":
                @pl.when(z != x)
                def _():
                    got.wait_recv()
            else:
                wait_bytes(GRAD[name][4].at[k, pl.ds(0, 3)], got)
            fin.start()
        rs[l, name, 5] = fin

    def rs5(l, name):
        @pl.when(s == l)
        def _():
            rs[l, name, 5].wait_recv()

    def edge(l, value):
        moved = rc(TT.at[l, s], TT.at[l, s], PX[0] if l == 1 else PX[1], cond=(s != l))
        TT[l, s] = value
        swap = rc(TT.at[l, 1 - k], EO.at[k], SIB, cond=(s == l))

        @pl.when(s != l)
        def _():
            moved.start()

        def finish():
            @pl.when(s == l)
            def _():
                moved.wait_recv()
                swap.start()
                EO[k] = TT[l, k]

        def done():
            @pl.when(s == l)
            def _():
                swap.wait_recv()
        return finish, done

    e0 = lengths[k, 0]
    e1 = e0 + lengths[k, 1]
    qi = lax.broadcasted_iota(jnp.int32, (T, T), 0)
    ki = lax.broadcasted_iota(jnp.int32, (T, T), 1)

    def doc(i):
        return jnp.where(i >= e0, 1, 0) + jnp.where(i >= e1, 1, 0)

    def allowed():
        return (doc(qi) == doc(ki)) & (ki <= qi)

    lane = lax.broadcasted_iota(jnp.int32, (T, 128), 1)

    def head(value, hh):
        return jnp.where((lane < 64) if hh == 0 else (lane >= 64), value, jnp.zeros_like(value))

    def rope(v):
        return v * cos_ref[...] + pltpu.roll(v, HX - 32, 1) * sa_ref[...] + pltpu.roll(v, 32, 1) * sb_ref[...]

    def rope_t(v):
        return v * cos_ref[...] - pltpu.roll(v, HX - 32, 1) * sa_ref[...] - pltpu.roll(v, 32, 1) * sb_ref[...]

    def gain(l, i):
        tiles = []
        for t in range(8):
            a = Gn[l, t // 2, 2 * (t % 2)].astype(F32) + Gn[l, t // 2, 2 * (t % 2) + 1].astype(F32)
            tiles.append(a[i : i + 1])
        return jnp.concatenate(tiles, axis=1)

    def mix(l):
        return 0.5 * l

    def norm_one(l, XR):
        g = gain(l, 0)
        for b in range(4):
            r = pl.ds(b * 64, 64)
            xf = XR[r, :].astype(F32)
            inv = lax.rsqrt(jnp.mean(xf * xf, axis=-1, keepdims=True) + EPS)
            N1[l, r, :] = (xf * inv * g).astype(BF)
        return push(N1.at[l], N1s.at[l], SIB)

    def wq(l):
        return Wq[l].reshape(D, 768)

    def project(l):
        n = N1[l]
        w = wq(l)
        QKV[l, 0] = rope(dot(n, w[:, 0:256])).astype(BF)
        QKV[l, 1] = rope(dot(n, w[:, 256:512])).astype(BF)
        v = dot(n, w[:, 512:768])
        if l == 1:
            v = 0.5 * v + 0.5 * QKV[0, 2].astype(F32)
        QKV[l, 2] = v.astype(BF)

    def attend(l):
        ok = allowed()
        for t in range(2):
            cols = pl.ds(128 * t, 128)
            qt, kt, vt = QKV[l, 0, :, cols], QKV[l, 1, :, cols], QKV[l, 2, :, cols]
            acc = jnp.zeros((T, 128), F32)
            for hh in range(2):
                sc = jnp.where(ok, dot_nt(head(qt, hh), kt) * 0.125, -1e30)
                ex = jnp.exp(sc - jnp.max(sc, axis=-1, keepdims=True))
                pr = (ex / jnp.sum(ex, axis=-1, keepdims=True)).astype(BF)
                PR[l, 2 * t + hh] = pr
                acc = acc + dot(pr, head(vt, hh))
            O[l, x, :, cols] = acc.astype(BF)
        return gather_heads(l)

    def hidden(l, XR, got):
        got.c()
        osib = push(O.at[l], Os.at[l], SIB)
        g = gain(l, 1)
        w = Wo[l].reshape(D, D)
        o = jnp.concatenate([O[l, b] for b in range(4)], axis=1)
        H[l] = XR[...].astype(F32) + dot(o, w)
        for b in range(4):
            r = pl.ds(b * 64, 64)
            hf = H[l, r, :]
            inv = lax.rsqrt(jnp.mean(hf * hf, axis=-1, keepdims=True) + EPS)
            N2[l, r, :] = (hf * inv * g).astype(BF)
        nsib = push(N2.at[l], N2s.at[l], SIB)
        return osib, nsib

    def gate_up(l):
        n = N2[l]
        GU[l, 0] = dot(n, Wgu[l, :, :, :, 0:FP].reshape(D, FP))
        GU[l, 1] = dot(n, Wgu[l, :, :, :, FP : 2 * FP].reshape(D, FP))
        for b in range(4):
            r = pl.ds(b * 64, 64)
            ga, up = GU[l, 0, r, :], GU[l, 1, r, :]
            M[l, r, :] = (ga * jax.nn.sigmoid(ga) * up).astype(BF)
        return push(M.at[l], Ms.at[l], SIB)

    def down(l, i):
        part = dot(M[l], Wd[l]).astype(BF)
        return scatter_sums(i, lambda b: part[b * 64 : (b + 1) * 64])

    def back_ff(l, DY, i):
        dy = DY[...]
        dm = dot_nt(dy, Wd[l])
        ga, up = GU[l, 0], GU[l, 1]
        sg = jax.nn.sigmoid(ga)
        DGU[l, 0] = (dm * up * sg * (1.0 + ga * (1.0 - sg))).astype(BF)
        DGU[l, 1] = (dm * ga * sg).astype(BF)
        sib = push(DGU.at[l, 1 - k], DGUs.at[l], SIB)
        part = (dot_nt(DGU[l, 0], Wgu[l, :, :, :, 0:FP].reshape(D, FP))
                + dot_nt(DGU[l, 1], Wgu[l, :, :, :, FP : 2 * FP].reshape(D, FP))).astype(BF)
        got = scatter_sums(i, lambda b: part[b * 64 : (b + 1) * 64])
        return sib, got

    def grads_d(l, DY, msib, dysib):
        wait_recv([msib, dysib])
        Gd[l] = (dot_tn(M[l], DY[:, half(D)]) + dot_tn(Ms[l], DYs[l])).astype(BF)
        r1a(l, "d")

    def grads_gu(l, nsib, gsib):
        wait_recv([nsib, gsib])
        Ggu[l] = (dot_tn(N2[l], DGU[l, k]) + dot_tn(N2s[l], DGUs[l])).astype(BF).reshape(4, 4, SH, FP)
        r1a(l, "gu")

    def back_hidden(l, DY, i, got):
        dn = summed(i, got)
        hf = H[l, own, :]
        g = gain(l, 1)
        inv = lax.rsqrt(jnp.mean(hf * hf, axis=-1, keepdims=True) + EPS)
        GS[0, 2 * l + 1 : 2 * l + 2] = jnp.sum(dn * hf * inv, axis=0, keepdims=True)
        e = dn * g
        dh = DY[own, :].astype(F32) + inv * e - hf * (inv * inv * inv) * jnp.mean(e * hf, axis=-1, keepdims=True)
        DH[l] = dh
        DHB[l, own, :] = dh.astype(BF)
        return gather_rows(DHB.at[l])

    def back_attend(l, got, i):
        got.c()
        hs = pl.ds(pl.multiple_of(x * HX + (1 - k) * 128, 128), 128)
        hsib = push(DHB.at[l, :, hs], DHBs.at[l], SIB)
        do = dot_nt(DHB[l], Wo[l, x].reshape(HX, D)).astype(BF)
        dqs, dks, dvs = [], [], []
        for t in range(2):
            cols = pl.ds(128 * t, 128)
            qt, kt, vt = QKV[l, 0, :, cols], QKV[l, 1, :, cols], QKV[l, 2, :, cols]
            dot_ = do[:, 128 * t : 128 * (t + 1)]
            dq = dk = dv = jnp.zeros((T, 128), F32)
            for hh in range(2):
                pr = PR[l, 2 * t + hh]
                pf = pr.astype(F32)
                dom = head(dot_, hh)
                dpp = dot_nt(dom, vt)
                ds = (pf * (dpp - jnp.sum(pf * dpp, axis=-1, keepdims=True))).astype(BF)
                dq = dq + dot(ds, head(kt, hh))
                dk = dk + dot_tn(ds, head(qt, hh))
                dv = dv + dot_tn(pr, dom)
            dqs.append(dq)
            dks.append(dk)
            dvs.append(dv)
        dq = (jnp.concatenate(dqs, axis=1) * 0.125).astype(BF).astype(F32)
        dk = (jnp.concatenate(dks, axis=1) * 0.125).astype(BF).astype(F32)
        dv = jnp.concatenate(dvs, axis=1)
        DP[l, :, 0:256] = rope_t(dq).astype(BF)
        DP[l, :, 256:512] = rope_t(dk).astype(BF)
        if l == 1:
            dvt = dv.astype(BF)
            DP[l, :, 512:768] = (0.5 * dvt.astype(F32)).astype(BF)
        else:
            dvt = (dv + DP[1, :, 512:768].astype(F32)).astype(BF)
            DP[l, :, 512:768] = dvt
        psib = push(DP.at[l, :, other_half(768)], DPs.at[l], SIB)
        part = dot_nt(DP[l], wq(l)).astype(BF)
        got = scatter_sums(i, lambda b: part[b * 64 : (b + 1) * 64])
        return hsib, psib, got

    def grads_q(l, n1sib, psib):
        wait_recv([n1sib, psib])
        Gq[l] = (dot_tn(N1[l], DP[l, :, half(768)]) + dot_tn(N1s[l], DPs[l])).astype(BF).reshape(4, 4, SH, 384)
        r1a(l, "q")

    def grads_o(l, osib, hsib):
        wait_recv([osib, hsib])
        hs = pl.ds(pl.multiple_of(x * HX + k * 128, 128), 128)
        for b in range(4):
            Go[l, b] = (dot_tn(O[l, b], DHB[l, :, hs]) + dot_tn(Os[l, b], DHBs[l])).astype(BF).reshape(4, SH, 128)
        r1a(l, "o")

    def back_input(l, XR, i, got):
        dn = summed(i, got)
        xf = XR[own, :].astype(F32)
        g = gain(l, 0)
        inv = lax.rsqrt(jnp.mean(xf * xf, axis=-1, keepdims=True) + EPS)
        GS[0, 2 * l : 2 * l + 1] = jnp.sum(dn * xf * inv, axis=0, keepdims=True)
        e = dn * g
        dx = DH[l] + inv * e - xf * (inv * inv * inv) * jnp.mean(e * xf, axis=-1, keepdims=True)
        return dx.astype(BF)

    def gsum_a(i, to):
        idx = new_recv()
        for j, t in enumerate(to):
            push(GS.at[i], GR.at[i, j], t, idx)
        return i, len(to), idx

    def gsum_b(sent_to):
        i, n, idx = sent_to
        wait_bytes(GR.at[i, pl.ds(0, n)], idx)
        total = GS[i]
        for j in range(n):
            total = total + GR[i, j]
        GS[i + 1] = total

    X0 = E.at[0]
    DY1 = E.at[1]
    NAMES = ("g", "q", "o", "gu", "d")
    GS[0] = jnp.zeros((8, D), F32)
    for l in range(2):
        Wd[l, FX:FP, :] = jnp.zeros((FP - FX, D), BF)
    for name in NAMES:
        s1a(0, name)
    e_loc.wait()
    e_sib.wait_recv()
    mine2 = pl.ds(pl.multiple_of(xh * 128, 128), 128)
    e_got = push3([E.at[s, mine2]] * 3, [E.at[s, mine2]] * 3, PX)
    for name in NAMES:
        s1b(0, name)
    for name in NAMES:
        s1a(1, name)
    s2a(0, "g")
    s2a(0, "q")
    s2a(0, "o")
    s2a(0, "gu")
    s3(0, "g")
    wait_recv(e_got)
    dysib = [None, push(DY1.at[:, other_half(D)], DYs.at[1], SIB)]
    n1sib = [norm_one(0, X0), None]
    s2b(0, "q")
    s2a(0, "d")
    s2b(0, "o")
    s3(0, "q")
    s2b(0, "gu")
    for name in NAMES:
        s1b(1, name)
    ag_done(0, "q")
    project(0)
    s2b(0, "d")
    s3(0, "o")
    got = attend(0)
    s2a(1, "g")
    s2a(1, "q")
    got.b()
    s3(0, "gu")
    s2a(1, "o")
    s2a(1, "gu")
    s3(0, "d")
    ag_done(0, "o")
    osib, nsib, msib = [None, None], [None, None], [None, None]
    osib[0], nsib[0] = hidden(0, X0, got)
    s2b(1, "q")
    ag_done(0, "gu")
    msib[0] = gate_up(0)
    s2a(1, "d")
    s2b(1, "o")
    ag_done(0, "d")
    got = down(0, 0)
    s2b(1, "gu")
    s3(1, "g")
    s3(1, "q")
    got.b()
    s2b(1, "d")
    s3(1, "o")
    X1[own, :] = (summed(0, got) + H[0, own, :]).astype(BF)
    got = gather_rows(X1)
    s3(1, "gu")
    got.b()
    s3(1, "d")
    got.c()
    n1sib[1] = norm_one(1, X1)
    ag_done(1, "q")
    project(1)
    got = attend(1)
    got.b()
    ag_done(1, "o")
    osib[1], nsib[1] = hidden(1, X1, got)
    ag_done(1, "gu")
    msib[1] = gate_up(1)
    ag_done(1, "d")
    y_red = down(1, 1)

    gsib, got = back_ff(1, DY1, 2)
    y_red.b()
    grads_d(1, DY1, msib[1], dysib[1])
    got.b()
    grads_gu(1, nsib[1], gsib)
    y_fin, y_done = edge(1, (summed(1, y_red) + H[1, own, :]).astype(BF))
    got = back_hidden(1, DY1, 2, got)
    r1b(1, "d")
    got.b()
    hsib, psib, got = back_attend(1, got, 3)
    grads_q(1, n1sib[1], psib)
    got.b()
    grads_o(1, osib[1], hsib)
    r1b(1, "gu")
    r2a(1, "d")
    DY0[own, :] = back_input(1, X1, 3, got)
    got = gather_rows(DY0)
    y_fin()
    r1b(1, "q")
    got.b()
    r1b(1, "o")
    r2a(1, "gu")
    r2b(1, "d")
    got.c()
    dysib[0] = push(DY0.at[:, other_half(D)], DYs.at[0], SIB)

    gsib, got = back_ff(0, DY0, 4)
    grads_d(0, DY0, msib[0], dysib[0])
    got.b()
    r2a(1, "q")
    r2a(1, "o")
    grads_gu(0, nsib[0], gsib)
    r2b(1, "gu")
    rs3(1, "d")
    got = back_hidden(0, DY0, 4, got)
    r1b(0, "d")
    got.b()
    r2b(1, "q")
    r2b(1, "o")
    hsib, psib, got = back_attend(0, got, 5)
    grads_q(0, n1sib[0], psib)
    got.b()
    grads_o(0, osib[0], hsib)
    r1b(0, "gu")
    r2a(0, "d")
    rs3(1, "gu")
    rs3(1, "q")
    rs3(1, "o")
    dx = back_input(0, X0, 5, got)
    x_fin, x_done = edge(0, dx)
    g0 = gsum_a(0, PX)
    r1b(0, "q")
    r1b(0, "o")
    r2a(0, "gu")
    r2b(0, "d")
    gsum_b(g0)
    g0 = gsum_a(1, PY)
    x_fin()
    for name in ("d", "gu", "q", "o"):
        rs4(1, name)
    r2a(0, "q")
    r2a(0, "o")
    gsum_b(g0)
    g0 = gsum_a(2, PZ)
    rs3(0, "d")
    r2b(0, "gu")
    r2b(0, "q")
    r2b(0, "o")
    gsum_b(g0)
    g0 = gsum_a(3, [SIB])
    rs3(0, "gu")
    rs3(0, "q")
    rs3(0, "o")
    gsum_b(g0)
    for name in ("d", "gu", "q", "o"):
        rs4(0, name)
    for name in ("d", "gu", "q", "o"):
        rs5(1, name)
        rs5(0, name)
    x_done()
    y_done()
    outs = [local(a, b) for a, b in
            ((OUTq, oq_hbm), (OUTo, oo_hbm), (OUTgu, ogu_hbm), (OUTd, od_hbm), (EO, edge_hbm), (GS.at[4], gsum_hbm))]
    for o in outs:
        o.start()
    flush()
    for o in outs:
        o.wait()
    assert counter[0] <= N_RECV and counter[1] <= N_LOC and counter[2] <= N_SEND, counter


def run_kernel(lengths, ends, q_src, o_src, gu_src, d_src, gain_src, cos, sa, sb):
    V = pltpu.VMEM
    sh = jax.ShapeDtypeStruct
    any_ = pl.BlockSpec(memory_space=pl.ANY)
    vm = pl.BlockSpec(memory_space=pltpu.VMEM)
    out_shape = [
        sh((2, 4, SH, 384), BF), sh((2, 4, SH, 128), BF), sh((2, 4, SH, FP), BF), sh((2, DR, 512), BF),
        sh((2, BT, D), BF), sh((8, D), F32), sh((GROUP_BYTES // 4096, 16, 128), BF),
    ]
    scratch = [
        V((2, 4, 4, SH, 768), BF), V((2, 4, 4, SH, D), BF), V((2, 4, 4, SH, 2 * FP), BF), V((2, FP, D), BF),
        V((2, 4, 4, 16, 128), BF),
        V((2, T, D), BF), V((T, D), BF), V((T, D), BF),
        V((2, T, D), BF), V((2, T, D), BF), V((2, T, D), BF), V((2, T, D), BF),
        V((2, T, D), F32), V((2, 3, T, HX), BF), V((2, 4, T, T), BF),
        V((2, 4, T, HX), BF), V((2, 4, T, HX), BF),
        V((2, 2, T, FP), F32), V((2, T, FP), BF), V((2, T, FP), BF),
        V((2, 2, T, FP), BF), V((2, T, FP), BF),
        V((2, T, 768), BF), V((2, T, 384), BF),
        V((2, T, D), BF), V((2, T, 128), BF), V((2, T, 512), BF), V((2, BT, D), F32),
        V((6, 4, BT, D), BF), V((6, 3, BT, D), BF),
        V((2, 4, 4, SH, 384), BF), V((2, 4, 4, SH, 128), BF), V((2, 4, 4, SH, FP), BF), V((2, FP, 512), BF),
        V((2, 2, 3, 4, 32, 384), BF), V((2, 2, 3, 4, 32, 128), BF), V((2, 2, 3, 4, 32, FP), BF),
        V((2, 3, DR, 512), BF),
        V((2, 2, 3, 32, 384), BF), V((2, 2, 3, 32, 128), BF), V((2, 2, 3, 32, FP), BF), V((2, 3, DR, 512), BF),
        V((2, 2, 4, 32, 384), BF), V((2, 2, 4, 32, 128), BF), V((2, 2, 4, 32, FP), BF), V((2, DR, 512), BF),
        V((2, 4, SH, 384), BF), V((2, 4, SH, 128), BF), V((2, 4, SH, FP), BF), V((2, DR, 512), BF),
        V((SH, 384), BF), V((SH, 128), BF), V((SH, FP), BF), V((DR, 512), BF),
        V((5, 8, D), F32), V((4, 3, 8, D), F32), V((2, 2, BT, D), BF), V((2, BT, D), BF),
        pltpu.SemaphoreType.DMA((N_SEND,)), pltpu.SemaphoreType.DMA((N_RECV,)), pltpu.SemaphoreType.DMA((N_LOC,)),
    ]
    return pl.pallas_call(
        kernel,
        out_shape=out_shape,
        in_specs=[pl.BlockSpec(memory_space=pltpu.SMEM)] + [any_] * 6 + [vm] * 3,
        out_specs=[any_] * 7,
        scratch_shapes=scratch,
        name="two_layers",
        compiler_params=pltpu.CompilerParams(
            collective_id=0, has_side_effects=True, vmem_limit_bytes=64 * 1024 * 1024 - 65536
        ),
    )(lengths, ends, q_src, o_src, gu_src, d_src, gain_src, cos, sa, sb)


def tables(doc_lengths):
    ends = jnp.cumsum(doc_lengths)
    i = jnp.arange(T, dtype=jnp.int32)
    start = jnp.where(i >= ends[1], ends[1], jnp.where(i >= ends[0], ends[0], 0))
    pos = (i - start).astype(F32)
    lane = jnp.arange(HX, dtype=jnp.int32) % 64
    freq = 10000.0 ** (-(lane % 32).astype(F32) / 32.0)
    phase = pos[:, None] * freq[None, :]
    cos, sin = jnp.cos(phase), jnp.sin(phase)
    first = (lane < 32)[None, :]
    return cos, jnp.where(first, -sin, 0.0), jnp.where(first, 0.0, sin)


def per_device(ends_in, lengths, qkv_w, out_w, gate_w, up_w, down_w, gains):
    s = lax.axis_index("section")
    d = lax.axis_index("dp")
    k = lax.rem(lax.axis_index("ctx"), 2)
    ends = ends_in[0, :, 0]
    doc = lengths[:, 0]
    q_src = qkv_w[0].astype(BF).reshape(SH, 3, 4, HX).transpose(2, 0, 1, 3).reshape(4, SH, 768)

    def ff_slices(w):
        return jnp.pad(w.astype(BF).reshape(SH, 4, FX), ((0, 0), (0, 0), (0, FP - FX))).transpose(1, 0, 2)

    gu_src = jnp.concatenate([ff_slices(gate_w[0]), ff_slices(up_w[0])], axis=2)
    o_src = out_w[0].astype(BF)
    d_src = down_w[0].astype(BF)
    gb = gains[0].astype(BF)
    odd = lax.rem(d, 2) == 1
    gain_src = jnp.where(odd, jnp.pad(gb, ((0, 14), (64, 0))), jnp.pad(gb, ((0, 14), (0, 64))))
    cos, sa, sb = tables(lax.dynamic_index_in_dim(doc, k, 0, keepdims=False))
    oq, oo, ogu, od, edge, gsum, _ = run_kernel(doc, ends, q_src, o_src, gu_src, d_src, gain_src, cos, sa, sb)
    qkv = oq.transpose(2, 1, 0, 3).reshape(SH, 4, 3, HX).transpose(0, 2, 1, 3).reshape(SH, 3 * D).astype(F32)
    out = oo.transpose(2, 1, 0, 3).reshape(SH, D).astype(F32)
    gate = ogu[0].transpose(1, 0, 2)[:, :, :FX].reshape(SH, FF).astype(F32)
    up = ogu[1].transpose(1, 0, 2)[:, :, :FX].reshape(SH, FF).astype(F32)
    down = od.transpose(1, 0, 2).reshape(DR, D).astype(F32)
    gg = lax.dynamic_slice(gsum, (2 * s, d * SH), (2, SH))
    return edge[None, :, None], qkv[None], out[None], gate[None], up[None], down[None], gg[None]


def solution(mesh):
    in_specs = (
        P("section", None, "dp", "ctx", None),
        P(None, "dp", None),
        P("section", "dp", None),
        P("section", "dp", None),
        P("section", "dp", None),
        P("section", "dp", None),
        P("section", "dp", None),
        P("section", None, "dp"),
    )
    out_specs = (
        P("section", None, "dp", "ctx", None),
        P("section", "dp", None),
        P("section", "dp", None),
        P("section", "dp", None),
        P("section", "dp", None),
        P("section", "dp", None),
        P("section", None, "dp"),
    )
    return jax.shard_map(per_device, mesh=mesh, in_specs=in_specs, out_specs=out_specs, check_vma=False)
```

```python
import jax
import jax.numpy as jnp
import numpy as np
from jax import lax
from jax.experimental import pallas as pl
from jax.experimental.pallas import tpu as pltpu
from jax.sharding import PartitionSpec as P

T = 256
D = 1024
FF = 2816
FX = FF // 4
FP = 768
HX = 256
SH = 64
DR = 176
BT = 64
EPS = 1e-5
MESH = pl.DeviceIdType.MESH
BF = jnp.bfloat16
F32 = jnp.float32


def dot(a, b):
    return jnp.dot(a, b, preferred_element_type=F32)


def dot_nt(a, b):
    return lax.dot_general(a, b, (((1,), (1,)), ((), ())), preferred_element_type=F32)


def dot_tn(a, b):
    return lax.dot_general(a, b, (((0,), (0,)), ((), ())), preferred_element_type=F32)


N_SEND = 64
N_RECV = 264
N_LOC = 18
GROUP_BYTES = 4 * 1024 * 1024


def kernel(
    lengths, ends, q_w, o_w, gate_w, up_w, d_w, gains, angles,
    oq_hbm, oo_hbm, ogu_hbm, od_hbm, edge_hbm, gsum_hbm, dummy,
    Wq, Wo, Wgu, Wd, Gn,
    E, X1, DY0, N1, N1s, N2, N2s, H, QKV, PR, O, Os, GU, M, Ms, DGU, DGUs, DP, DPs, DHB, DHBs, DYs, DH,
    PS, PRV,
    Gq, Go, Ggu, Gd, R1q, R1o, R1gu, R1d, R2q, R2o, R2gu, R2d, Sq, So, Sgu, Sd, OUTq, OUTo, OUTgu, OUTd,
    FSq, FSo, FSgu, FSd, GS, GR, TT, EO,
    CS, QT, GT, OT, DT, NT, gain_in,
    ssem, rsem, lsem,
):
    s = lax.axis_index("section")
    dp = lax.axis_index("dp")
    c = lax.axis_index("ctx")
    xh = lax.div(c, 2)
    k = lax.rem(c, 2)
    x = xh * 2 + s
    z = lax.div(dp, 4)
    y = lax.rem(dp, 4)

    def dev(x_, y_, z_, k_):
        return (lax.rem(x_, 2), z_ * 4 + y_, lax.div(x_, 2) * 2 + k_)

    def ring(v):
        return [lax.rem(v + 1, 4), lax.rem(v + 3, 4), lax.rem(v + 2, 4)]

    X3, Y3, Z3 = ring(x), ring(y), ring(z)
    PX = [dev(v, y, z, k) for v in X3]
    PY = [dev(x, v, z, k) for v in Y3]
    PZ = [dev(x, y, v, k) for v in Z3]
    SIB = dev(x, y, z, 1 - k)

    bar = pltpu.get_barrier_semaphore()
    partners = PX + PY + PZ + [SIB]
    for p in partners:
        pl.semaphore_signal(bar, inc=1, device_id=p, device_id_type=MESH)
    pl.semaphore_wait(bar, len(partners))

    counter = [0, 0, 0]
    sent = []
    groups = []

    def size(ref):
        n = 2 if ref.dtype == BF else 4
        for v in ref.shape:
            n *= v
        return n

    def new_recv():
        counter[0] += 1
        return counter[0] - 1

    def rc(src, dst, to, recv=None, cond=None):
        recv = new_recv() if recv is None else recv
        if cond is None:
            if not groups or groups[-1][2] or groups[-1][1] + size(src) > GROUP_BYTES:
                groups.append([counter[2], 0, False])
                counter[2] += 1
            groups[-1][1] += size(src)
            i = groups[-1][0]
        else:
            i = counter[2]
            counter[2] += 1
        desc = pltpu.make_async_remote_copy(
            src_ref=src, dst_ref=dst, send_sem=ssem.at[i], recv_sem=rsem.at[recv],
            device_id=to, device_id_type=MESH,
        )
        if cond is not None:
            sent.append((cond, desc))
        return desc

    def push(src, dst, to, recv=None):
        desc = rc(src, dst, to, recv)
        desc.start()
        return desc

    def push3(srcs, dsts, to):
        return [push(a, b, t) for a, b, t in zip(srcs, dsts, to)]

    def wait_recv(descs):
        for desc in descs:
            desc.wait_recv()

    def wait_bytes(ref, recv):
        pltpu.make_async_remote_copy(
            src_ref=ref, dst_ref=ref, send_sem=ssem.at[0], recv_sem=rsem.at[recv], device_id=SIB, device_id_type=MESH,
        ).wait_recv()

    def close():
        if groups:
            groups[-1][2] = True
        return len(groups)

    def flush(first, last):
        for i, total, _ in groups[first:last]:
            ref = dummy.at[pl.ds(0, total // 4096)]
            pltpu.make_async_copy(ref, ref, ssem.at[i]).wait()

    def flush_conditional():
        for cond, desc in sent:
            @pl.when(cond)
            def _(desc=desc):
                desc.wait_send()

    class Gather:
        def __init__(self, ring, blk, both):
            (self.p, self.m, self.o), self.me, self.P, self.M = ring
            self.blk, self.both = blk, both

        def a(self):
            self.r = [new_recv() for _ in range(3)]
            h0, h1 = self.blk(self.me, 0), self.blk(self.me, 1)
            push(h0, h0, self.P, self.r[0])
            push(h1, h1, self.M, self.r[1])
            push(h1, h1, self.P, self.r[2])
            push(h0, h0, self.M, self.r[2])
            return self

        def b(self):
            left, right = self.blk(self.m, 0), self.blk(self.p, 1)
            wait_bytes(left, self.r[0])
            push(left, left, self.P, self.r[2])
            wait_bytes(right, self.r[1])
            push(right, right, self.M, self.r[2])
            return self

        def c(self):
            wait_bytes(self.both, self.r[2])

    class Reduce:
        def __init__(self, ring, part, buf, both):
            (self.p, self.m, self.o), self.me, self.P, self.M = ring
            self.part, self.buf, self.both = part, buf, both

        def a(self):
            self.r = [new_recv() for _ in range(3)]
            part, buf = self.part, self.buf
            push(part(self.o, 0), buf(0, 0), self.P, self.r[0])
            push(part(self.o, 1), buf(0, 1), self.M, self.r[1])
            push(part(self.p, 1), buf(1, 1), self.P, self.r[2])
            push(part(self.m, 0), buf(2, 0), self.M, self.r[2])
            return self

        def b(self):
            part, buf = self.part, self.buf
            for h, j, to in ((0, self.p, self.P), (1, self.m, self.M)):
                ref, got = part(j, h), buf(0, h)
                wait_bytes(got, self.r[h])
                ref[...] = (ref[...].astype(F32) + got[...].astype(F32)).astype(BF)
                push(ref, buf(1 + h, h), to, self.r[2])
            return self

        def c(self):
            wait_bytes(self.both, self.r[2])

    RX = ((X3[0], X3[1], X3[2]), x, PX[0], PX[1])
    RY = ((Y3[0], Y3[1], Y3[2]), y, PY[0], PY[1])
    RZ = ((Z3[0], Z3[1], Z3[2]), z, PZ[0], PZ[1])

    def local(src, dst):
        i = counter[1]
        counter[1] += 1
        return pltpu.make_async_copy(src, dst, lsem.at[i])

    def half(width):
        return pl.ds(pl.multiple_of(k * (width // 2), 128), width // 2)

    def other_half(width):
        return pl.ds(pl.multiple_of((1 - k) * (width // 2), 128), width // 2)

    own = pl.ds(pl.multiple_of(x * BT, BT), BT)

    tx = lax.rem(x + 3 - 2 * k, 4)
    TO = dev(tx, y, z, k)
    REG = {"q": (Wq, 768), "o": (Wo, 1024), "gu": (Wgu, 2 * FP)}
    pre = {}
    down_rows = pl.ds(pl.multiple_of(y * DR, 16), DR)
    slices = (x, tx)
    q_in = GU.at[1, 0, pl.ds(128, 128), pl.ds(0, 384)]
    gu_in = GU.at[1, 0, pl.ds(0, 128), :]
    d_in = GU.at[1, 1, pl.ds(0, DR), pl.ds(0, 512)]
    o_in = GU.at[1, 1, pl.ds(192, SH), pl.ds(0, 512)]
    q_cp = []
    for j in range(2):
        for i in range(3):
            piece = 3 * k + i
            col = D * lax.div(piece, 2) + HX * slices[j] + 128 * lax.rem(piece, 2)
            q_cp.append(local(q_w.at[0, :, pl.ds(pl.multiple_of(col, 128), 128)],
                              GU.at[1, 0, pl.ds(128 + SH * j, SH), pl.ds(128 * i, 128)]))
    o_cp = local(o_w.at[0, :, half(D)], o_in)
    d_cp = local(d_w.at[0, :, half(D)], d_in)
    gu_cp = []
    for w in (gate_w, up_w):
        pair = []
        for j in range(2):
            col = 2 * FX * lax.div(slices[j], 2) + (FX - 64) * lax.rem(slices[j], 2)
            pair.append((w.at[0, :, pl.ds(pl.multiple_of(col, 128), FP)], GU.at[1, 0, pl.ds(SH * j, SH), :]))
        gu_cp.append(pair)
    gu_cp = [[local(*c) for c in gu_cp[0]], None, gu_cp[1]]
    gu_cp[1] = [pltpu.make_async_copy(*c, lsem.at[counter[1] - 2 + j]) for j, c in enumerate(gu_cp.pop())]
    for cp in q_cp:
        cp.start()
    for kk in range(2):
        @pl.when(k == kk)
        def _(kk=kk):
            for cp in gu_cp[kk]:
                cp.start()
    o_cp.start()
    d_cp.start()

    odd = lax.rem(dp, 2) == 1
    gz = jnp.zeros((2, SH), F32)
    gv = gains[0].astype(F32)
    NT[...] = jnp.zeros((16, 128), BF)
    gain_in[...] = jnp.zeros((16, 128), F32)
    gain_in[0:2, :] = jnp.where(odd, jnp.concatenate([gz, gv], axis=1), jnp.concatenate([gv, gz], axis=1))
    NT[...] = gain_in[...].astype(BF)
    Gn[s, z, y] = NT[...]
    pre["g"] = rc(NT, Gn.at[s, z, y], TO)
    pre["g"].start()

    for cp in q_cp:
        cp.wait()
    QT[...] = q_in[SH : 2 * SH, :].astype(BF)
    pre["q"] = rc(QT, Wq.at[s, z, y, :, half(768)], TO)
    pre["q"].start()
    Wq[s, z, y, :, half(768)] = q_in[0:SH, :].astype(BF)

    o_cp.wait()
    OT[...] = o_in[...].astype(BF)
    pre["o"] = rc(OT, Wo.at[s, z, y, :, half(D)], TO)
    pre["o"].start()
    Wo[s, z, y, :, half(D)] = OT[...]

    wide = lax.broadcasted_iota(jnp.int32, (SH, FP), 1)

    def hidden_slice(j):
        v = gu_in[SH * j : SH * (j + 1), :]
        v = jnp.where(lax.rem(slices[j], 2) == 1, pltpu.roll(v, FP - 64, 1), v)
        return jnp.where(wide < FX, v, 0.0).astype(BF)

    for cp in gu_cp[0]:
        cp.wait()
    GT[...] = hidden_slice(1)
    pre["gu"] = rc(GT, Wgu.at[s, z, y, :, half(2 * FP)], TO)
    pre["gu"].start()
    Wgu[s, z, y, :, half(2 * FP)] = hidden_slice(0)

    d_cp.wait()
    DT[...] = d_in[...].astype(BF)
    pre["d"] = rc(DT, Wd.at[s, down_rows, half(D)], TO, cond=(z == tx))

    @pl.when(z == tx)
    def _():
        pre["d"].start()

    @pl.when(z == x)
    def _():
        Wd[s, down_rows, half(D)] = DT[...]

    mine = pl.ds(pl.multiple_of(xh * 128 + k * 64, 64), 64)
    e_loc = local(ends.at[0, k, 0], E.at[s, mine])
    e_loc.start()
    e_sib = push(ends.at[0, 1 - k, 0], E.at[s, mine], SIB)

    ag = {}

    def ready(l, name):
        @pl.when(s != l)
        def _():
            pre[name].wait_recv()

    def rows16(base, h):
        return pl.ds(base + 16 * h, 16)

    def quarter(h):
        return pl.ds(pl.multiple_of(k * 512 + h * 256, 128), 256)

    is_src, is_p, is_m, is_f = z == x, z == X3[0], z == X3[1], z == X3[2]

    def s1a(l, name):
        if name == "d":
            ref = Wd.at[l, down_rows, half(D)]
            idx = new_recv()
            up = rc(ref, ref, PZ[0], recv=idx, cond=is_src)
            dn = rc(ref, ref, PZ[1], recv=idx, cond=is_src)

            @pl.when(is_src)
            def _():
                ready(l, "d")
                up.start()
                dn.start()
            ag[l, "d", 1] = up, idx
            return
        ready(l, name)
        if name == "g":
            ref = Gn.at[l, z, y]
            ag[l, name, 1] = new_recv()
            for to in PY:
                push(ref, ref, to, ag[l, name, 1])
            return
        W, width = REG[name]
        cols = half(width)
        ag[l, name, 1] = (
            Gather(RY, lambda j, h: W.at[l, z, j, rows16(0, h), cols], W.at[l, z, pl.ds(0, 2), pl.ds(0, 32), cols]).a(),
            Gather(RZ, lambda j, h: W.at[l, j, y, rows16(32, h), cols], W.at[l, pl.ds(0, 2), y, pl.ds(0, 32), cols]).a(),
        )

    def s1b(l, name):
        if name == "g":
            return
        first = ag[l, name, 1]
        if name == "d":
            got, idx = first
            h0, h1 = Wd.at[l, down_rows, quarter(0)], Wd.at[l, down_rows, quarter(1)]
            to_f = [rc(h0, h0, PZ[0], recv=idx, cond=is_p), rc(h1, h1, PZ[1], recv=idx, cond=is_m)]
            for cond, desc in zip((is_p, is_m), to_f):
                @pl.when(cond)
                def _(desc=desc):
                    got.wait_recv()
                    desc.start()
            return
        first[0].b()
        first[1].b()

    def s2a(l, name):
        first = ag[l, name, 1]
        if name == "g":
            wait_bytes(Gn.at[l, z, pl.ds(0, 3)], first)
            ref = Gn.at[l, z]
            ag[l, name, 2] = new_recv()
            for to in PZ:
                push(ref, ref, to, ag[l, name, 2])
            return
        if name == "d":
            @pl.when(is_f)
            def _():
                first[0].wait_recv()

            def blk(j, h):
                return Wd.at[l, pl.ds(pl.multiple_of(j * DR, 16), DR), quarter(h)]
            ag[l, name, 2] = (Gather(RY, blk, Wd.at[l, pl.ds(0, 2 * DR), half(D)]).a(),)
            return
        W, width = REG[name]
        cols = half(width)
        first[0].c()
        ga = Gather(RZ, lambda j, h: W.at[l, j, :, rows16(0, h), cols], W.at[l, pl.ds(0, 2), :, pl.ds(0, 32), cols]).a()
        first[1].c()
        gb = Gather(RY, lambda j, h: W.at[l, :, j, rows16(32, h), cols], W.at[l, :, pl.ds(0, 2), pl.ds(0, 32), cols]).a()
        ag[l, name, 2] = (ga, gb)

    def s2b(l, name):
        if name != "g":
            for g in ag[l, name, 2]:
                g.b()

    def s3(l, name):
        if name == "g":
            wait_bytes(Gn.at[l, pl.ds(0, 3)], ag[l, name, 2])
            return
        for g in ag[l, name, 2]:
            g.c()
        if name == "d":
            ref = Wd.at[l, pl.ds(0, FX), half(D)]
        else:
            W, width = REG[name]
            ref = W.at[l, :, :, :, half(width)]
        ag[l, name, 3] = push(ref, ref, SIB)

    def ag_done(l, name):
        wait_recv([ag[l, name, 3]])

    def gather_rows(ref):
        return Gather(RX, lambda j, h: ref.at[pl.ds(pl.multiple_of(j * BT + h * 32, 32), 32)], ref.at[pl.ds(0, 128)]).a()

    def gather_heads(l):
        return Gather(RX, lambda j, h: O.at[l, j, pl.ds(h * 128, 128)], O.at[l, pl.ds(0, 2)]).a()

    def scatter_sums(i, value_of):
        for b in range(4):
            PS[i, b] = value_of(b)
        return Reduce(RX, lambda j, h: PS.at[i, j, pl.ds(h * 32, 32)], lambda n, h: PRV.at[i, n, pl.ds(h * 32, 32)],
                      PRV.at[i, pl.ds(1, 2)]).a()

    def summed(i, red):
        red.c()
        return PS[i, x].astype(F32) + PRV[i, 1].astype(F32) + PRV[i, 2].astype(F32)

    GRAD = {"q": (Gq, R1q, R2q, Sq, OUTq, FSq, 384), "o": (Go, R1o, R2o, So, OUTo, FSo, 128),
            "gu": (Ggu, R1gu, R2gu, Sgu, OUTgu, FSgu, FP)}
    rs = {}

    def grad_ref(name, l):
        if name == "gu" and l == 0:
            return Wgu.at[1, :, :, :, pl.ds(0, FP)]
        return GRAD[name][0].at[0 if name == "gu" else l]

    def r1a(l, name):
        if name == "d":
            def part(j, h):
                return Gd.at[l, pl.ds(pl.multiple_of(j * DR, 16), DR), pl.ds(h * 256, 256)]
            rs[l, name, 1] = Reduce(RY, part, lambda n, h: R1d.at[l, n, :, pl.ds(h * 256, 256)], R1d.at[l, pl.ds(1, 2)]).a()
            return
        _, R1, R2, S, OUT, FS, width = GRAD[name]
        G = grad_ref(name, l)
        rs[l, name, 1] = (
            Reduce(RZ, lambda j, h: G.at[j, :, rows16(0, h)], lambda n, h: R1.at[l, 0, n, :, rows16(0, h)],
                   R1.at[l, 0, pl.ds(1, 2)]).a(),
            Reduce(RY, lambda j, h: G.at[:, j, rows16(32, h)], lambda n, h: R1.at[l, 1, n, :, rows16(0, h)],
                   R1.at[l, 1, pl.ds(1, 2)]).a(),
        )

    def r1b(l, name):
        first = rs[l, name, 1]
        if name == "d":
            first.b()
            return
        first[0].b()
        first[1].b()

    def r2a(l, name):
        first = rs[l, name, 1]
        if name == "d":
            first.c()
            Sd[l] = (Gd[l, down_rows].astype(F32) + R1d[l, 1].astype(F32) + R1d[l, 2].astype(F32)).astype(BF)
            idx = new_recv()
            to = [rc(Sd.at[l, :, pl.ds(0, 256)], R2d.at[l, 0, :, pl.ds(0, 256)], PZ[1], recv=idx, cond=is_f),
                  rc(Sd.at[l, :, pl.ds(256, 256)], R2d.at[l, 0, :, pl.ds(256, 256)], PZ[0], recv=idx, cond=is_f)]

            @pl.when(is_f)
            def _():
                to[0].start()
                to[1].start()
            rs[l, name, 2] = to
            return
        _, R1, R2, S, OUT, FS, width = GRAD[name]
        G = grad_ref(name, l)
        first[0].c()
        S[l, 0] = (G[z, :, pl.ds(0, 32)].astype(F32) + R1[l, 0, 1].astype(F32) + R1[l, 0, 2].astype(F32)).astype(BF)
        a = Reduce(RY, lambda j, h: S.at[l, 0, j, rows16(0, h)], lambda n, h: R2.at[l, 0, n, rows16(0, h)],
                   R2.at[l, 0, pl.ds(1, 2)]).a()
        first[1].c()
        S[l, 1] = (G[:, y, pl.ds(32, 32)].astype(F32) + R1[l, 1, 1].astype(F32) + R1[l, 1, 2].astype(F32)).astype(BF)
        b = Reduce(RZ, lambda j, h: S.at[l, 1, j, rows16(0, h)], lambda n, h: R2.at[l, 1, n, rows16(0, h)],
                   R2.at[l, 1, pl.ds(1, 2)]).a()
        rs[l, name, 2] = (a, b)

    def r2b(l, name):
        second = rs[l, name, 2]
        if name == "d":
            idx = [new_recv(), new_recv()]
            fin = [rc(Sd.at[l], R2d.at[l, 1], PZ[1], recv=idx[0], cond=is_p),
                   rc(Sd.at[l], R2d.at[l, 2], PZ[0], recv=idx[1], cond=is_m)]
            for cond, got, h, desc in ((is_p, second[0], 0, fin[0]), (is_m, second[1], 1, fin[1])):
                @pl.when(cond)
                def _(got=got, h=h, desc=desc):
                    got.wait_recv()
                    cols = pl.ds(256 * h, 256)
                    Sd[l, :, cols] = (Sd[l, :, cols].astype(F32) + R2d[l, 0, :, cols].astype(F32)).astype(BF)
                    desc.start()
            rs[l, name, 3] = fin
            return
        second[0].b()
        second[1].b()

    def rs3(l, name):
        idx = new_recv()
        if name == "d":
            fin = rs[l, name, 3]
            far = rc(OUTd.at[k], OUTd.at[k], PX[2], recv=idx, cond=is_src & (s == l))
            near = [rc(FSd, OUTd.at[k], PX[j], recv=idx, cond=is_src & (s != l)) for j in range(2)]

            @pl.when(is_src)
            def _():
                wait_recv(fin)
                total = (Sd[l].astype(F32) + R2d[l, 1].astype(F32) + R2d[l, 2].astype(F32)).astype(BF)

                @pl.when(s == l)
                def _():
                    OUTd[k] = total
                    far.start()

                @pl.when(s != l)
                def _():
                    FSd[...] = total
                    for desc in near:
                        desc.start()
            rs[l, name, 4] = far
            return
        G, R1, R2, S, OUT, FS, width = GRAD[name]
        second = rs[l, name, 2]
        second[0].c()
        second[1].c()
        top = (S[l, 0, y].astype(F32) + R2[l, 0, 1].astype(F32) + R2[l, 0, 2].astype(F32)).astype(BF)
        low = (S[l, 1, z].astype(F32) + R2[l, 1, 1].astype(F32) + R2[l, 1, 2].astype(F32)).astype(BF)
        slot = OUT.at[k, x]
        far = rc(slot, slot, PX[2], recv=idx, cond=(s == l))
        near = [rc(FS, slot, PX[j], recv=idx, cond=(s != l)) for j in range(2)]

        @pl.when(s == l)
        def _():
            OUT[k, x, 0:32] = top
            OUT[k, x, 32:64] = low
            far.start()

        @pl.when(s != l)
        def _():
            FS[0:32] = top
            FS[32:64] = low
            for desc in near:
                desc.start()
        rs[l, name, 4] = idx

    def rs4(l, name):
        got = rs[l, name, 4]
        ref = OUTd.at[k] if name == "d" else GRAD[name][4].at[k]
        fin = rc(ref, ref, SIB, cond=(s == l))

        @pl.when(s == l)
        def _():
            if name == "d":
                @pl.when(z != x)
                def _():
                    got.wait_recv()
            else:
                wait_bytes(GRAD[name][4].at[k, pl.ds(0, 3)], got)
            fin.start()
        rs[l, name, 5] = fin

    def rs5(l, name):
        @pl.when(s == l)
        def _():
            rs[l, name, 5].wait_recv()

    def edge(l, value):
        moved = rc(TT.at[l, s], TT.at[l, s], PX[0] if l == 1 else PX[1], cond=(s != l))
        TT[l, s] = value
        swap = rc(TT.at[l, 1 - k], EO.at[k], SIB, cond=(s == l))

        @pl.when(s != l)
        def _():
            moved.start()

        def finish():
            @pl.when(s == l)
            def _():
                moved.wait_recv()
                swap.start()
                EO[k] = TT[l, k]

        def done():
            @pl.when(s == l)
            def _():
                swap.wait_recv()
        return finish, done

    e0 = lengths[k, 0, 0]
    e1 = e0 + lengths[k, 0, 1]
    qi = lax.broadcasted_iota(jnp.int32, (T, T), 0)
    ki = lax.broadcasted_iota(jnp.int32, (T, T), 1)

    def doc(i):
        return jnp.where(i >= e0, 1, 0) + jnp.where(i >= e1, 1, 0)

    def allowed():
        return (doc(qi) == doc(ki)) & (ki <= qi)

    lane = lax.broadcasted_iota(jnp.int32, (T, 128), 1)

    def head(value, hh):
        return jnp.where((lane < 64) if hh == 0 else (lane >= 64), value, jnp.zeros_like(value))

    def make_angles():
        row = lax.broadcasted_iota(jnp.int32, (T, T), 0)
        start = jnp.where(row >= e1, e1, jnp.where(row >= e0, e0, 0))
        pick = jnp.where(ki == row - start, 1.0, 0.0).astype(BF)
        cos = dot(pick, angles[:, 0:128]) + dot(pick, angles[:, 128:256])
        sin = dot(pick, angles[:, 256:384]) + dot(pick, angles[:, 384:512])
        first = (lane < 32) | ((lane >= 64) & (lane < 96))
        CS[0] = cos
        CS[1] = jnp.where(first, -sin, 0.0)
        CS[2] = jnp.where(first, 0.0, sin)

    def turn(v, sign):
        tiles = []
        for t in range(2):
            u = v[:, 128 * t : 128 * (t + 1)]
            rot = pltpu.roll(u, 96, 1) * CS[1] + pltpu.roll(u, 32, 1) * CS[2]
            tiles.append(u * CS[0] + rot if sign > 0 else u * CS[0] - rot)
        return jnp.concatenate(tiles, axis=1)

    def rope(v):
        return turn(v, 1)

    def rope_t(v):
        return turn(v, -1)

    def gain(l, i):
        tiles = []
        for t in range(8):
            a = Gn[l, t // 2, 2 * (t % 2)].astype(F32) + Gn[l, t // 2, 2 * (t % 2) + 1].astype(F32)
            tiles.append(a[i : i + 1])
        return jnp.concatenate(tiles, axis=1)

    def mix(l):
        return 0.5 * l

    def norm_one(l, XR):
        g = gain(l, 0)
        for b in range(4):
            r = pl.ds(b * 64, 64)
            xf = XR[r, :].astype(F32)
            inv = lax.rsqrt(jnp.mean(xf * xf, axis=-1, keepdims=True) + EPS)
            N1[l, r, :] = (xf * inv * g).astype(BF)
        return push(N1.at[l], N1s.at[l], SIB)

    def wq(l):
        return Wq[l].reshape(D, 768)

    def project(l):
        n = N1[l]
        w = wq(l)
        QKV[l, 0] = rope(dot(n, w[:, 0:256])).astype(BF)
        QKV[l, 1] = rope(dot(n, w[:, 256:512])).astype(BF)
        v = dot(n, w[:, 512:768])
        if l == 1:
            v = 0.5 * v + 0.5 * QKV[0, 2].astype(F32)
        QKV[l, 2] = v.astype(BF)

    def attend(l):
        ok = allowed()
        for t in range(2):
            cols = pl.ds(128 * t, 128)
            qt, kt, vt = QKV[l, 0, :, cols], QKV[l, 1, :, cols], QKV[l, 2, :, cols]
            acc = jnp.zeros((T, 128), F32)
            for hh in range(2):
                sc = jnp.where(ok, dot_nt(head(qt, hh), kt) * 0.125, -1e30)
                ex = jnp.exp(sc - jnp.max(sc, axis=-1, keepdims=True))
                pr = (ex / jnp.sum(ex, axis=-1, keepdims=True)).astype(BF)
                PR[l, 2 * t + hh] = pr
                acc = acc + dot(pr, head(vt, hh))
            O[l, x, :, cols] = acc.astype(BF)
        return gather_heads(l)

    def hidden(l, XR, got):
        got.c()
        osib = push(O.at[l], Os.at[l], SIB)
        g = gain(l, 1)
        w = Wo[l].reshape(D, D)
        o = jnp.concatenate([O[l, b] for b in range(4)], axis=1)
        H[l] = XR[...].astype(F32) + dot(o, w)
        for b in range(4):
            r = pl.ds(b * 64, 64)
            hf = H[l, r, :]
            inv = lax.rsqrt(jnp.mean(hf * hf, axis=-1, keepdims=True) + EPS)
            N2[l, r, :] = (hf * inv * g).astype(BF)
        nsib = push(N2.at[l], N2s.at[l], SIB)
        return osib, nsib

    def gate_up(l):
        n = N2[l]
        GU[l, 0] = dot(n, Wgu[l, :, :, :, 0:FP].reshape(D, FP))
        GU[l, 1] = dot(n, Wgu[l, :, :, :, FP : 2 * FP].reshape(D, FP))
        for b in range(4):
            r = pl.ds(b * 64, 64)
            ga, up = GU[l, 0, r, :], GU[l, 1, r, :]
            M[l, r, :] = (ga * jax.nn.sigmoid(ga) * up).astype(BF)
        return push(M.at[l], Ms.at[l], SIB)

    def down(l, i):
        part = dot(M[l], Wd[l]).astype(BF)
        return scatter_sums(i, lambda b: part[b * 64 : (b + 1) * 64])

    def gain_grad(i, row, ref):
        total = jnp.zeros((1, D), F32)
        for b in range(4):
            v = ref[pl.ds(b * BT, BT), :].astype(F32)
            inv = lax.rsqrt(jnp.mean(v * v, axis=-1, keepdims=True) + EPS)
            total = total + jnp.sum(PS[i, b].astype(F32) * (v * inv), axis=0, keepdims=True)
        GS[0, row : row + 1] = total

    def back_ff(l, DY, i):
        dy = DY[...]
        dm = dot_nt(dy, Wd[l])
        ga, up = GU[l, 0], GU[l, 1]
        sg = jax.nn.sigmoid(ga)
        DGU[l, 0] = (dm * up * sg * (1.0 + ga * (1.0 - sg))).astype(BF)
        DGU[l, 1] = (dm * ga * sg).astype(BF)
        sib = push(DGU.at[l, 1 - k], DGUs.at[l], SIB)
        part = (dot_nt(DGU[l, 0], Wgu[l, :, :, :, 0:FP].reshape(D, FP))
                + dot_nt(DGU[l, 1], Wgu[l, :, :, :, FP : 2 * FP].reshape(D, FP))).astype(BF)
        got = scatter_sums(i, lambda b: part[b * 64 : (b + 1) * 64])
        return sib, got

    def grads_d(l, DY, msib, dysib):
        wait_recv([msib, dysib])
        Gd[l] = (dot_tn(M[l], DY[:, half(D)]) + dot_tn(Ms[l], DYs[l])).astype(BF)
        r1a(l, "d")

    def grads_gu(l, nsib, gsib):
        wait_recv([nsib, gsib])
        grad_ref("gu", l)[...] = (dot_tn(N2[l], DGU[l, k]) + dot_tn(N2s[l], DGUs[l])).astype(BF).reshape(4, 4, SH, FP)
        r1a(l, "gu")

    def back_hidden(l, DY, i, got):
        dn = summed(i, got)
        hf = H[l, own, :]
        g = gain(l, 1)
        inv = lax.rsqrt(jnp.mean(hf * hf, axis=-1, keepdims=True) + EPS)
        e = dn * g
        dh = DY[own, :].astype(F32) + inv * e - hf * (inv * inv * inv) * jnp.mean(e * hf, axis=-1, keepdims=True)
        DH[l] = dh
        DHB[l, own, :] = dh.astype(BF)
        return gather_rows(DHB.at[l])

    def back_attend(l, got, i):
        got.c()
        hs = pl.ds(pl.multiple_of(x * HX + (1 - k) * 128, 128), 128)
        hsib = push(DHB.at[l, :, hs], DHBs.at[l], SIB)
        do = dot_nt(DHB[l], Wo[l, x].reshape(HX, D)).astype(BF)
        dqs, dks, dvs = [], [], []
        for t in range(2):
            cols = pl.ds(128 * t, 128)
            qt, kt, vt = QKV[l, 0, :, cols], QKV[l, 1, :, cols], QKV[l, 2, :, cols]
            dot_ = do[:, 128 * t : 128 * (t + 1)]
            dq = dk = dv = jnp.zeros((T, 128), F32)
            for hh in range(2):
                pr = PR[l, 2 * t + hh]
                pf = pr.astype(F32)
                dom = head(dot_, hh)
                dpp = dot_nt(dom, vt)
                ds = (pf * (dpp - jnp.sum(pf * dpp, axis=-1, keepdims=True))).astype(BF)
                dq = dq + dot(ds, head(kt, hh))
                dk = dk + dot_tn(ds, head(qt, hh))
                dv = dv + dot_tn(pr, dom)
            dqs.append(dq)
            dks.append(dk)
            dvs.append(dv)
        dq = (jnp.concatenate(dqs, axis=1) * 0.125).astype(BF).astype(F32)
        dk = (jnp.concatenate(dks, axis=1) * 0.125).astype(BF).astype(F32)
        dv = jnp.concatenate(dvs, axis=1)
        DP[l, :, 0:256] = rope_t(dq).astype(BF)
        DP[l, :, 256:512] = rope_t(dk).astype(BF)
        if l == 1:
            dvt = dv.astype(BF)
            DP[l, :, 512:768] = (0.5 * dvt.astype(F32)).astype(BF)
        else:
            dvt = (dv + DP[1, :, 512:768].astype(F32)).astype(BF)
            DP[l, :, 512:768] = dvt
        psib = push(DP.at[l, :, other_half(768)], DPs.at[l], SIB)
        part = dot_nt(DP[l], wq(l)).astype(BF)
        got = scatter_sums(i, lambda b: part[b * 64 : (b + 1) * 64])
        return hsib, psib, got

    def grads_q(l, n1sib, psib):
        wait_recv([n1sib, psib])
        Gq[l] = (dot_tn(N1[l], DP[l, :, half(768)]) + dot_tn(N1s[l], DPs[l])).astype(BF).reshape(4, 4, SH, 384)
        r1a(l, "q")

    def grads_o(l, osib, hsib):
        wait_recv([osib, hsib])
        hs = pl.ds(pl.multiple_of(x * HX + k * 128, 128), 128)
        for b in range(4):
            Go[l, b] = (dot_tn(O[l, b], DHB[l, :, hs]) + dot_tn(Os[l, b], DHBs[l])).astype(BF).reshape(4, SH, 128)
        r1a(l, "o")

    def back_input(l, XR, i, got):
        dn = summed(i, got)
        xf = XR[own, :].astype(F32)
        g = gain(l, 0)
        inv = lax.rsqrt(jnp.mean(xf * xf, axis=-1, keepdims=True) + EPS)
        e = dn * g
        dx = DH[l] + inv * e - xf * (inv * inv * inv) * jnp.mean(e * xf, axis=-1, keepdims=True)
        return dx.astype(BF)

    def gsum_a(i, to):
        idx = new_recv()
        for j, t in enumerate(to):
            push(GS.at[i], GR.at[i, j], t, idx)
        return i, len(to), idx

    def gsum_b(sent_to):
        i, n, idx = sent_to
        wait_bytes(GR.at[i, pl.ds(0, n)], idx)
        total = GS[i]
        for j in range(n):
            total = total + GR[i, j]
        GS[i + 1] = total

    X0 = E.at[0]
    DY1 = E.at[1]
    NAMES = ("g", "q", "o", "gu", "d")
    GS[0] = jnp.zeros((8, D), F32)
    for l in range(2):
        Wd[l, FX:FP, :] = jnp.zeros((FP - FX, D), BF)
    for name in NAMES:
        s1a(0, name)
    e_loc.wait()
    e_sib.wait_recv()
    mine2 = pl.ds(pl.multiple_of(xh * 128, 128), 128)
    e_got = push3([E.at[s, mine2]] * 3, [E.at[s, mine2]] * 3, PX)
    for name in ("q", "o", "gu"):
        s1b(0, name)
    s2a(0, "q")
    for name in ("g", "q", "o", "gu"):
        s1a(1, name)
    s2a(0, "g")
    s2a(0, "o")
    s2a(0, "gu")
    make_angles()
    s1b(0, "d")
    s2b(0, "q")
    s1a(1, "d")
    s2a(0, "d")
    s2b(0, "o")
    s2b(0, "gu")
    s3(0, "q")
    s3(0, "g")
    wait_recv(e_got)
    n1sib = [norm_one(0, X0), None]
    for name in ("q", "o", "gu"):
        s1b(1, name)
    s2b(0, "d")
    ag_done(0, "q")
    project(0)
    s3(0, "o")
    got = attend(0)
    dysib = [None, push(DY1.at[:, other_half(D)], DYs.at[1], SIB)]
    s2a(1, "g")
    s2a(1, "q")
    s1b(1, "d")
    s3(0, "gu")
    got.b()
    s2a(1, "o")
    s2a(1, "gu")
    s3(0, "d")
    ag_done(0, "o")
    osib, nsib, msib = [None, None], [None, None], [None, None]
    osib[0], nsib[0] = hidden(0, X0, got)
    s2b(1, "q")
    ag_done(0, "gu")
    msib[0] = gate_up(0)
    ag_done(0, "d")
    got = down(0, 0)
    s2a(1, "d")
    s2b(1, "o")
    got.b()
    s2b(1, "gu")
    s3(1, "g")
    X1[own, :] = (summed(0, got) + H[0, own, :]).astype(BF)
    got = gather_rows(X1)
    s3(1, "q")
    s2b(1, "d")
    got.b()
    s3(1, "o")
    s3(1, "gu")
    s3(1, "d")
    early = close()
    got.c()
    n1sib[1] = norm_one(1, X1)
    ag_done(1, "q")
    project(1)
    got = attend(1)
    got.b()
    ag_done(1, "o")
    osib[1], nsib[1] = hidden(1, X1, got)
    ag_done(1, "gu")
    msib[1] = gate_up(1)
    ag_done(1, "d")
    y_red = down(1, 1)

    gsib, got = back_ff(1, DY1, 2)
    grads_d(1, DY1, msib[1], dysib[1])
    gain_grad(2, 3, H.at[1])
    got.b()
    y_red.b()
    grads_gu(1, nsib[1], gsib)
    got = back_hidden(1, DY1, 2, got)
    r1b(1, "d")
    y_fin, y_done = edge(1, (summed(1, y_red) + H[1, own, :]).astype(BF))
    got.b()
    hsib, psib, got = back_attend(1, got, 3)
    grads_o(1, osib[1], hsib)
    gain_grad(3, 2, X1)
    got.b()
    grads_q(1, n1sib[1], psib)
    r1b(1, "gu")
    r2a(1, "d")
    DY0[own, :] = back_input(1, X1, 3, got)
    got = gather_rows(DY0)
    y_fin()
    r1b(1, "o")
    got.b()
    r1b(1, "q")
    r2a(1, "gu")
    r2b(1, "d")
    got.c()
    dysib[0] = push(DY0.at[:, other_half(D)], DYs.at[0], SIB)

    gsib, got = back_ff(0, DY0, 4)
    r2a(1, "o")
    gain_grad(4, 1, H.at[0])
    got.b()
    r2a(1, "q")
    grads_d(0, DY0, msib[0], dysib[0])
    flush(0, early)
    grads_gu(0, nsib[0], gsib)
    r2b(1, "gu")
    rs3(1, "d")
    got = back_hidden(0, DY0, 4, got)
    r1b(0, "d")
    r2b(1, "o")
    r2b(1, "q")
    got.b()
    rs3(1, "gu")
    hsib, psib, got = back_attend(0, got, 5)
    gain_grad(5, 0, X0)
    g0 = gsum_a(0, PX)
    grads_o(0, osib[0], hsib)
    got.b()
    grads_q(0, n1sib[0], psib)
    r1b(0, "gu")
    gsum_b(g0)
    g0 = gsum_a(1, PY)
    r2a(0, "d")
    dx = back_input(0, X0, 5, got)
    x_fin, x_done = edge(0, dx)
    r1b(0, "o")
    r1b(0, "q")
    gsum_b(g0)
    g0 = gsum_a(2, PZ)
    rs3(1, "o")
    rs3(1, "q")
    r2a(0, "gu")
    r2b(0, "d")
    r2a(0, "o")
    r2a(0, "q")
    x_fin()
    for name in ("d", "gu"):
        rs4(1, name)
    gsum_b(g0)
    g0 = gsum_a(3, [SIB])
    r2b(0, "gu")
    rs3(0, "d")
    r2b(0, "o")
    r2b(0, "q")
    for name in ("o", "q"):
        rs4(1, name)
    rs3(0, "gu")
    rs3(0, "o")
    rs3(0, "q")
    for name in ("d", "gu", "o", "q"):
        rs4(0, name)
    gsum_b(g0)
    x_done()
    y_done()
    for name in ("d", "gu", "o", "q"):
        rs5(1, name)
        rs5(0, name)
    outs = [local(a, b) for a, b in
            ((OUTq, oq_hbm), (OUTo, oo_hbm), (OUTgu, ogu_hbm), (OUTd, od_hbm), (EO, edge_hbm), (GS.at[4], gsum_hbm))]
    for o in outs:
        o.start()
    flush(early, len(groups))
    flush_conditional()
    for o in outs:
        o.wait()
    assert counter[0] <= N_RECV and counter[1] <= N_LOC and counter[2] <= N_SEND, counter


def epilogue(*refs):
    given, (edges, qkv, out, gate, up, down, gg), held, sem = refs[:6], refs[6:13], refs[13:19], refs[19]
    copies = [pltpu.make_async_copy(a, b, sem.at[i]) for i, (a, b) in enumerate(zip(given, held))]
    for cp in copies:
        cp.start()
    for cp in copies:
        cp.wait()
    oq, oo, ogu, od, edge, gsum = held
    s = lax.axis_index("section")
    dp = lax.axis_index("dp")
    edges[0, :, 0] = edge[...]
    for x in range(4):
        a, b = oq[0, x].astype(F32), oq[1, x].astype(F32)
        qkv[0, :, HX * x : HX * (x + 1)] = a[:, 0:256]
        qkv[0, :, D + HX * x : D + HX * x + 128] = a[:, 256:384]
        qkv[0, :, D + HX * x + 128 : D + HX * (x + 1)] = b[:, 0:128]
        qkv[0, :, 2 * D + HX * x : 2 * D + HX * (x + 1)] = b[:, 128:384]
        for h in range(2):
            out[0, :, HX * x + 128 * h : HX * x + 128 * (h + 1)] = oo[h, x].astype(F32)
    for h, ref in ((0, gate), (1, up)):
        for p in range(2):
            a = ogu[h, 2 * p].astype(F32)
            b = pltpu.roll(ogu[h, 2 * p + 1].astype(F32), 64, 1)
            c = 2 * FX * p
            ref[0, :, c : c + 640] = a[:, 0:640]
            ref[0, :, c + 640 : c + 768] = a[:, 640:768] + b[:, 0:128]
            ref[0, :, c + 768 : c + 2 * FX] = b[:, 128:768]
    for h in range(2):
        down[0, :, 512 * h : 512 * (h + 1)] = od[h].astype(F32)
    tile = gsum[:, pl.ds(pl.multiple_of(128 * lax.div(dp, 2), 128), 128)]
    tile = jnp.where(lax.rem(dp, 2) == 1, pltpu.roll(tile, 64, 1), tile)
    rows = jnp.where(s == 1, tile[2:4], tile[0:2])
    gg[0] = rows[:, 0:SH]


def run_kernel(lengths, ends, qkv_w, out_w, gate_w, up_w, down_w, gains, angles):
    V = pltpu.VMEM
    sh = jax.ShapeDtypeStruct
    any_ = pl.BlockSpec(memory_space=pl.ANY)
    vm = pl.BlockSpec(memory_space=pltpu.VMEM)
    out_shape = [
        sh((2, 4, SH, 384), BF), sh((2, 4, SH, 128), BF), sh((2, 4, SH, FP), BF), sh((2, DR, 512), BF),
        sh((2, BT, D), BF), sh((8, D), F32), sh((GROUP_BYTES // 4096, 16, 128), BF),
    ]
    scratch = [
        V((2, 4, 4, SH, 768), BF), V((2, 4, 4, SH, D), BF), V((2, 4, 4, SH, 2 * FP), BF), V((2, FP, D), BF),
        V((2, 4, 4, 16, 128), BF),
        V((2, T, D), BF), V((T, D), BF), V((T, D), BF),
        V((2, T, D), BF), V((2, T, D), BF), V((2, T, D), BF), V((2, T, D), BF),
        V((2, T, D), F32), V((2, 3, T, HX), BF), V((2, 4, T, T), BF),
        V((2, 4, T, HX), BF), V((2, 4, T, HX), BF),
        V((2, 2, T, FP), F32), V((2, T, FP), BF), V((2, T, FP), BF),
        V((2, 2, T, FP), BF), V((2, T, FP), BF),
        V((2, T, 768), BF), V((2, T, 384), BF),
        V((2, T, D), BF), V((2, T, 128), BF), V((2, T, 512), BF), V((2, BT, D), F32),
        V((6, 4, BT, D), BF), V((6, 3, BT, D), BF),
        V((2, 4, 4, SH, 384), BF), V((2, 4, 4, SH, 128), BF), V((1, 4, 4, SH, FP), BF), V((2, FP, 512), BF),
        V((2, 2, 3, 4, 32, 384), BF), V((2, 2, 3, 4, 32, 128), BF), V((2, 2, 3, 4, 32, FP), BF),
        V((2, 3, DR, 512), BF),
        V((2, 2, 3, 32, 384), BF), V((2, 2, 3, 32, 128), BF), V((2, 2, 3, 32, FP), BF), V((2, 3, DR, 512), BF),
        V((2, 2, 4, 32, 384), BF), V((2, 2, 4, 32, 128), BF), V((2, 2, 4, 32, FP), BF), V((2, DR, 512), BF),
        V((2, 4, SH, 384), BF), V((2, 4, SH, 128), BF), V((2, 4, SH, FP), BF), V((2, DR, 512), BF),
        V((SH, 384), BF), V((SH, 128), BF), V((SH, FP), BF), V((DR, 512), BF),
        V((5, 8, D), F32), V((4, 3, 8, D), F32), V((2, 2, BT, D), BF), V((2, BT, D), BF),
        V((3, T, 128), F32), V((SH, 384), BF), V((SH, FP), BF), V((SH, 512), BF), V((DR, 512), BF),
        V((16, 128), BF), V((16, 128), F32),
        pltpu.SemaphoreType.DMA((N_SEND,)), pltpu.SemaphoreType.DMA((N_RECV,)), pltpu.SemaphoreType.DMA((N_LOC,)),
    ]
    return pl.pallas_call(
        kernel,
        out_shape=out_shape,
        in_specs=[pl.BlockSpec(memory_space=pltpu.SMEM)] + [any_] * 6 + [vm] * 2,
        out_specs=[any_] * 7,
        scratch_shapes=scratch,
        name="two_layers",
        compiler_params=pltpu.CompilerParams(
            collective_id=0, has_side_effects=True, vmem_limit_bytes=64 * 1024 * 1024 - 65536
        ),
    )(lengths, ends, qkv_w, out_w, gate_w, up_w, down_w, gains, angles)


def angle_table():
    pos = np.arange(T, dtype=np.float64)[:, None]
    freq = 10000.0 ** (-(np.arange(128) % 32) / 32.0)
    parts = []
    for v in (np.cos(pos * freq), np.sin(pos * freq)):
        high = v.astype(jnp.bfloat16)
        parts += [high, (v - high.astype(np.float64)).astype(jnp.bfloat16)]
    return np.concatenate(parts, axis=1)


def per_device(ends_in, lengths, qkv_w, out_w, gate_w, up_w, down_w, gains):
    oq, oo, ogu, od, edge, gsum, _ = run_kernel(
        lengths, ends_in, qkv_w, out_w, gate_w, up_w, down_w, gains, jnp.asarray(angle_table()))
    sh = jax.ShapeDtypeStruct
    return pl.pallas_call(
        epilogue,
        out_shape=[
            sh((1, 2, 1, BT, D), BF), sh((1, SH, 3 * D), F32), sh((1, SH, D), F32), sh((1, SH, FF), F32),
            sh((1, SH, FF), F32), sh((1, DR, D), F32), sh((1, 2, SH), F32),
        ],
        in_specs=[pl.BlockSpec(memory_space=pl.ANY)] * 6,
        out_specs=[pl.BlockSpec(memory_space=pltpu.VMEM)] * 7,
        scratch_shapes=[pltpu.VMEM(v.shape, v.dtype) for v in (oq, oo, ogu, od, edge, gsum)]
        + [pltpu.SemaphoreType.DMA((6,))],
        name="place_outputs",
        compiler_params=pltpu.CompilerParams(vmem_limit_bytes=63 * 1024 * 1024),
    )(oq, oo, ogu, od, edge, gsum)


def solution(mesh):
    in_specs = (
        P("section", None, "dp", "ctx", None),
        P(None, "dp", None),
        P("section", "dp", None),
        P("section", "dp", None),
        P("section", "dp", None),
        P("section", "dp", None),
        P("section", "dp", None),
        P("section", None, "dp"),
    )
    out_specs = (
        P("section", None, "dp", "ctx", None),
        P("section", "dp", None),
        P("section", "dp", None),
        P("section", "dp", None),
        P("section", "dp", None),
        P("section", "dp", None),
        P("section", None, "dp"),
    )
    return jax.shard_map(per_device, mesh=mesh, in_specs=in_specs, out_specs=out_specs, check_vma=False)
```

```python
import jax
import jax.numpy as jnp
import numpy as np
from jax import lax
from jax.experimental import pallas as pl
from jax.experimental.pallas import tpu as pltpu
from jax.sharding import PartitionSpec as P

T = 256
D = 1024
FF = 2816
FX = FF // 4
FP = 768
HX = 256
SH = 64
DR = 176
BT = 64
TH = 128
BH = 32
EPS = 1e-5
MESH = pl.DeviceIdType.MESH
BF = jnp.bfloat16
F32 = jnp.float32


def dot(a, b):
    return jnp.dot(a, b, preferred_element_type=F32)


def dot_nt(a, b):
    return lax.dot_general(a, b, (((1,), (1,)), ((), ())), preferred_element_type=F32)


def dot_tn(a, b):
    return lax.dot_general(a, b, (((0,), (0,)), ((), ())), preferred_element_type=F32)


N_SEND = 76
N_RECV = 244
N_LOC = 18
GROUP_BYTES = 4 * 1024 * 1024


def kernel(
    lengths, ends, q_w, o_w, gate_w, up_w, d_w, gains, angles,
    oq_hbm, oo_hbm, ogu_hbm, od_hbm, edge_hbm, gsum_hbm, dummy,
    Wq, Wo, Wgu, Wd, Gn,
    E, X1, DY0, N1, N1s, N2, N2s, H, QKV, PR, O, Os, GU, M, Ms, DGU, DGUs, DP, DPs, DHB, DHBs, DYs, DH, KV0, ED,
    PS, PRV,
    Gq, Go, Ggu, Gd, R1q, R1o, R1gu, R1d, R2q, R2o, R2gu, R2d, Sq, So, Sgu, Sd, OUTq, OUTo, OUTgu, OUTd,
    FSq, FSo, FSgu, FSd, GS, GR, TT, EO,
    CS, QT, GT, OT, DT, NT, gain_in,
    ssem, rsem, lsem,
):
    s = lax.axis_index("section")
    dp = lax.axis_index("dp")
    c = lax.axis_index("ctx")
    xh = lax.div(c, 2)
    k = lax.rem(c, 2)
    x = xh * 2 + s
    z = lax.div(dp, 4)
    y = lax.rem(dp, 4)

    def dev(x_, y_, z_, k_):
        return (lax.rem(x_, 2), z_ * 4 + y_, lax.div(x_, 2) * 2 + k_)

    def ring(v):
        return [lax.rem(v + 1, 4), lax.rem(v + 3, 4), lax.rem(v + 2, 4)]

    X3, Y3, Z3 = ring(x), ring(y), ring(z)
    PX = [dev(v, y, z, k) for v in X3]
    PY = [dev(x, v, z, k) for v in Y3]
    PZ = [dev(x, y, v, k) for v in Z3]
    SIB = dev(x, y, z, 1 - k)

    bar = pltpu.get_barrier_semaphore()
    partners = PX + PY + PZ + [SIB]
    for p in partners:
        pl.semaphore_signal(bar, inc=1, device_id=p, device_id_type=MESH)
    pl.semaphore_wait(bar, len(partners))

    counter = [0, 0, 0]
    sent = []
    groups = []

    def size(ref):
        n = 2 if ref.dtype == BF else 4
        for v in ref.shape:
            n *= v
        return n

    def new_recv():
        counter[0] += 1
        return counter[0] - 1

    def rc(src, dst, to, recv=None, cond=None):
        recv = new_recv() if recv is None else recv
        if cond is None:
            if not groups or groups[-1][2] or groups[-1][1] + size(src) > GROUP_BYTES:
                groups.append([counter[2], 0, False])
                counter[2] += 1
            groups[-1][1] += size(src)
            i = groups[-1][0]
        else:
            i = counter[2]
            counter[2] += 1
        desc = pltpu.make_async_remote_copy(
            src_ref=src, dst_ref=dst, send_sem=ssem.at[i], recv_sem=rsem.at[recv],
            device_id=to, device_id_type=MESH,
        )
        if cond is not None:
            sent.append((cond, desc))
        return desc

    def push(src, dst, to, recv=None):
        desc = rc(src, dst, to, recv)
        desc.start()
        return desc

    def push3(srcs, dsts, to):
        return [push(a, b, t) for a, b, t in zip(srcs, dsts, to)]

    def wait_recv(descs):
        for desc in descs:
            desc.wait_recv()

    def wait_bytes(ref, recv):
        pltpu.make_async_remote_copy(
            src_ref=ref, dst_ref=ref, send_sem=ssem.at[0], recv_sem=rsem.at[recv], device_id=SIB, device_id_type=MESH,
        ).wait_recv()

    def close():
        if groups:
            groups[-1][2] = True
        return len(groups)

    def flush(first, last):
        for i, total, _ in groups[first:last]:
            ref = dummy.at[pl.ds(0, total // 4096)]
            pltpu.make_async_copy(ref, ref, ssem.at[i]).wait()

    def flush_conditional():
        for cond, desc in sent:
            @pl.when(cond)
            def _(desc=desc):
                desc.wait_send()

    class Gather:
        def __init__(self, ring, blk, some, direct=False):
            (self.p, self.m, self.o), self.me, self.to = ring
            self.blk, self.some, self.direct = blk, some, direct

        def a(self):
            self.r = [new_recv() for _ in range(1 if self.direct else 3)]
            if self.direct:
                for to in self.to:
                    push(self.blk(self.me, None), self.blk(self.me, None), to, self.r[0])
                return self
            h0, h1 = self.blk(self.me, 0), self.blk(self.me, 1)
            push(h0, h0, self.to[0], self.r[0])
            push(h1, h1, self.to[1], self.r[1])
            push(h1, h1, self.to[0], self.r[2])
            push(h0, h0, self.to[1], self.r[2])
            return self

        def b(self):
            if not self.direct:
                left, right = self.blk(self.m, 0), self.blk(self.p, 1)
                wait_bytes(left, self.r[0])
                push(left, left, self.to[0], self.r[2])
                wait_bytes(right, self.r[1])
                push(right, right, self.to[1], self.r[2])
            return self

        def c(self):
            if self.direct:
                wait_bytes(self.some(3), self.r[0])
            else:
                wait_bytes(self.some(2), self.r[2])

    class Reduce:
        def __init__(self, ring, part, buf, some, direct=False):
            (self.p, self.m, self.o), self.me, self.to = ring
            self.part, self.buf, self.some, self.direct = part, buf, some, direct
            self.terms = (0, 1, 2) if direct else (1, 2)

        def a(self):
            self.r = [new_recv() for _ in range(1 if self.direct else 3)]
            part, buf = self.part, self.buf
            if self.direct:
                for i, (j, to) in enumerate(zip((self.p, self.m, self.o), self.to)):
                    push(part(j, None), buf(i, None), to, self.r[0])
                return self
            push(part(self.o, 0), buf(0, 0), self.to[0], self.r[0])
            push(part(self.o, 1), buf(0, 1), self.to[1], self.r[1])
            push(part(self.p, 1), buf(1, 1), self.to[0], self.r[2])
            push(part(self.m, 0), buf(2, 0), self.to[1], self.r[2])
            return self

        def b(self):
            if self.direct:
                return self
            part, buf = self.part, self.buf
            for h, j, to in ((0, self.p, self.to[0]), (1, self.m, self.to[1])):
                ref, got = part(j, h), buf(0, h)
                wait_bytes(got, self.r[h])
                ref[...] = (ref[...].astype(F32) + got[...].astype(F32)).astype(BF)
                push(ref, buf(1 + h, h), to, self.r[2])
            return self

        def c(self):
            if self.direct:
                wait_bytes(self.some(0, 3), self.r[0])
            else:
                wait_bytes(self.some(1, 2), self.r[2])

        def total(self):
            value = self.part(self.me, None)[...].astype(F32)
            for i in self.terms:
                value = value + self.buf(i, None)[...].astype(F32)
            return value

    RX, RY, RZ = (X3, x, PX), (Y3, y, PY), (Z3, z, PZ)

    def path_rows(path, paths, h):
        n = 64 // len(paths)
        base = n * paths.index(path)
        return pl.ds(base, n) if h is None else pl.ds(base + h * (n // 2), n // 2)

    def sub(base, width, h):
        return pl.ds(base, width) if h is None else pl.ds(base + h * (width // 2), width // 2)

    def local(src, dst):
        i = counter[1]
        counter[1] += 1
        return pltpu.make_async_copy(src, dst, lsem.at[i])

    def half(width):
        return pl.ds(pl.multiple_of(k * (width // 2), 128), width // 2)

    def other_half(width):
        return pl.ds(pl.multiple_of((1 - k) * (width // 2), 128), width // 2)

    tx = lax.rem(x + 3 - 2 * k, 4)
    TO = dev(tx, y, z, k)
    REG = {"q": (Wq, 768), "o": (Wo, 1024), "gu": (Wgu, 2 * FP)}
    pre = {}
    down_rows = pl.ds(pl.multiple_of(y * DR, 16), DR)
    slices = (x, tx)
    q_in = GU.at[1, 0, pl.ds(128, 128), pl.ds(0, 384)]
    gu_in = GU.at[1, 0, pl.ds(0, 128), :]
    d_in = GU.at[1, 1, pl.ds(0, DR), pl.ds(0, 512)]
    o_in = GU.at[1, 1, pl.ds(192, SH), pl.ds(0, 512)]
    q_cp = []
    for j in range(2):
        for i in range(3):
            piece = 3 * k + i
            col = D * lax.div(piece, 2) + HX * slices[j] + 128 * lax.rem(piece, 2)
            q_cp.append(local(q_w.at[0, :, pl.ds(pl.multiple_of(col, 128), 128)],
                              GU.at[1, 0, pl.ds(128 + SH * j, SH), pl.ds(128 * i, 128)]))
    o_cp = local(o_w.at[0, :, half(D)], o_in)
    d_cp = local(d_w.at[0, :, half(D)], d_in)
    gu_cp = []
    for w in (gate_w, up_w):
        pair = []
        for j in range(2):
            col = 2 * FX * lax.div(slices[j], 2) + (FX - 64) * lax.rem(slices[j], 2)
            pair.append((w.at[0, :, pl.ds(pl.multiple_of(col, 128), FP)], GU.at[1, 0, pl.ds(SH * j, SH), :]))
        gu_cp.append(pair)
    gu_cp = [[local(*c) for c in gu_cp[0]], None, gu_cp[1]]
    gu_cp[1] = [pltpu.make_async_copy(*c, lsem.at[counter[1] - 2 + j]) for j, c in enumerate(gu_cp.pop())]
    for cp in q_cp:
        cp.start()
    for kk in range(2):
        @pl.when(k == kk)
        def _(kk=kk):
            for cp in gu_cp[kk]:
                cp.start()
    o_cp.start()
    d_cp.start()

    odd = lax.rem(dp, 2) == 1
    gz = jnp.zeros((2, SH), F32)
    gv = gains[0].astype(F32)
    NT[...] = jnp.zeros((16, 128), BF)
    gain_in[...] = jnp.zeros((16, 128), F32)
    gain_in[0:2, :] = jnp.where(odd, jnp.concatenate([gz, gv], axis=1), jnp.concatenate([gv, gz], axis=1))
    NT[...] = gain_in[...].astype(BF)
    Gn[z, y, s] = NT[...]
    pre["g"] = rc(NT, Gn.at[z, y, s], TO)
    pre["g"].start()

    for cp in q_cp:
        cp.wait()
    QT[...] = q_in[SH : 2 * SH, :].astype(BF)
    pre["q"] = rc(QT, Wq.at[s, z, y, :, half(768)], TO)
    pre["q"].start()
    Wq[s, z, y, :, half(768)] = q_in[0:SH, :].astype(BF)

    o_cp.wait()
    OT[...] = o_in[...].astype(BF)
    pre["o"] = rc(OT, Wo.at[s, z, y, :, half(D)], TO)
    pre["o"].start()
    Wo[s, z, y, :, half(D)] = OT[...]

    wide = lax.broadcasted_iota(jnp.int32, (SH, FP), 1)

    def hidden_slice(j):
        v = gu_in[SH * j : SH * (j + 1), :]
        v = jnp.where(lax.rem(slices[j], 2) == 1, pltpu.roll(v, FP - 64, 1), v)
        return jnp.where(wide < FX, v, 0.0).astype(BF)

    for cp in gu_cp[0]:
        cp.wait()
    GT[...] = hidden_slice(1)
    pre["gu"] = rc(GT, Wgu.at[s, z, y, :, half(2 * FP)], TO)
    pre["gu"].start()
    Wgu[s, z, y, :, half(2 * FP)] = hidden_slice(0)

    d_cp.wait()
    DT[...] = d_in[...].astype(BF)
    pre["d"] = rc(DT, Wd.at[s, down_rows, half(D)], TO, cond=(z == tx))

    @pl.when(z == tx)
    def _():
        pre["d"].start()

    @pl.when(z == x)
    def _():
        Wd[s, down_rows, half(D)] = DT[...]

    mine = pl.ds(pl.multiple_of(xh * 128 + k * 64, 64), 64)
    e_loc = local(ends.at[0, k, 0], E.at[s, mine])
    e_loc.start()
    e_sib = push(ends.at[0, 1 - k, 0], E.at[s, mine], SIB)

    ag = {}

    def ready(l, name):
        @pl.when(s != l)
        def _():
            pre[name].wait_recv()

    def quarter(h):
        return half(D) if h is None else pl.ds(pl.multiple_of(k * 512 + h * 256, 128), 256)

    is_src, is_p, is_m, is_f = z == x, z == X3[0], z == X3[1], z == X3[2]

    AG_PATHS = {(l, name): "AB" for l in range(2) for name in REG}
    AG_DIRECT = ((0, "q"),)

    def g1():
        for l in range(2):
            ready(l, "g")
        ref = Gn.at[z, y]
        ag["g"] = new_recv()
        for to in PY:
            push(ref, ref, to, ag["g"])

    def g2():
        wait_bytes(Gn.at[z, pl.ds(0, 3)], ag["g"])
        ref = Gn.at[z]
        ag["g"] = new_recv()
        for to in PZ:
            push(ref, ref, to, ag["g"])

    def g3():
        wait_bytes(Gn.at[pl.ds(0, 3)], ag["g"])

    def s1a(l, name):
        if name == "d":
            ref = Wd.at[l, down_rows, half(D)]
            idx = new_recv()
            up = rc(ref, ref, PZ[0], recv=idx, cond=is_src)
            dn = rc(ref, ref, PZ[1], recv=idx, cond=is_src)

            @pl.when(is_src)
            def _():
                ready(l, "d")
                up.start()
                dn.start()
            ag[l, "d", 1] = up, idx
            return
        ready(l, name)
        W, width = REG[name]
        cols = half(width)
        paths, direct = AG_PATHS[l, name], (l, name) in AG_DIRECT
        first = []
        for path in paths:
            rows = lambda h, path=path: path_rows(path, paths, h)
            if path == "A":
                g = Gather(RY, lambda j, h, rows=rows: W.at[l, z, j, rows(h), cols],
                           lambda n, rows=rows: W.at[l, z, pl.ds(0, n), rows(None), cols], direct)
            else:
                g = Gather(RZ, lambda j, h, rows=rows: W.at[l, j, y, rows(h), cols],
                           lambda n, rows=rows: W.at[l, pl.ds(0, n), y, rows(None), cols], direct)
            first.append(g.a())
        ag[l, name, 1] = first

    def s1b(l, name):
        first = ag[l, name, 1]
        if name == "d":
            got, idx = first
            h0, h1 = Wd.at[l, down_rows, quarter(0)], Wd.at[l, down_rows, quarter(1)]
            to_f = [rc(h0, h0, PZ[0], recv=idx, cond=is_p), rc(h1, h1, PZ[1], recv=idx, cond=is_m)]
            for cond, desc in zip((is_p, is_m), to_f):
                @pl.when(cond)
                def _(desc=desc):
                    got.wait_recv()
                    desc.start()
            return
        for g in first:
            g.b()

    def s2a(l, name):
        first = ag[l, name, 1]
        if name == "d":
            @pl.when(is_f)
            def _():
                first[0].wait_recv()

            def blk(j, h):
                return Wd.at[l, pl.ds(pl.multiple_of(j * DR, 16), DR), quarter(h)]
            ag[l, name, 2] = [Gather(RY, blk, lambda n: Wd.at[l, pl.ds(0, n * DR), half(D)]).a()]
            return
        W, width = REG[name]
        cols = half(width)
        paths, direct = AG_PATHS[l, name], (l, name) in AG_DIRECT
        second = []
        for path, g in zip(paths, first):
            rows = lambda h, path=path: path_rows(path, paths, h)
            g.c()
            if path == "A":
                g = Gather(RZ, lambda j, h, rows=rows: W.at[l, j, :, rows(h), cols],
                           lambda n, rows=rows: W.at[l, pl.ds(0, n), :, rows(None), cols], direct)
            else:
                g = Gather(RY, lambda j, h, rows=rows: W.at[l, :, j, rows(h), cols],
                           lambda n, rows=rows: W.at[l, :, pl.ds(0, n), rows(None), cols], direct)
            second.append(g.a())
        ag[l, name, 2] = second

    def s2b(l, name):
        for g in ag[l, name, 2]:
            g.b()

    def s3(l, name):
        for g in ag[l, name, 2]:
            g.c()
        if name == "d":
            ref = Wd.at[l, pl.ds(0, FX), half(D)]
        else:
            W, width = REG[name]
            ref = W.at[l, :, :, :, half(width)]
        ag[l, name, 3] = push(ref, ref, SIB)

    def ag_done(l, name):
        wait_recv([ag[l, name, 3]])

    class Share:
        def __init__(self, ref, three):
            self.r, self.three = new_recv(), three
            for to in PX:
                push(ref, ref, to, self.r)

        def c(self):
            wait_bytes(self.three, self.r)

    class Meet:
        def __init__(self, i, a, part):
            self.i, self.a, self.r = i, a, new_recv()
            for j in range(4):
                PS[i, a, j] = part[BH * j : BH * (j + 1)]
            for n, (j, to) in enumerate(zip(X3, PX)):
                push(PS.at[i, a, j], PRV.at[i, a, n], to, self.r)

        def c(self):
            wait_bytes(PRV.at[self.i, self.a], self.r)
            total = PS[self.i, self.a, x].astype(F32)
            for n in range(3):
                total = total + PRV[self.i, self.a, n].astype(F32)
            return total

    def rows_of(a):
        return pl.ds(TH * a, TH)

    def own(a):
        return pl.ds(pl.multiple_of(TH * a + BH * x, BH), BH)

    def share_rows(ref, a):
        return Share(ref.at[own(a)], ref.at[pl.ds(0, 3 * BH)])

    GRAD = {"q": (Gq, R1q, R2q, Sq, OUTq, FSq, 384), "o": (Go, R1o, R2o, So, OUTo, FSo, 128),
            "gu": (Ggu, R1gu, R2gu, Sgu, OUTgu, FSgu, FP)}
    rs = {}

    def grad_ref(name, l):
        if name == "gu" and l == 0:
            return Wgu.at[1, :, :, :, pl.ds(0, FP)]
        return GRAD[name][0].at[0 if name == "gu" else l]

    RS_PATHS = {(l, name): "AB" for l in range(2) for name in GRAD}
    RS_DIRECT = ((0, "q"), (0, "o"))

    def r1a(l, name):
        if name == "d":
            def part(j, h):
                return Gd.at[l, pl.ds(pl.multiple_of(j * DR, 16), DR), sub(0, 512, h)]
            rs[l, name, 1] = [Reduce(RY, part, lambda n, h: R1d.at[l, n, :, sub(0, 512, h)],
                                     lambda i0, n: R1d.at[l, pl.ds(i0, n)]).a()]
            return
        _, R1, R2, S, OUT, FS, width = GRAD[name]
        G = grad_ref(name, l)
        paths, direct = RS_PATHS[l, name], (l, name) in RS_DIRECT
        first = []
        for path in paths:
            rows = lambda h, path=path: path_rows(path, paths, h)
            buf = lambda n, h, rows=rows: R1.at[l, n, :, rows(h)]
            some = lambda i0, n, rows=rows: R1.at[l, pl.ds(i0, n), :, rows(None)]
            if path == "A":
                r = Reduce(RZ, lambda j, h, rows=rows: G.at[j, :, rows(h)], buf, some, direct)
            else:
                r = Reduce(RY, lambda j, h, rows=rows: G.at[:, j, rows(h)], buf, some, direct)
            first.append(r.a())
        rs[l, name, 1] = first

    def r1b(l, name):
        for r in rs[l, name, 1]:
            r.b()

    def r2a(l, name):
        first = rs[l, name, 1]
        if name == "d":
            first[0].c()
            Sd[l] = first[0].total().astype(BF)
            idx = new_recv()
            to = [rc(Sd.at[l, :, pl.ds(0, 256)], R2d.at[l, 0, :, pl.ds(0, 256)], PZ[1], recv=idx, cond=is_f),
                  rc(Sd.at[l, :, pl.ds(256, 256)], R2d.at[l, 0, :, pl.ds(256, 256)], PZ[0], recv=idx, cond=is_f)]

            @pl.when(is_f)
            def _():
                to[0].start()
                to[1].start()
            rs[l, name, 2] = to
            return
        _, R1, R2, S, OUT, FS, width = GRAD[name]
        paths, direct = RS_PATHS[l, name], (l, name) in RS_DIRECT
        second = []
        for path, r in zip(paths, first):
            rows = lambda h, path=path: path_rows(path, paths, h)
            r.c()
            S[l, :, rows(None)] = r.total().astype(BF)
            r = Reduce(RY if path == "A" else RZ, lambda j, h, rows=rows: S.at[l, j, rows(h)],
                       lambda n, h, rows=rows: R2.at[l, n, rows(h)],
                       lambda i0, n, rows=rows: R2.at[l, pl.ds(i0, n), rows(None)], direct)
            second.append(r.a())
        rs[l, name, 2] = second

    def r2b(l, name):
        second = rs[l, name, 2]
        if name == "d":
            idx = [new_recv(), new_recv()]
            fin = [rc(Sd.at[l], R2d.at[l, 1], PZ[1], recv=idx[0], cond=is_p),
                   rc(Sd.at[l], R2d.at[l, 2], PZ[0], recv=idx[1], cond=is_m)]
            for cond, got, h, desc in ((is_p, second[0], 0, fin[0]), (is_m, second[1], 1, fin[1])):
                @pl.when(cond)
                def _(got=got, h=h, desc=desc):
                    got.wait_recv()
                    cols = pl.ds(256 * h, 256)
                    Sd[l, :, cols] = (Sd[l, :, cols].astype(F32) + R2d[l, 0, :, cols].astype(F32)).astype(BF)
                    desc.start()
            rs[l, name, 3] = fin
            return
        for r in second:
            r.b()

    def rs3(l, name):
        idx = new_recv()
        if name == "d":
            fin = rs[l, name, 3]
            far = rc(OUTd.at[k], OUTd.at[k], PX[2], recv=idx, cond=is_src & (s == l))
            near = [rc(FSd, OUTd.at[k], PX[j], recv=idx, cond=is_src & (s != l)) for j in range(2)]

            @pl.when(is_src)
            def _():
                wait_recv(fin)
                total = (Sd[l].astype(F32) + R2d[l, 1].astype(F32) + R2d[l, 2].astype(F32)).astype(BF)

                @pl.when(s == l)
                def _():
                    OUTd[k] = total
                    far.start()

                @pl.when(s != l)
                def _():
                    FSd[...] = total
                    for desc in near:
                        desc.start()
            rs[l, name, 4] = far
            return
        _, R1, R2, S, OUT, FS, width = GRAD[name]
        paths = RS_PATHS[l, name]
        second = rs[l, name, 2]
        for r in second:
            r.c()
        sums = [(path_rows(path, paths, None), r.total().astype(BF)) for path, r in zip(paths, second)]
        slot = OUT.at[k, x]
        far = rc(slot, slot, PX[2], recv=idx, cond=(s == l))
        near = [rc(FS, slot, PX[j], recv=idx, cond=(s != l)) for j in range(2)]

        @pl.when(s == l)
        def _():
            for rows, value in sums:
                OUT[k, x, rows] = value
            far.start()

        @pl.when(s != l)
        def _():
            for rows, value in sums:
                FS[rows] = value
            for desc in near:
                desc.start()
        rs[l, name, 4] = idx

    def rs4(l, name):
        got = rs[l, name, 4]
        ref = OUTd.at[k] if name == "d" else GRAD[name][4].at[k]
        fin = rc(ref, ref, SIB, cond=(s == l))

        @pl.when(s == l)
        def _():
            if name == "d":
                @pl.when(z != x)
                def _():
                    got.wait_recv()
            else:
                wait_bytes(GRAD[name][4].at[k, pl.ds(0, 3)], got)
            fin.start()
        rs[l, name, 5] = fin

    def rs5(l, name):
        @pl.when(s == l)
        def _():
            rs[l, name, 5].wait_recv()

    landed = {}

    def edge(l, a, value):
        if l not in landed:
            landed[l] = new_recv()
        goal = 2 * a + l
        ED[l, a] = value

        @pl.when(x == goal)
        def _():
            TT[l, x] = value

        for j in range(3):
            desc = rc(ED.at[l, a], TT.at[l, x], PX[j], recv=landed[l], cond=(X3[j] == goal))

            @pl.when(X3[j] == goal)
            def _(desc=desc):
                desc.start()

    swaps = {}

    def edge_swap(l):
        swaps[l] = rc(TT.at[l, pl.ds(2 * (1 - k), 2)], EO.at[k], SIB, cond=(s == l))

        @pl.when(s == l)
        def _():
            wait_bytes(TT.at[l, pl.ds(0, 3)], landed[l])
            swaps[l].start()
            EO[k] = TT[l, pl.ds(2 * k, 2)]

    def edge_done(l):
        @pl.when(s == l)
        def _():
            swaps[l].wait_recv()

    e0 = lengths[k, 0, 0]
    e1 = e0 + lengths[k, 0, 1]
    def doc(i):
        return jnp.where(i >= e0, 1, 0) + jnp.where(i >= e1, 1, 0)

    def keys(a):
        return TH * (a + 1)

    def allowed(a):
        qi = lax.broadcasted_iota(jnp.int32, (TH, keys(a)), 0) + TH * a
        ki = lax.broadcasted_iota(jnp.int32, (TH, keys(a)), 1)
        return (doc(qi) == doc(ki)) & (ki <= qi)

    def head(value, hh):
        lane = lax.broadcasted_iota(jnp.int32, value.shape, 1)
        return jnp.where((lane < 64) if hh == 0 else (lane >= 64), value, jnp.zeros_like(value))

    def make_angles():
        row = lax.broadcasted_iota(jnp.int32, (T, T), 0)
        ki = lax.broadcasted_iota(jnp.int32, (T, T), 1)
        lane = lax.broadcasted_iota(jnp.int32, (T, 128), 1)
        start = jnp.where(row >= e1, e1, jnp.where(row >= e0, e0, 0))
        pick = jnp.where(ki == row - start, 1.0, 0.0).astype(BF)
        cos = dot(pick, angles[:, 0:128]) + dot(pick, angles[:, 128:256])
        sin = dot(pick, angles[:, 256:384]) + dot(pick, angles[:, 384:512])
        first = (lane < 32) | ((lane >= 64) & (lane < 96))
        CS[0] = cos
        CS[1] = jnp.where(first, -sin, 0.0)
        CS[2] = jnp.where(first, 0.0, sin)

    def turn(v, sign, a):
        r = rows_of(a)
        tiles = []
        for t in range(2):
            u = v[:, 128 * t : 128 * (t + 1)]
            rot = pltpu.roll(u, 96, 1) * CS[1, r] + pltpu.roll(u, 32, 1) * CS[2, r]
            tiles.append(u * CS[0, r] + rot if sign > 0 else u * CS[0, r] - rot)
        return jnp.concatenate(tiles, axis=1)

    def gain(l, i):
        tiles = []
        for t in range(8):
            a = Gn[t // 2, 2 * (t % 2), l].astype(F32) + Gn[t // 2, 2 * (t % 2) + 1, l].astype(F32)
            tiles.append(a[i : i + 1])
        return jnp.concatenate(tiles, axis=1)

    def norm_rows(ref, out, g, a):
        for b in range(2):
            r = pl.ds(TH * a + 64 * b, 64)
            v = ref[r, :].astype(F32)
            inv = lax.rsqrt(jnp.mean(v * v, axis=-1, keepdims=True) + EPS)
            out[r, :] = (v * inv * g).astype(BF)

    def wq(l):
        return Wq[l].reshape(D, 768)

    def project(l, XR, a):
        r = rows_of(a)
        norm_rows(XR, N1.at[l], gain(l, 0), a)
        n = N1[l, r]
        w = wq(l)
        QKV[l, 0, r] = turn(dot(n, w[:, 0:256]), 1, a).astype(BF)
        QKV[l, 1, r] = turn(dot(n, w[:, 256:512]), 1, a).astype(BF)
        v = dot(n, w[:, 512:768])
        if l == 1:
            v = 0.5 * v + 0.5 * QKV[0, 2, r].astype(F32)
        QKV[l, 2, r] = v.astype(BF)

    def attend(l, a):
        ok = allowed(a)
        r, nk = rows_of(a), keys(a)
        for t in range(2):
            cols = pl.ds(128 * t, 128)
            qt, kt, vt = QKV[l, 0, r, cols], QKV[l, 1, 0:nk, cols], QKV[l, 2, 0:nk, cols]
            acc = jnp.zeros((TH, 128), F32)
            for hh in range(2):
                sc = jnp.where(ok, dot_nt(head(qt, hh), kt) * 0.125, -1e30)
                ex = jnp.exp(sc - jnp.max(sc, axis=-1, keepdims=True))
                pr = (ex / jnp.sum(ex, axis=-1, keepdims=True)).astype(BF)
                PR[l, 2 * t + hh, r, 0:nk] = pr
                acc = acc + dot(pr, head(vt, hh))
            O[l, x, r, cols] = acc.astype(BF)
        return Share(O.at[l, x, r], O.at[l, pl.ds(0, 3), r])

    def feed(l, XR, got, i, a):
        r = rows_of(a)
        got.c()
        o = jnp.concatenate([O[l, b, r] for b in range(4)], axis=1)
        H[l, r] = XR[r, :].astype(F32) + dot(o, Wo[l].reshape(D, D))
        norm_rows(H.at[l], N2.at[l], gain(l, 1), a)
        if a == 0:
            ag_done(l, "gu")
        n = N2[l, r]
        GU[l, 0, r] = dot(n, Wgu[l, :, :, :, 0:FP].reshape(D, FP))
        GU[l, 1, r] = dot(n, Wgu[l, :, :, :, FP : 2 * FP].reshape(D, FP))
        for b in range(2):
            q = pl.ds(TH * a + 64 * b, 64)
            ga, up = GU[l, 0, q, :], GU[l, 1, q, :]
            M[l, q, :] = (ga * jax.nn.sigmoid(ga) * up).astype(BF)
        if a == 0:
            ag_done(l, "d")
        return Meet(i, a, dot(M[l, r], Wd[l]).astype(BF))

    def gain_grad(i, row, ref):
        total = jnp.zeros((1, D), F32)
        for a in range(2):
            for j in range(4):
                v = ref[pl.ds(TH * a + BH * j, BH), :].astype(F32)
                inv = lax.rsqrt(jnp.mean(v * v, axis=-1, keepdims=True) + EPS)
                total = total + jnp.sum(PS[i, a, j].astype(F32) * (v * inv), axis=0, keepdims=True)
        GS[0, row : row + 1] = total

    def back_ff(l, DY, i, a):
        r = rows_of(a)
        dm = dot_nt(DY[r, :], Wd[l])
        ga, up = GU[l, 0, r], GU[l, 1, r]
        sg = jax.nn.sigmoid(ga)
        DGU[l, 0, r] = (dm * up * sg * (1.0 + ga * (1.0 - sg))).astype(BF)
        DGU[l, 1, r] = (dm * ga * sg).astype(BF)
        part = (dot_nt(DGU[l, 0, r], Wgu[l, :, :, :, 0:FP].reshape(D, FP))
                + dot_nt(DGU[l, 1, r], Wgu[l, :, :, :, FP : 2 * FP].reshape(D, FP))).astype(BF)
        return Meet(i, a, part)

    def grads_d(l, DY, msib, dysib):
        wait_recv([msib, dysib])
        Gd[l] = (dot_tn(M[l], DY[:, half(D)]) + dot_tn(Ms[l], DYs[l])).astype(BF)
        r1a(l, "d")

    def grads_gu(l, nsib, gsib):
        wait_recv([nsib, gsib])
        grad_ref("gu", l)[...] = (dot_tn(N2[l], DGU[l, k]) + dot_tn(N2s[l], DGUs[l])).astype(BF).reshape(4, 4, SH, FP)
        r1a(l, "gu")

    def back_hidden(l, DY, got, a):
        dn = got.c()
        hf = H[l, own(a), :]
        inv = lax.rsqrt(jnp.mean(hf * hf, axis=-1, keepdims=True) + EPS)
        e = dn * gain(l, 1)
        dh = DY[own(a), :].astype(F32) + inv * e - hf * (inv * inv * inv) * jnp.mean(e * hf, axis=-1, keepdims=True)
        DH[l, a] = dh
        DHB[l, own(a), :] = dh.astype(BF)
        return share_rows(DHB.at[l], a)

    def back_attend(l, got, i, a):
        r, nk = rows_of(a), keys(a)
        got.c()
        do = dot_nt(DHB[l, r], Wo[l, x].reshape(HX, D)).astype(BF)
        dqs, dks, dvs = [], [], []
        for t in range(2):
            cols = pl.ds(128 * t, 128)
            qt, kt, vt = QKV[l, 0, r, cols], QKV[l, 1, 0:nk, cols], QKV[l, 2, 0:nk, cols]
            dot_ = do[:, 128 * t : 128 * (t + 1)]
            dq = jnp.zeros((TH, 128), F32)
            dk = dv = jnp.zeros((nk, 128), F32)
            for hh in range(2):
                pr = PR[l, 2 * t + hh, r, 0:nk]
                pf = pr.astype(F32)
                dom = head(dot_, hh)
                dpp = dot_nt(dom, vt)
                ds = (pf * (dpp - jnp.sum(pf * dpp, axis=-1, keepdims=True))).astype(BF)
                dq = dq + dot(ds, head(kt, hh))
                dk = dk + dot_tn(ds, head(qt, hh))
                dv = dv + dot_tn(pr, dom)
            dqs.append(dq)
            dks.append(dk)
            dvs.append(dv)
        dq, dk, dv = (jnp.concatenate(v, axis=1) for v in (dqs, dks, dvs))
        if a == 1:
            KV0[0] = dk[0:TH]
            KV0[1] = dv[0:TH]
            dk, dv = dk[TH:], dv[TH:]
        else:
            dk, dv = dk + KV0[0], dv + KV0[1]
        DP[l, r, 0:256] = turn((dq * 0.125).astype(BF).astype(F32), -1, a).astype(BF)
        DP[l, r, 256:512] = turn((dk * 0.125).astype(BF).astype(F32), -1, a).astype(BF)
        if l == 1:
            DP[l, r, 512:768] = (0.5 * dv.astype(BF).astype(F32)).astype(BF)
        else:
            DP[l, r, 512:768] = (dv + DP[1, r, 512:768].astype(F32)).astype(BF)
        return Meet(i, a, dot_nt(DP[l, r], wq(l)).astype(BF))

    def grads_q(l, n1sib, psib):
        wait_recv([n1sib, psib])
        Gq[l] = (dot_tn(N1[l], DP[l, :, half(768)]) + dot_tn(N1s[l], DPs[l])).astype(BF).reshape(4, 4, SH, 384)
        r1a(l, "q")

    def push_heads(l):
        hs = pl.ds(pl.multiple_of(x * HX + (1 - k) * 128, 128), 128)
        return push(DHB.at[l, :, hs], DHBs.at[l], SIB)

    def grads_o(l, osib, hsib):
        wait_recv([osib, hsib])
        hs = pl.ds(pl.multiple_of(x * HX + k * 128, 128), 128)
        for b in range(4):
            Go[l, b] = (dot_tn(O[l, b], DHB[l, :, hs]) + dot_tn(Os[l, b], DHBs[l])).astype(BF).reshape(4, SH, 128)
        r1a(l, "o")

    def back_input(l, XR, got, a):
        dn = got.c()
        xf = XR[own(a), :].astype(F32)
        inv = lax.rsqrt(jnp.mean(xf * xf, axis=-1, keepdims=True) + EPS)
        e = dn * gain(l, 0)
        dx = DH[l, a] + inv * e - xf * (inv * inv * inv) * jnp.mean(e * xf, axis=-1, keepdims=True)
        return dx.astype(BF)

    def gsum_a(i, to):
        idx = new_recv()
        for j, t in enumerate(to):
            push(GS.at[i], GR.at[i, j], t, idx)
        return i, len(to), idx

    def gsum_b(sent_to):
        i, n, idx = sent_to
        wait_bytes(GR.at[i, pl.ds(0, n)], idx)
        total = GS[i]
        for j in range(n):
            total = total + GR[i, j]
        GS[i + 1] = total

    X0 = E.at[0]
    DY1 = E.at[1]
    GS[0] = jnp.zeros((8, D), F32)
    for l in range(2):
        Wd[l, FX:FP, :] = jnp.zeros((FP - FX, D), BF)
    s1a(0, "q")
    g1()
    s1a(0, "o")
    s1a(0, "gu")
    s1a(0, "d")
    e_loc.wait()
    e_sib.wait_recv()
    mine2 = pl.ds(pl.multiple_of(xh * 128, 128), 128)
    e_got = push3([E.at[s, mine2]] * 3, [E.at[s, mine2]] * 3, PX)
    s2a(0, "q")
    g2()
    s1b(0, "o")
    s1b(0, "gu")
    make_angles()
    s3(0, "q")
    s2a(0, "o")
    s2a(0, "gu")
    s1b(0, "d")
    s1a(1, "q")
    g3()
    wait_recv(e_got)
    s1a(1, "o")
    s1a(1, "gu")
    s1a(1, "d")
    s2a(0, "d")
    ag_done(0, "q")
    n1sib, osib, nsib, msib = [None, None], [None, None], [None, None], [None, None]
    project(0, X0, 0)
    g0 = attend(0, 0)
    s2b(0, "o")
    s2b(0, "gu")
    project(0, X0, 1)
    n1sib[0] = push(N1.at[0], N1s.at[0], SIB)
    g1 = attend(0, 1)
    dysib = [None, push(DY1.at[:, other_half(D)], DYs.at[1], SIB)]
    s3(0, "o")
    s2b(0, "d")
    for name in ("q", "o", "gu"):
        s1b(1, name)
    s3(0, "gu")
    s2a(1, "q")
    s1b(1, "d")
    s3(0, "d")
    s2a(1, "o")
    s2a(1, "gu")
    ag_done(0, "o")
    m0 = feed(0, X0, g0, 0, 0)
    s2b(1, "q")
    m1 = feed(0, X0, g1, 0, 1)
    osib[0] = push(O.at[0], Os.at[0], SIB)
    nsib[0] = push(N2.at[0], N2s.at[0], SIB)
    msib[0] = push(M.at[0], Ms.at[0], SIB)
    s2a(1, "d")
    s2b(1, "o")
    X1[own(0), :] = (m0.c() + H[0, own(0), :]).astype(BF)
    g0 = share_rows(X1, 0)
    s2b(1, "gu")
    X1[own(1), :] = (m1.c() + H[0, own(1), :]).astype(BF)
    g1 = share_rows(X1, 1)
    s3(1, "q")
    s2b(1, "d")
    s3(1, "o")
    g0.c()
    ag_done(1, "q")
    project(1, X1, 0)
    g0 = attend(1, 0)
    s3(1, "gu")
    s3(1, "d")
    early = close()
    g1.c()
    project(1, X1, 1)
    n1sib[1] = push(N1.at[1], N1s.at[1], SIB)
    g1 = attend(1, 1)
    ag_done(1, "o")
    y0 = feed(1, X1, g0, 1, 0)
    y1 = feed(1, X1, g1, 1, 1)
    osib[1] = push(O.at[1], Os.at[1], SIB)
    nsib[1] = push(N2.at[1], N2s.at[1], SIB)
    msib[1] = push(M.at[1], Ms.at[1], SIB)

    m1 = back_ff(1, DY1, 2, 1)
    m0 = back_ff(1, DY1, 2, 0)
    gsib = push(DGU.at[1, 1 - k], DGUs.at[1], SIB)
    grads_d(1, DY1, msib[1], dysib[1])
    g1 = back_hidden(1, DY1, m1, 1)
    grads_gu(1, nsib[1], gsib)
    g0 = back_hidden(1, DY1, m0, 0)
    r1b(1, "d")
    m1 = back_attend(1, g1, 3, 1)
    m0 = back_attend(1, g0, 3, 0)
    hsib = push_heads(1)
    psib = push(DP.at[1, :, other_half(768)], DPs.at[1], SIB)
    r1b(1, "gu")
    edge(1, 0, (y0.c() + H[1, own(0), :]).astype(BF))
    edge(1, 1, (y1.c() + H[1, own(1), :]).astype(BF))
    grads_q(1, n1sib[1], psib)
    DY0[own(1), :] = back_input(1, X1, m1, 1)
    g1 = share_rows(DY0, 1)
    DY0[own(0), :] = back_input(1, X1, m0, 0)
    g0 = share_rows(DY0, 0)
    r2a(1, "d")
    grads_o(1, osib[1], hsib)
    r2a(1, "gu")

    g1.c()
    m1 = back_ff(0, DY0, 4, 1)
    g0.c()
    m0 = back_ff(0, DY0, 4, 0)
    gsib = push(DGU.at[0, 1 - k], DGUs.at[0], SIB)
    dysib[0] = push(DY0.at[:, other_half(D)], DYs.at[0], SIB)
    r2b(1, "d")
    r1b(1, "q")
    flush(0, early)
    grads_d(0, DY0, msib[0], dysib[0])
    g1 = back_hidden(0, DY0, m1, 1)
    grads_gu(0, nsib[0], gsib)
    g0 = back_hidden(0, DY0, m0, 0)
    r1b(1, "o")
    r2b(1, "gu")
    m1 = back_attend(0, g1, 5, 1)
    m0 = back_attend(0, g0, 5, 0)
    hsib = push_heads(0)
    psib = push(DP.at[0, :, other_half(768)], DPs.at[0], SIB)
    r1b(0, "d")
    gain_grad(5, 0, X0)
    gain_grad(4, 1, H.at[0])
    gain_grad(3, 2, X1)
    gain_grad(2, 3, H.at[1])
    g = gsum_a(0, PX)
    r1b(0, "gu")
    grads_q(0, n1sib[0], psib)
    grads_o(0, osib[0], hsib)
    r2a(1, "q")
    r2a(1, "o")
    edge(0, 1, back_input(0, X0, m1, 1))
    edge(0, 0, back_input(0, X0, m0, 0))
    rs3(1, "d")
    r2a(0, "d")
    gsum_b(g)
    g = gsum_a(1, PY)
    r2a(0, "gu")
    r2a(0, "q")
    r2a(0, "o")
    edge_swap(0)
    r2b(0, "d")
    rs3(1, "gu")
    gsum_b(g)
    g = gsum_a(2, PZ)
    r2b(1, "q")
    r2b(1, "o")
    r2b(0, "gu")
    edge_swap(1)
    rs4(1, "d")
    rs3(0, "q")
    rs3(0, "o")
    rs3(0, "d")
    gsum_b(g)
    g = gsum_a(3, [SIB])
    rs3(1, "q")
    rs3(1, "o")
    rs3(0, "gu")
    rs4(1, "gu")
    rs4(0, "q")
    rs4(0, "o")
    rs4(0, "d")
    rs4(1, "q")
    rs4(1, "o")
    gsum_b(g)
    edge_done(0)
    edge_done(1)
    rs4(0, "gu")
    for name in ("d", "q", "o", "gu"):
        rs5(1, name)
        rs5(0, name)
    outs = [local(a, b) for a, b in
            ((OUTq, oq_hbm), (OUTo, oo_hbm), (OUTgu, ogu_hbm), (OUTd, od_hbm), (EO, edge_hbm), (GS.at[4], gsum_hbm))]
    for o in outs:
        o.start()
    flush(early, len(groups))
    flush_conditional()
    for o in outs:
        o.wait()
    assert counter[0] <= N_RECV and counter[1] <= N_LOC and counter[2] <= N_SEND, counter


def epilogue(*refs):
    given, (edges, qkv, out, gate, up, down, gg), held, sem = refs[:6], refs[6:13], refs[13:19], refs[19]
    copies = [pltpu.make_async_copy(a, b, sem.at[i]) for i, (a, b) in enumerate(zip(given, held))]
    for cp in copies:
        cp.start()
    for cp in copies:
        cp.wait()
    oq, oo, ogu, od, edge, gsum = held
    s = lax.axis_index("section")
    dp = lax.axis_index("dp")
    edges[0, :, 0] = edge[...].reshape(2, BT, D)
    for x in range(4):
        a, b = oq[0, x].astype(F32), oq[1, x].astype(F32)
        qkv[0, :, HX * x : HX * (x + 1)] = a[:, 0:256]
        qkv[0, :, D + HX * x : D + HX * x + 128] = a[:, 256:384]
        qkv[0, :, D + HX * x + 128 : D + HX * (x + 1)] = b[:, 0:128]
        qkv[0, :, 2 * D + HX * x : 2 * D + HX * (x + 1)] = b[:, 128:384]
        for h in range(2):
            out[0, :, HX * x + 128 * h : HX * x + 128 * (h + 1)] = oo[h, x].astype(F32)
    for h, ref in ((0, gate), (1, up)):
        for p in range(2):
            a = ogu[h, 2 * p].astype(F32)
            b = pltpu.roll(ogu[h, 2 * p + 1].astype(F32), 64, 1)
            c = 2 * FX * p
            ref[0, :, c : c + 640] = a[:, 0:640]
            ref[0, :, c + 640 : c + 768] = a[:, 640:768] + b[:, 0:128]
            ref[0, :, c + 768 : c + 2 * FX] = b[:, 128:768]
    for h in range(2):
        down[0, :, 512 * h : 512 * (h + 1)] = od[h].astype(F32)
    tile = gsum[:, pl.ds(pl.multiple_of(128 * lax.div(dp, 2), 128), 128)]
    tile = jnp.where(lax.rem(dp, 2) == 1, pltpu.roll(tile, 64, 1), tile)
    rows = jnp.where(s == 1, tile[2:4], tile[0:2])
    gg[0] = rows[:, 0:SH]


def run_kernel(lengths, ends, qkv_w, out_w, gate_w, up_w, down_w, gains, angles):
    V = pltpu.VMEM
    sh = jax.ShapeDtypeStruct
    any_ = pl.BlockSpec(memory_space=pl.ANY)
    vm = pl.BlockSpec(memory_space=pltpu.VMEM)
    out_shape = [
        sh((2, 4, SH, 384), BF), sh((2, 4, SH, 128), BF), sh((2, 4, SH, FP), BF), sh((2, DR, 512), BF),
        sh((2, 2, BH, D), BF), sh((8, D), F32), sh((GROUP_BYTES // 4096, 16, 128), BF),
    ]
    scratch = [
        V((2, 4, 4, SH, 768), BF), V((2, 4, 4, SH, D), BF), V((2, 4, 4, SH, 2 * FP), BF), V((2, FP, D), BF),
        V((4, 4, 2, 16, 128), BF),
        V((2, T, D), BF), V((T, D), BF), V((T, D), BF),
        V((2, T, D), BF), V((2, T, D), BF), V((2, T, D), BF), V((2, T, D), BF),
        V((2, T, D), F32), V((2, 3, T, HX), BF), V((2, 4, T, T), BF),
        V((2, 4, T, HX), BF), V((2, 4, T, HX), BF),
        V((2, 2, T, FP), F32), V((2, T, FP), BF), V((2, T, FP), BF),
        V((2, 2, T, FP), BF), V((2, T, FP), BF),
        V((2, T, 768), BF), V((2, T, 384), BF),
        V((2, T, D), BF), V((2, T, 128), BF), V((2, T, 512), BF), V((2, 2, BH, D), F32),
        V((2, TH, HX), F32), V((2, 2, BH, D), BF),
        V((6, 2, 4, BH, D), BF), V((6, 2, 3, BH, D), BF),
        V((2, 4, 4, SH, 384), BF), V((2, 4, 4, SH, 128), BF), V((1, 4, 4, SH, FP), BF), V((2, FP, 512), BF),
        V((2, 3, 4, SH, 384), BF), V((2, 3, 4, SH, 128), BF), V((2, 3, 4, SH, FP), BF), V((2, 3, DR, 512), BF),
        V((2, 3, SH, 384), BF), V((2, 3, SH, 128), BF), V((2, 3, SH, FP), BF), V((2, 3, DR, 512), BF),
        V((2, 4, SH, 384), BF), V((2, 4, SH, 128), BF), V((2, 4, SH, FP), BF), V((2, DR, 512), BF),
        V((2, 4, SH, 384), BF), V((2, 4, SH, 128), BF), V((2, 4, SH, FP), BF), V((2, DR, 512), BF),
        V((SH, 384), BF), V((SH, 128), BF), V((SH, FP), BF), V((DR, 512), BF),
        V((5, 8, D), F32), V((4, 3, 8, D), F32), V((2, 4, BH, D), BF), V((2, 2, BH, D), BF),
        V((3, T, 128), F32), V((SH, 384), BF), V((SH, FP), BF), V((SH, 512), BF), V((DR, 512), BF),
        V((16, 128), BF), V((16, 128), F32),
        pltpu.SemaphoreType.DMA((N_SEND,)), pltpu.SemaphoreType.DMA((N_RECV,)), pltpu.SemaphoreType.DMA((N_LOC,)),
    ]
    return pl.pallas_call(
        kernel,
        out_shape=out_shape,
        in_specs=[pl.BlockSpec(memory_space=pltpu.SMEM)] + [any_] * 6 + [vm] * 2,
        out_specs=[any_] * 7,
        scratch_shapes=scratch,
        name="two_layers",
        compiler_params=pltpu.CompilerParams(
            collective_id=0, has_side_effects=True, vmem_limit_bytes=64 * 1024 * 1024 - 65536
        ),
    )(lengths, ends, qkv_w, out_w, gate_w, up_w, down_w, gains, angles)


def angle_table():
    pos = np.arange(T, dtype=np.float64)[:, None]
    freq = 10000.0 ** (-(np.arange(128) % 32) / 32.0)
    parts = []
    for v in (np.cos(pos * freq), np.sin(pos * freq)):
        high = v.astype(jnp.bfloat16)
        parts += [high, (v - high.astype(np.float64)).astype(jnp.bfloat16)]
    return np.concatenate(parts, axis=1)


def per_device(ends_in, lengths, qkv_w, out_w, gate_w, up_w, down_w, gains):
    oq, oo, ogu, od, edge, gsum, _ = run_kernel(
        lengths, ends_in, qkv_w, out_w, gate_w, up_w, down_w, gains, jnp.asarray(angle_table()))
    sh = jax.ShapeDtypeStruct
    return pl.pallas_call(
        epilogue,
        out_shape=[
            sh((1, 2, 1, BT, D), BF), sh((1, SH, 3 * D), F32), sh((1, SH, D), F32), sh((1, SH, FF), F32),
            sh((1, SH, FF), F32), sh((1, DR, D), F32), sh((1, 2, SH), F32),
        ],
        in_specs=[pl.BlockSpec(memory_space=pl.ANY)] * 6,
        out_specs=[pl.BlockSpec(memory_space=pltpu.VMEM)] * 7,
        scratch_shapes=[pltpu.VMEM(v.shape, v.dtype) for v in (oq, oo, ogu, od, edge, gsum)]
        + [pltpu.SemaphoreType.DMA((6,))],
        name="place_outputs",
        compiler_params=pltpu.CompilerParams(vmem_limit_bytes=63 * 1024 * 1024),
    )(oq, oo, ogu, od, edge, gsum)


def solution(mesh):
    in_specs = (
        P("section", None, "dp", "ctx", None),
        P(None, "dp", None),
        P("section", "dp", None),
        P("section", "dp", None),
        P("section", "dp", None),
        P("section", "dp", None),
        P("section", "dp", None),
        P("section", None, "dp"),
    )
    out_specs = (
        P("section", None, "dp", "ctx", None),
        P("section", "dp", None),
        P("section", "dp", None),
        P("section", "dp", None),
        P("section", "dp", None),
        P("section", "dp", None),
        P("section", None, "dp"),
    )
    return jax.shard_map(per_device, mesh=mesh, in_specs=in_specs, out_specs=out_specs, check_vma=False)
```

```python
import jax
import jax.numpy as jnp
import numpy as np
from jax import lax
from jax.experimental import pallas as pl
from jax.experimental.pallas import tpu as pltpu
from jax.sharding import PartitionSpec as P

T = 256
D = 1024
FF = 2816
FX = FF // 4
FP = 768
HX = 256
SH = 64
DR = 176
BT = 64
TH = 128
BH = 32
EPS = 1e-5
MESH = pl.DeviceIdType.MESH
BF = jnp.bfloat16
F32 = jnp.float32


def dot(a, b):
    return jnp.dot(a, b, preferred_element_type=F32)


def dot_nt(a, b):
    return lax.dot_general(a, b, (((1,), (1,)), ((), ())), preferred_element_type=F32)


def dot_tn(a, b):
    return lax.dot_general(a, b, (((0,), (0,)), ((), ())), preferred_element_type=F32)


N_SEND = 76
N_RECV = 244
N_LOC = 18
GROUP_BYTES = 4 * 1024 * 1024


def kernel(
    lengths, ends, q_w, o_w, gate_w, up_w, d_w, gains, angles,
    oq_hbm, oo_hbm, ogu_hbm, od_hbm, edge_hbm, gsum_hbm, dummy,
    Wq, Wo, Wgu, Wd, Gn,
    E, X1, DY0, N1, N1s, N2, N2s, H, QKV, PR, O, Os, GU, M, Ms, DGU, DGUs, DP, DPs, DHB, DHBs, DYs, DH, KV0, ED,
    PS, PRV,
    Gq, Go, Ggu, Gd, R1q, R1o, R1gu, R1d, R2q, R2o, R2gu, R2d, Sq, So, Sgu, Sd, OUTq, OUTo, OUTgu, OUTd,
    FSq, FSo, FSgu, FSd, GS, GR, TT, EO,
    CS, QT, GT, OT, DT, NT, gain_in,
    ssem, rsem, lsem,
):
    s = lax.axis_index("section")
    dp = lax.axis_index("dp")
    c = lax.axis_index("ctx")
    xh = lax.div(c, 2)
    k = lax.rem(c, 2)
    x = xh * 2 + s
    z = lax.div(dp, 4)
    y = lax.rem(dp, 4)

    def dev(x_, y_, z_, k_):
        return (lax.rem(x_, 2), z_ * 4 + y_, lax.div(x_, 2) * 2 + k_)

    def ring(v):
        return [lax.rem(v + 1, 4), lax.rem(v + 3, 4), lax.rem(v + 2, 4)]

    X3, Y3, Z3 = ring(x), ring(y), ring(z)
    PX = [dev(v, y, z, k) for v in X3]
    PY = [dev(x, v, z, k) for v in Y3]
    PZ = [dev(x, y, v, k) for v in Z3]
    SIB = dev(x, y, z, 1 - k)

    bar = pltpu.get_barrier_semaphore()
    partners = PX + PY + PZ + [SIB]
    for p in partners:
        pl.semaphore_signal(bar, inc=1, device_id=p, device_id_type=MESH)

    counter = [0, 0, 0]
    sent = []
    groups = []

    def size(ref):
        n = 2 if ref.dtype == BF else 4
        for v in ref.shape:
            n *= v
        return n

    def new_recv():
        counter[0] += 1
        return counter[0] - 1

    def rc(src, dst, to, recv=None, cond=None):
        recv = new_recv() if recv is None else recv
        if cond is None:
            if not groups or groups[-1][2] or groups[-1][1] + size(src) > GROUP_BYTES:
                groups.append([counter[2], 0, False])
                counter[2] += 1
            groups[-1][1] += size(src)
            i = groups[-1][0]
        else:
            i = counter[2]
            counter[2] += 1
        desc = pltpu.make_async_remote_copy(
            src_ref=src, dst_ref=dst, send_sem=ssem.at[i], recv_sem=rsem.at[recv],
            device_id=to, device_id_type=MESH,
        )
        if cond is not None:
            sent.append((cond, desc))
        return desc

    def push(src, dst, to, recv=None):
        desc = rc(src, dst, to, recv)
        desc.start()
        return desc

    def push3(srcs, dsts, to):
        return [push(a, b, t) for a, b, t in zip(srcs, dsts, to)]

    def wait_recv(descs):
        for desc in descs:
            desc.wait_recv()

    def wait_bytes(ref, recv):
        pltpu.make_async_remote_copy(
            src_ref=ref, dst_ref=ref, send_sem=ssem.at[0], recv_sem=rsem.at[recv], device_id=SIB, device_id_type=MESH,
        ).wait_recv()

    def close():
        if groups:
            groups[-1][2] = True
        return len(groups)

    def flush(first, last):
        for i, total, _ in groups[first:last]:
            ref = dummy.at[pl.ds(0, total // 4096)]
            pltpu.make_async_copy(ref, ref, ssem.at[i]).wait()

    def flush_conditional():
        for cond, desc in sent:
            @pl.when(cond)
            def _(desc=desc):
                desc.wait_send()

    class Gather:
        def __init__(self, ring, blk, some, direct=False):
            (self.p, self.m, self.o), self.me, self.to = ring
            self.blk, self.some, self.direct = blk, some, direct

        def a(self):
            self.r = [new_recv() for _ in range(1 if self.direct else 3)]
            if self.direct:
                for to in self.to:
                    push(self.blk(self.me, None), self.blk(self.me, None), to, self.r[0])
                return self
            h0, h1 = self.blk(self.me, 0), self.blk(self.me, 1)
            push(h0, h0, self.to[0], self.r[0])
            push(h1, h1, self.to[1], self.r[1])
            push(h1, h1, self.to[0], self.r[2])
            push(h0, h0, self.to[1], self.r[2])
            return self

        def b(self):
            if not self.direct:
                left, right = self.blk(self.m, 0), self.blk(self.p, 1)
                wait_bytes(left, self.r[0])
                push(left, left, self.to[0], self.r[2])
                wait_bytes(right, self.r[1])
                push(right, right, self.to[1], self.r[2])
            return self

        def c(self):
            if self.direct:
                wait_bytes(self.some(3), self.r[0])
            else:
                wait_bytes(self.some(2), self.r[2])

    class Reduce:
        def __init__(self, ring, part, buf, some, direct=False):
            (self.p, self.m, self.o), self.me, self.to = ring
            self.part, self.buf, self.some, self.direct = part, buf, some, direct
            self.terms = (0, 1, 2) if direct else (1, 2)

        def a(self):
            self.r = [new_recv() for _ in range(1 if self.direct else 3)]
            part, buf = self.part, self.buf
            if self.direct:
                for i, (j, to) in enumerate(zip((self.p, self.m, self.o), self.to)):
                    push(part(j, None), buf(i, None), to, self.r[0])
                return self
            push(part(self.o, 0), buf(0, 0), self.to[0], self.r[0])
            push(part(self.o, 1), buf(0, 1), self.to[1], self.r[1])
            push(part(self.p, 1), buf(1, 1), self.to[0], self.r[2])
            push(part(self.m, 0), buf(2, 0), self.to[1], self.r[2])
            return self

        def b(self):
            if self.direct:
                return self
            part, buf = self.part, self.buf
            for h, j, to in ((0, self.p, self.to[0]), (1, self.m, self.to[1])):
                ref, got = part(j, h), buf(0, h)
                wait_bytes(got, self.r[h])
                ref[...] = (ref[...].astype(F32) + got[...].astype(F32)).astype(BF)
                push(ref, buf(1 + h, h), to, self.r[2])
            return self

        def c(self):
            if self.direct:
                wait_bytes(self.some(0, 3), self.r[0])
            else:
                wait_bytes(self.some(1, 2), self.r[2])

        def total(self):
            value = self.part(self.me, None)[...].astype(F32)
            for i in self.terms:
                value = value + self.buf(i, None)[...].astype(F32)
            return value

    RX, RY, RZ = (X3, x, PX), (Y3, y, PY), (Z3, z, PZ)

    def path_rows(path, paths, h):
        n = 64 // len(paths)
        base = n * paths.index(path)
        return pl.ds(base, n) if h is None else pl.ds(base + h * (n // 2), n // 2)

    def sub(base, width, h):
        return pl.ds(base, width) if h is None else pl.ds(base + h * (width // 2), width // 2)

    def local(src, dst):
        i = counter[1]
        counter[1] += 1
        return pltpu.make_async_copy(src, dst, lsem.at[i])

    def half(width):
        return pl.ds(pl.multiple_of(k * (width // 2), 128), width // 2)

    def other_half(width):
        return pl.ds(pl.multiple_of((1 - k) * (width // 2), 128), width // 2)

    tx = lax.rem(x + 3 - 2 * k, 4)
    TO = dev(tx, y, z, k)
    REG = {"q": (Wq, 768), "o": (Wo, 1024), "gu": (Wgu, 2 * FP)}
    pre = {}
    down_rows = pl.ds(pl.multiple_of(y * DR, 16), DR)
    slices = (x, tx)
    q_in = GU.at[1, 0, pl.ds(128, 128), pl.ds(0, 384)]
    gu_in = GU.at[1, 0, pl.ds(0, 128), :]
    d_in = GU.at[1, 1, pl.ds(0, DR), pl.ds(0, 512)]
    o_in = GU.at[1, 1, pl.ds(192, SH), pl.ds(0, 512)]
    q_cp = []
    for j in range(2):
        for i in range(3):
            piece = 3 * k + i
            col = D * lax.div(piece, 2) + HX * slices[j] + 128 * lax.rem(piece, 2)
            q_cp.append(local(q_w.at[0, :, pl.ds(pl.multiple_of(col, 128), 128)],
                              GU.at[1, 0, pl.ds(128 + SH * j, SH), pl.ds(128 * i, 128)]))
    o_cp = local(o_w.at[0, :, half(D)], o_in)
    d_cp = local(d_w.at[0, :, half(D)], d_in)
    gu_cp = []
    for w in (gate_w, up_w):
        pair = []
        for j in range(2):
            col = 2 * FX * lax.div(slices[j], 2) + (FX - 64) * lax.rem(slices[j], 2)
            pair.append((w.at[0, :, pl.ds(pl.multiple_of(col, 128), FP)], GU.at[1, 0, pl.ds(SH * j, SH), :]))
        gu_cp.append(pair)
    gu_cp = [[local(*c) for c in gu_cp[0]], None, gu_cp[1]]
    gu_cp[1] = [pltpu.make_async_copy(*c, lsem.at[counter[1] - 2 + j]) for j, c in enumerate(gu_cp.pop())]
    for cp in q_cp:
        cp.start()
    for kk in range(2):
        @pl.when(k == kk)
        def _(kk=kk):
            for cp in gu_cp[kk]:
                cp.start()
    o_cp.start()
    d_cp.start()

    odd = lax.rem(dp, 2) == 1
    gz = jnp.zeros((2, SH), F32)
    gv = gains[0].astype(F32)
    NT[...] = jnp.zeros((16, 128), BF)
    gain_in[...] = jnp.zeros((16, 128), F32)
    gain_in[0:2, :] = jnp.where(odd, jnp.concatenate([gz, gv], axis=1), jnp.concatenate([gv, gz], axis=1))
    NT[...] = gain_in[...].astype(BF)
    Gn[z, y, s] = NT[...]
    pl.semaphore_wait(bar, len(partners))
    pre["g"] = rc(NT, Gn.at[z, y, s], TO)
    pre["g"].start()

    for cp in q_cp:
        cp.wait()
    QT[...] = q_in[SH : 2 * SH, :].astype(BF)
    pre["q"] = rc(QT, Wq.at[s, z, y, :, half(768)], TO)
    pre["q"].start()
    Wq[s, z, y, :, half(768)] = q_in[0:SH, :].astype(BF)

    o_cp.wait()
    OT[...] = o_in[...].astype(BF)
    pre["o"] = rc(OT, Wo.at[s, z, y, :, half(D)], TO)
    pre["o"].start()
    Wo[s, z, y, :, half(D)] = OT[...]

    wide = lax.broadcasted_iota(jnp.int32, (SH, FP), 1)

    def hidden_slice(j):
        v = gu_in[SH * j : SH * (j + 1), :]
        v = jnp.where(lax.rem(slices[j], 2) == 1, pltpu.roll(v, FP - 64, 1), v)
        return jnp.where(wide < FX, v, 0.0).astype(BF)

    for cp in gu_cp[0]:
        cp.wait()
    GT[...] = hidden_slice(1)
    pre["gu"] = rc(GT, Wgu.at[s, z, y, :, half(2 * FP)], TO)
    pre["gu"].start()
    Wgu[s, z, y, :, half(2 * FP)] = hidden_slice(0)

    d_cp.wait()
    DT[...] = d_in[...].astype(BF)
    pre["d"] = rc(DT, Wd.at[s, down_rows, half(D)], TO, cond=(z == tx))

    @pl.when(z == tx)
    def _():
        pre["d"].start()

    @pl.when(z == x)
    def _():
        Wd[s, down_rows, half(D)] = DT[...]

    mine = pl.ds(pl.multiple_of(xh * 128 + k * 64, 64), 64)
    e_loc = local(ends.at[0, k, 0], E.at[s, mine])
    e_loc.start()
    e_sib = push(ends.at[0, 1 - k, 0], E.at[s, mine], SIB)

    ag = {}

    def ready(l, name):
        @pl.when(s != l)
        def _():
            pre[name].wait_recv()

    def quarter(h):
        return half(D) if h is None else pl.ds(pl.multiple_of(k * 512 + h * 256, 128), 256)

    is_src, is_p, is_m, is_f = z == x, z == X3[0], z == X3[1], z == X3[2]

    AG_PATHS = {(l, name): "AB" for l in range(2) for name in REG}
    AG_DIRECT = ((0, "q"),)

    def g1():
        for l in range(2):
            ready(l, "g")
        ref = Gn.at[z, y]
        ag["g"] = new_recv()
        for to in PY:
            push(ref, ref, to, ag["g"])

    def g2():
        wait_bytes(Gn.at[z, pl.ds(0, 3)], ag["g"])
        ref = Gn.at[z]
        ag["g"] = new_recv()
        for to in PZ:
            push(ref, ref, to, ag["g"])

    def g3():
        wait_bytes(Gn.at[pl.ds(0, 3)], ag["g"])

    def s1a(l, name):
        if name == "d":
            ref = Wd.at[l, down_rows, half(D)]
            idx = new_recv()
            up = rc(ref, ref, PZ[0], recv=idx, cond=is_src)
            dn = rc(ref, ref, PZ[1], recv=idx, cond=is_src)

            @pl.when(is_src)
            def _():
                ready(l, "d")
                up.start()
                dn.start()
            ag[l, "d", 1] = up, idx
            return
        ready(l, name)
        W, width = REG[name]
        cols = half(width)
        paths, direct = AG_PATHS[l, name], (l, name) in AG_DIRECT
        first = []
        for path in paths:
            rows = lambda h, path=path: path_rows(path, paths, h)
            if path == "A":
                g = Gather(RY, lambda j, h, rows=rows: W.at[l, z, j, rows(h), cols],
                           lambda n, rows=rows: W.at[l, z, pl.ds(0, n), rows(None), cols], direct)
            else:
                g = Gather(RZ, lambda j, h, rows=rows: W.at[l, j, y, rows(h), cols],
                           lambda n, rows=rows: W.at[l, pl.ds(0, n), y, rows(None), cols], direct)
            first.append(g.a())
        ag[l, name, 1] = first

    def s1b(l, name):
        first = ag[l, name, 1]
        if name == "d":
            got, idx = first
            h0, h1 = Wd.at[l, down_rows, quarter(0)], Wd.at[l, down_rows, quarter(1)]
            to_f = [rc(h0, h0, PZ[0], recv=idx, cond=is_p), rc(h1, h1, PZ[1], recv=idx, cond=is_m)]
            for cond, desc in zip((is_p, is_m), to_f):
                @pl.when(cond)
                def _(desc=desc):
                    got.wait_recv()
                    desc.start()
            return
        for g in first:
            g.b()

    def s2a(l, name):
        first = ag[l, name, 1]
        if name == "d":
            @pl.when(is_f)
            def _():
                first[0].wait_recv()

            def blk(j, h):
                return Wd.at[l, pl.ds(pl.multiple_of(j * DR, 16), DR), quarter(h)]
            ag[l, name, 2] = [Gather(RY, blk, lambda n: Wd.at[l, pl.ds(0, n * DR), half(D)]).a()]
            return
        W, width = REG[name]
        cols = half(width)
        paths, direct = AG_PATHS[l, name], (l, name) in AG_DIRECT
        second = []
        for path, g in zip(paths, first):
            rows = lambda h, path=path: path_rows(path, paths, h)
            g.c()
            if path == "A":
                g = Gather(RZ, lambda j, h, rows=rows: W.at[l, j, :, rows(h), cols],
                           lambda n, rows=rows: W.at[l, pl.ds(0, n), :, rows(None), cols], direct)
            else:
                g = Gather(RY, lambda j, h, rows=rows: W.at[l, :, j, rows(h), cols],
                           lambda n, rows=rows: W.at[l, :, pl.ds(0, n), rows(None), cols], direct)
            second.append(g.a())
        ag[l, name, 2] = second

    def s2b(l, name):
        for g in ag[l, name, 2]:
            g.b()

    def s3(l, name):
        for g in ag[l, name, 2]:
            g.c()
        if name == "d":
            ref = Wd.at[l, pl.ds(0, FX), half(D)]
        else:
            W, width = REG[name]
            ref = W.at[l, :, :, :, half(width)]
        ag[l, name, 3] = push(ref, ref, SIB)

    def ag_done(l, name):
        wait_recv([ag[l, name, 3]])

    class Share:
        def __init__(self, ref, three):
            self.r, self.three = new_recv(), three
            for to in PX:
                push(ref, ref, to, self.r)

        def c(self):
            wait_bytes(self.three, self.r)

    class Meet:
        def __init__(self, i, a, part):
            self.i, self.a, self.r = i, a, new_recv()
            for j in range(4):
                PS[i, a, j] = part[BH * j : BH * (j + 1)]
            for n, (j, to) in enumerate(zip(X3, PX)):
                push(PS.at[i, a, j], PRV.at[i, a, n], to, self.r)

        def c(self):
            wait_bytes(PRV.at[self.i, self.a], self.r)
            total = PS[self.i, self.a, x].astype(F32)
            for n in range(3):
                total = total + PRV[self.i, self.a, n].astype(F32)
            return total

    def rows_of(a):
        return pl.ds(TH * a, TH)

    def own(a):
        return pl.ds(pl.multiple_of(TH * a + BH * x, BH), BH)

    def share_rows(ref, a):
        return Share(ref.at[own(a)], ref.at[pl.ds(0, 3 * BH)])

    GRAD = {"q": (Gq, R1q, R2q, Sq, OUTq, FSq, 384), "o": (Go, R1o, R2o, So, OUTo, FSo, 128),
            "gu": (Ggu, R1gu, R2gu, Sgu, OUTgu, FSgu, FP)}
    rs = {}

    def grad_ref(name, l):
        if name == "gu" and l == 0:
            return Wgu.at[1, :, :, :, pl.ds(0, FP)]
        return GRAD[name][0].at[0 if name == "gu" else l]

    RS_PATHS = {(l, name): "AB" for l in range(2) for name in GRAD}
    RS_DIRECT = ((0, "q"), (0, "o"))

    def r1a(l, name):
        if name == "d":
            def part(j, h):
                return Gd.at[l, pl.ds(pl.multiple_of(j * DR, 16), DR), sub(0, 512, h)]
            rs[l, name, 1] = [Reduce(RY, part, lambda n, h: R1d.at[l, n, :, sub(0, 512, h)],
                                     lambda i0, n: R1d.at[l, pl.ds(i0, n)]).a()]
            return
        _, R1, R2, S, OUT, FS, width = GRAD[name]
        G = grad_ref(name, l)
        paths, direct = RS_PATHS[l, name], (l, name) in RS_DIRECT
        first = []
        for path in paths:
            rows = lambda h, path=path: path_rows(path, paths, h)
            buf = lambda n, h, rows=rows: R1.at[l, n, :, rows(h)]
            some = lambda i0, n, rows=rows: R1.at[l, pl.ds(i0, n), :, rows(None)]
            if path == "A":
                r = Reduce(RZ, lambda j, h, rows=rows: G.at[j, :, rows(h)], buf, some, direct)
            else:
                r = Reduce(RY, lambda j, h, rows=rows: G.at[:, j, rows(h)], buf, some, direct)
            first.append(r.a())
        rs[l, name, 1] = first

    def r1b(l, name):
        for r in rs[l, name, 1]:
            r.b()

    def r2a(l, name):
        first = rs[l, name, 1]
        if name == "d":
            first[0].c()
            Sd[l] = first[0].total().astype(BF)
            idx = new_recv()
            to = [rc(Sd.at[l, :, pl.ds(0, 256)], R2d.at[l, 0, :, pl.ds(0, 256)], PZ[1], recv=idx, cond=is_f),
                  rc(Sd.at[l, :, pl.ds(256, 256)], R2d.at[l, 0, :, pl.ds(256, 256)], PZ[0], recv=idx, cond=is_f)]

            @pl.when(is_f)
            def _():
                to[0].start()
                to[1].start()
            rs[l, name, 2] = to
            return
        _, R1, R2, S, OUT, FS, width = GRAD[name]
        paths, direct = RS_PATHS[l, name], (l, name) in RS_DIRECT
        second = []
        for path, r in zip(paths, first):
            rows = lambda h, path=path: path_rows(path, paths, h)
            r.c()
            S[l, :, rows(None)] = r.total().astype(BF)
            r = Reduce(RY if path == "A" else RZ, lambda j, h, rows=rows: S.at[l, j, rows(h)],
                       lambda n, h, rows=rows: R2.at[l, n, rows(h)],
                       lambda i0, n, rows=rows: R2.at[l, pl.ds(i0, n), rows(None)], direct)
            second.append(r.a())
        rs[l, name, 2] = second

    def r2b(l, name):
        second = rs[l, name, 2]
        if name == "d":
            idx = [new_recv(), new_recv()]
            fin = [rc(Sd.at[l], R2d.at[l, 1], PZ[1], recv=idx[0], cond=is_p),
                   rc(Sd.at[l], R2d.at[l, 2], PZ[0], recv=idx[1], cond=is_m)]
            for cond, got, h, desc in ((is_p, second[0], 0, fin[0]), (is_m, second[1], 1, fin[1])):
                @pl.when(cond)
                def _(got=got, h=h, desc=desc):
                    got.wait_recv()
                    cols = pl.ds(256 * h, 256)
                    Sd[l, :, cols] = (Sd[l, :, cols].astype(F32) + R2d[l, 0, :, cols].astype(F32)).astype(BF)
                    desc.start()
            rs[l, name, 3] = fin
            return
        for r in second:
            r.b()

    def rs3(l, name):
        idx = new_recv()
        if name == "d":
            fin = rs[l, name, 3]
            far = rc(OUTd.at[k], OUTd.at[k], PX[2], recv=idx, cond=is_src & (s == l))
            near = [rc(FSd, OUTd.at[k], PX[j], recv=idx, cond=is_src & (s != l)) for j in range(2)]

            @pl.when(is_src)
            def _():
                wait_recv(fin)
                total = (Sd[l].astype(F32) + R2d[l, 1].astype(F32) + R2d[l, 2].astype(F32)).astype(BF)

                @pl.when(s == l)
                def _():
                    OUTd[k] = total
                    far.start()

                @pl.when(s != l)
                def _():
                    FSd[...] = total
                    for desc in near:
                        desc.start()
            rs[l, name, 4] = far
            return
        _, R1, R2, S, OUT, FS, width = GRAD[name]
        paths = RS_PATHS[l, name]
        second = rs[l, name, 2]
        for r in second:
            r.c()
        sums = [(path_rows(path, paths, None), r.total().astype(BF)) for path, r in zip(paths, second)]
        slot = OUT.at[k, x]
        far = rc(slot, slot, PX[2], recv=idx, cond=(s == l))
        near = [rc(FS, slot, PX[j], recv=idx, cond=(s != l)) for j in range(2)]

        @pl.when(s == l)
        def _():
            for rows, value in sums:
                OUT[k, x, rows] = value
            far.start()

        @pl.when(s != l)
        def _():
            for rows, value in sums:
                FS[rows] = value
            for desc in near:
                desc.start()
        rs[l, name, 4] = idx

    def rs4(l, name):
        got = rs[l, name, 4]
        ref = OUTd.at[k] if name == "d" else GRAD[name][4].at[k]
        fin = rc(ref, ref, SIB, cond=(s == l))

        @pl.when(s == l)
        def _():
            if name == "d":
                @pl.when(z != x)
                def _():
                    got.wait_recv()
            else:
                wait_bytes(GRAD[name][4].at[k, pl.ds(0, 3)], got)
            fin.start()
        rs[l, name, 5] = fin

    def rs5(l, name):
        @pl.when(s == l)
        def _():
            rs[l, name, 5].wait_recv()

    landed = {}

    def edge(l, a, value):
        if l not in landed:
            landed[l] = new_recv()
        goal = 2 * a + l
        ED[l, a] = value

        @pl.when(x == goal)
        def _():
            TT[l, x] = value

        for j in range(3):
            desc = rc(ED.at[l, a], TT.at[l, x], PX[j], recv=landed[l], cond=(X3[j] == goal))

            @pl.when(X3[j] == goal)
            def _(desc=desc):
                desc.start()

    swaps = {}

    def edge_swap(l):
        swaps[l] = rc(TT.at[l, pl.ds(2 * (1 - k), 2)], EO.at[k], SIB, cond=(s == l))

        @pl.when(s == l)
        def _():
            wait_bytes(TT.at[l, pl.ds(0, 3)], landed[l])
            swaps[l].start()
            EO[k] = TT[l, pl.ds(2 * k, 2)]

    def edge_done(l):
        @pl.when(s == l)
        def _():
            swaps[l].wait_recv()

    e0 = lengths[k, 0, 0]
    e1 = e0 + lengths[k, 0, 1]
    def doc(i):
        return jnp.where(i >= e0, 1, 0) + jnp.where(i >= e1, 1, 0)

    def keys(a):
        return TH * (a + 1)

    def allowed(a):
        qi = lax.broadcasted_iota(jnp.int32, (TH, keys(a)), 0) + TH * a
        ki = lax.broadcasted_iota(jnp.int32, (TH, keys(a)), 1)
        return (doc(qi) == doc(ki)) & (ki <= qi)

    def head(value, hh):
        lane = lax.broadcasted_iota(jnp.int32, value.shape, 1)
        return jnp.where((lane < 64) if hh == 0 else (lane >= 64), value, jnp.zeros_like(value))

    def make_angles():
        row = lax.broadcasted_iota(jnp.int32, (T, T), 0)
        ki = lax.broadcasted_iota(jnp.int32, (T, T), 1)
        lane = lax.broadcasted_iota(jnp.int32, (T, 128), 1)
        start = jnp.where(row >= e1, e1, jnp.where(row >= e0, e0, 0))
        pick = jnp.where(ki == row - start, 1.0, 0.0).astype(BF)
        cos = dot(pick, angles[:, 0:128]) + dot(pick, angles[:, 128:256])
        sin = dot(pick, angles[:, 256:384]) + dot(pick, angles[:, 384:512])
        first = (lane < 32) | ((lane >= 64) & (lane < 96))
        CS[0] = cos
        CS[1] = jnp.where(first, -sin, 0.0)
        CS[2] = jnp.where(first, 0.0, sin)

    def turn(v, sign, a):
        r = rows_of(a)
        tiles = []
        for t in range(2):
            u = v[:, 128 * t : 128 * (t + 1)]
            rot = pltpu.roll(u, 96, 1) * CS[1, r] + pltpu.roll(u, 32, 1) * CS[2, r]
            tiles.append(u * CS[0, r] + rot if sign > 0 else u * CS[0, r] - rot)
        return jnp.concatenate(tiles, axis=1)

    def gain(l, i):
        tiles = []
        for t in range(8):
            a = Gn[t // 2, 2 * (t % 2), l].astype(F32) + Gn[t // 2, 2 * (t % 2) + 1, l].astype(F32)
            tiles.append(a[i : i + 1])
        return jnp.concatenate(tiles, axis=1)

    def norm_rows(ref, out, g, a):
        for b in range(2):
            r = pl.ds(TH * a + 64 * b, 64)
            v = ref[r, :].astype(F32)
            inv = lax.rsqrt(jnp.mean(v * v, axis=-1, keepdims=True) + EPS)
            out[r, :] = (v * inv * g).astype(BF)

    def wq(l):
        return Wq[l].reshape(D, 768)

    def project(l, XR, a):
        r = rows_of(a)
        norm_rows(XR, N1.at[l], gain(l, 0), a)
        n = N1[l, r]
        w = wq(l)
        QKV[l, 0, r] = turn(dot(n, w[:, 0:256]), 1, a).astype(BF)
        QKV[l, 1, r] = turn(dot(n, w[:, 256:512]), 1, a).astype(BF)
        v = dot(n, w[:, 512:768])
        if l == 1:
            v = 0.5 * v + 0.5 * QKV[0, 2, r].astype(F32)
        QKV[l, 2, r] = v.astype(BF)

    def attend(l, a):
        ok = allowed(a)
        r, nk = rows_of(a), keys(a)
        for t in range(2):
            cols = pl.ds(128 * t, 128)
            qt, kt, vt = QKV[l, 0, r, cols], QKV[l, 1, 0:nk, cols], QKV[l, 2, 0:nk, cols]
            acc = jnp.zeros((TH, 128), F32)
            for hh in range(2):
                sc = jnp.where(ok, dot_nt(head(qt, hh), kt) * 0.125, -1e30)
                ex = jnp.exp(sc - jnp.max(sc, axis=-1, keepdims=True))
                pr = (ex / jnp.sum(ex, axis=-1, keepdims=True)).astype(BF)
                PR[l, 2 * t + hh, r, 0:nk] = pr
                acc = acc + dot(pr, head(vt, hh))
            O[l, x, r, cols] = acc.astype(BF)
        return Share(O.at[l, x, r], O.at[l, pl.ds(0, 3), r])

    def feed(l, XR, got, i, a):
        r = rows_of(a)
        got.c()
        o = jnp.concatenate([O[l, b, r] for b in range(4)], axis=1)
        H[l, r] = XR[r, :].astype(F32) + dot(o, Wo[l].reshape(D, D))
        norm_rows(H.at[l], N2.at[l], gain(l, 1), a)
        if a == 0:
            ag_done(l, "gu")
        n = N2[l, r]
        GU[l, 0, r] = dot(n, Wgu[l, :, :, :, 0:FP].reshape(D, FP))
        GU[l, 1, r] = dot(n, Wgu[l, :, :, :, FP : 2 * FP].reshape(D, FP))
        for b in range(2):
            q = pl.ds(TH * a + 64 * b, 64)
            ga, up = GU[l, 0, q, :], GU[l, 1, q, :]
            M[l, q, :] = (ga * jax.nn.sigmoid(ga) * up).astype(BF)
        if a == 0:
            ag_done(l, "d")
        return Meet(i, a, dot(M[l, r], Wd[l]).astype(BF))

    def gain_grad(i, row, ref):
        total = jnp.zeros((1, D), F32)
        for a in range(2):
            for j in range(4):
                v = ref[pl.ds(TH * a + BH * j, BH), :].astype(F32)
                inv = lax.rsqrt(jnp.mean(v * v, axis=-1, keepdims=True) + EPS)
                total = total + jnp.sum(PS[i, a, j].astype(F32) * (v * inv), axis=0, keepdims=True)
        GS[0, row : row + 1] = total

    def back_ff(l, DY, i, a):
        r = rows_of(a)
        dm = dot_nt(DY[r, :], Wd[l])
        ga, up = GU[l, 0, r], GU[l, 1, r]
        sg = jax.nn.sigmoid(ga)
        DGU[l, 0, r] = (dm * up * sg * (1.0 + ga * (1.0 - sg))).astype(BF)
        DGU[l, 1, r] = (dm * ga * sg).astype(BF)
        part = (dot_nt(DGU[l, 0, r], Wgu[l, :, :, :, 0:FP].reshape(D, FP))
                + dot_nt(DGU[l, 1, r], Wgu[l, :, :, :, FP : 2 * FP].reshape(D, FP))).astype(BF)
        return Meet(i, a, part)

    def grads_d(l, DY, msib, dysib):
        wait_recv([msib, dysib])
        Gd[l] = (dot_tn(M[l], DY[:, half(D)]) + dot_tn(Ms[l], DYs[l])).astype(BF)
        r1a(l, "d")

    def grads_gu(l, nsib, gsib):
        wait_recv([nsib, gsib])
        grad_ref("gu", l)[...] = (dot_tn(N2[l], DGU[l, k]) + dot_tn(N2s[l], DGUs[l])).astype(BF).reshape(4, 4, SH, FP)
        r1a(l, "gu")

    def back_hidden(l, DY, got, a):
        dn = got.c()
        hf = H[l, own(a), :]
        inv = lax.rsqrt(jnp.mean(hf * hf, axis=-1, keepdims=True) + EPS)
        e = dn * gain(l, 1)
        dh = DY[own(a), :].astype(F32) + inv * e - hf * (inv * inv * inv) * jnp.mean(e * hf, axis=-1, keepdims=True)
        DH[l, a] = dh
        DHB[l, own(a), :] = dh.astype(BF)
        return share_rows(DHB.at[l], a)

    def back_attend(l, got, i, a):
        r, nk = rows_of(a), keys(a)
        got.c()
        do = dot_nt(DHB[l, r], Wo[l, x].reshape(HX, D)).astype(BF)
        dqs, dks, dvs = [], [], []
        for t in range(2):
            cols = pl.ds(128 * t, 128)
            qt, kt, vt = QKV[l, 0, r, cols], QKV[l, 1, 0:nk, cols], QKV[l, 2, 0:nk, cols]
            dot_ = do[:, 128 * t : 128 * (t + 1)]
            dq = jnp.zeros((TH, 128), F32)
            dk = dv = jnp.zeros((nk, 128), F32)
            for hh in range(2):
                pr = PR[l, 2 * t + hh, r, 0:nk]
                pf = pr.astype(F32)
                dom = head(dot_, hh)
                dpp = dot_nt(dom, vt)
                ds = (pf * (dpp - jnp.sum(pf * dpp, axis=-1, keepdims=True))).astype(BF)
                dq = dq + dot(ds, head(kt, hh))
                dk = dk + dot_tn(ds, head(qt, hh))
                dv = dv + dot_tn(pr, dom)
            dqs.append(dq)
            dks.append(dk)
            dvs.append(dv)
        dq, dk, dv = (jnp.concatenate(v, axis=1) for v in (dqs, dks, dvs))
        if a == 1:
            KV0[0] = dk[0:TH]
            KV0[1] = dv[0:TH]
            dk, dv = dk[TH:], dv[TH:]
        else:
            dk, dv = dk + KV0[0], dv + KV0[1]
        DP[l, r, 0:256] = turn((dq * 0.125).astype(BF).astype(F32), -1, a).astype(BF)
        DP[l, r, 256:512] = turn((dk * 0.125).astype(BF).astype(F32), -1, a).astype(BF)
        if l == 1:
            DP[l, r, 512:768] = (0.5 * dv.astype(BF).astype(F32)).astype(BF)
        else:
            DP[l, r, 512:768] = (dv + DP[1, r, 512:768].astype(F32)).astype(BF)
        return Meet(i, a, dot_nt(DP[l, r], wq(l)).astype(BF))

    def grads_q(l, n1sib, psib):
        wait_recv([n1sib, psib])
        Gq[l] = (dot_tn(N1[l], DP[l, :, half(768)]) + dot_tn(N1s[l], DPs[l])).astype(BF).reshape(4, 4, SH, 384)
        r1a(l, "q")

    def push_heads(l):
        hs = pl.ds(pl.multiple_of(x * HX + (1 - k) * 128, 128), 128)
        return push(DHB.at[l, :, hs], DHBs.at[l], SIB)

    def grads_o(l, osib, hsib):
        wait_recv([osib, hsib])
        hs = pl.ds(pl.multiple_of(x * HX + k * 128, 128), 128)
        for b in range(4):
            Go[l, b] = (dot_tn(O[l, b], DHB[l, :, hs]) + dot_tn(Os[l, b], DHBs[l])).astype(BF).reshape(4, SH, 128)
        r1a(l, "o")

    def back_input(l, XR, got, a):
        dn = got.c()
        xf = XR[own(a), :].astype(F32)
        inv = lax.rsqrt(jnp.mean(xf * xf, axis=-1, keepdims=True) + EPS)
        e = dn * gain(l, 0)
        dx = DH[l, a] + inv * e - xf * (inv * inv * inv) * jnp.mean(e * xf, axis=-1, keepdims=True)
        return dx.astype(BF)

    def gsum_a(i, to):
        idx = new_recv()
        for j, t in enumerate(to):
            push(GS.at[i], GR.at[i, j], t, idx)
        return i, len(to), idx

    def gsum_b(sent_to):
        i, n, idx = sent_to
        wait_bytes(GR.at[i, pl.ds(0, n)], idx)
        total = GS[i]
        for j in range(n):
            total = total + GR[i, j]
        GS[i + 1] = total

    X0 = E.at[0]
    DY1 = E.at[1]
    GS[0] = jnp.zeros((8, D), F32)
    for l in range(2):
        Wd[l, FX:FP, :] = jnp.zeros((FP - FX, D), BF)
    s1a(0, "q")
    g1()
    s1a(0, "o")
    e_loc.wait()
    e_sib.wait_recv()
    mine2 = pl.ds(pl.multiple_of(xh * 128, 128), 128)
    e_got = push3([E.at[s, mine2]] * 3, [E.at[s, mine2]] * 3, PX)
    s2a(0, "q")
    s1a(0, "gu")
    s1a(0, "d")
    g2()
    s1b(0, "o")
    make_angles()
    s1b(0, "gu")
    s3(0, "q")
    s2a(0, "o")
    s2a(0, "gu")
    s1b(0, "d")
    s1a(1, "q")
    g3()
    wait_recv(e_got)
    s1a(1, "o")
    s1a(1, "gu")
    s1a(1, "d")
    s2a(0, "d")
    ag_done(0, "q")
    n1sib, osib, nsib, msib = [None, None], [None, None], [None, None], [None, None]
    project(0, X0, 0)
    g0 = attend(0, 0)
    s2b(0, "o")
    s2b(0, "gu")
    project(0, X0, 1)
    n1sib[0] = push(N1.at[0], N1s.at[0], SIB)
    g1 = attend(0, 1)
    dysib = [None, push(DY1.at[:, other_half(D)], DYs.at[1], SIB)]
    s3(0, "o")
    s2b(0, "d")
    for name in ("q", "o", "gu"):
        s1b(1, name)
    s3(0, "gu")
    s2a(1, "q")
    s1b(1, "d")
    s3(0, "d")
    s2a(1, "o")
    s2a(1, "gu")
    ag_done(0, "o")
    m0 = feed(0, X0, g0, 0, 0)
    s2b(1, "q")
    m1 = feed(0, X0, g1, 0, 1)
    osib[0] = push(O.at[0], Os.at[0], SIB)
    nsib[0] = push(N2.at[0], N2s.at[0], SIB)
    msib[0] = push(M.at[0], Ms.at[0], SIB)
    s2a(1, "d")
    s2b(1, "o")
    X1[own(0), :] = (m0.c() + H[0, own(0), :]).astype(BF)
    g0 = share_rows(X1, 0)
    s2b(1, "gu")
    X1[own(1), :] = (m1.c() + H[0, own(1), :]).astype(BF)
    g1 = share_rows(X1, 1)
    s3(1, "q")
    s2b(1, "d")
    s3(1, "o")
    g0.c()
    ag_done(1, "q")
    project(1, X1, 0)
    g0 = attend(1, 0)
    s3(1, "gu")
    s3(1, "d")
    early = close()
    g1.c()
    project(1, X1, 1)
    n1sib[1] = push(N1.at[1], N1s.at[1], SIB)
    g1 = attend(1, 1)
    ag_done(1, "o")
    y0 = feed(1, X1, g0, 1, 0)
    y1 = feed(1, X1, g1, 1, 1)
    osib[1] = push(O.at[1], Os.at[1], SIB)
    nsib[1] = push(N2.at[1], N2s.at[1], SIB)
    msib[1] = push(M.at[1], Ms.at[1], SIB)

    m1 = back_ff(1, DY1, 2, 1)
    m0 = back_ff(1, DY1, 2, 0)
    gsib = push(DGU.at[1, 1 - k], DGUs.at[1], SIB)
    grads_d(1, DY1, msib[1], dysib[1])
    g1 = back_hidden(1, DY1, m1, 1)
    g0 = back_hidden(1, DY1, m0, 0)
    grads_gu(1, nsib[1], gsib)
    r1b(1, "d")
    m1 = back_attend(1, g1, 3, 1)
    m0 = back_attend(1, g0, 3, 0)
    hsib = push_heads(1)
    psib = push(DP.at[1, :, other_half(768)], DPs.at[1], SIB)
    r1b(1, "gu")
    edge(1, 0, (y0.c() + H[1, own(0), :]).astype(BF))
    edge(1, 1, (y1.c() + H[1, own(1), :]).astype(BF))
    grads_q(1, n1sib[1], psib)
    DY0[own(1), :] = back_input(1, X1, m1, 1)
    g1 = share_rows(DY0, 1)
    DY0[own(0), :] = back_input(1, X1, m0, 0)
    g0 = share_rows(DY0, 0)
    r2a(1, "d")
    grads_o(1, osib[1], hsib)
    r2a(1, "gu")

    g1.c()
    m1 = back_ff(0, DY0, 4, 1)
    g0.c()
    m0 = back_ff(0, DY0, 4, 0)
    gsib = push(DGU.at[0, 1 - k], DGUs.at[0], SIB)
    dysib[0] = push(DY0.at[:, other_half(D)], DYs.at[0], SIB)
    r2b(1, "d")
    r1b(1, "q")
    flush(0, early)
    grads_d(0, DY0, msib[0], dysib[0])
    g1 = back_hidden(0, DY0, m1, 1)
    grads_gu(0, nsib[0], gsib)
    g0 = back_hidden(0, DY0, m0, 0)
    r1b(1, "o")
    r2b(1, "gu")
    m1 = back_attend(0, g1, 5, 1)
    m0 = back_attend(0, g0, 5, 0)
    hsib = push_heads(0)
    psib = push(DP.at[0, :, other_half(768)], DPs.at[0], SIB)
    r1b(0, "d")
    gain_grad(5, 0, X0)
    gain_grad(4, 1, H.at[0])
    gain_grad(3, 2, X1)
    gain_grad(2, 3, H.at[1])
    g = gsum_a(0, PX)
    r1b(0, "gu")
    grads_q(0, n1sib[0], psib)
    grads_o(0, osib[0], hsib)
    r2a(1, "q")
    r2a(1, "o")
    edge(0, 1, back_input(0, X0, m1, 1))
    edge(0, 0, back_input(0, X0, m0, 0))
    rs3(1, "d")
    r2a(0, "d")
    gsum_b(g)
    g = gsum_a(1, PY)
    r2a(0, "gu")
    r2a(0, "q")
    r2a(0, "o")
    edge_swap(0)
    r2b(0, "d")
    rs3(1, "gu")
    gsum_b(g)
    g = gsum_a(2, PZ)
    r2b(1, "q")
    r2b(1, "o")
    r2b(0, "gu")
    edge_swap(1)
    rs4(1, "d")
    rs3(0, "q")
    rs3(0, "o")
    rs3(0, "d")
    gsum_b(g)
    g = gsum_a(3, [SIB])
    rs3(1, "q")
    rs3(1, "o")
    rs3(0, "gu")
    rs4(1, "gu")
    rs4(0, "q")
    rs4(0, "o")
    rs4(0, "d")
    rs4(1, "q")
    rs4(1, "o")
    gsum_b(g)
    edge_done(0)
    edge_done(1)
    rs4(0, "gu")
    outs = []

    def put(a, b):
        outs.append(local(a, b))
        outs[-1].start()
    put(EO, edge_hbm)
    put(GS.at[4], gsum_hbm)
    for name, a, b in (("d", OUTd, od_hbm), ("q", OUTq, oq_hbm), ("o", OUTo, oo_hbm), ("gu", OUTgu, ogu_hbm)):
        rs5(1, name)
        rs5(0, name)
        put(a, b)
    flush(early, len(groups))
    flush_conditional()
    for o in outs:
        o.wait()
    assert counter[0] <= N_RECV and counter[1] <= N_LOC and counter[2] <= N_SEND, counter


def epilogue(*refs):
    given, (edges, qkv, out, gate, up, down, gg), held, sem = refs[:6], refs[6:13], refs[13:19], refs[19]
    copies = [pltpu.make_async_copy(a, b, sem.at[i]) for i, (a, b) in enumerate(zip(given, held))]
    for cp in copies:
        cp.start()
    for cp in copies:
        cp.wait()
    oq, oo, ogu, od, edge, gsum = held
    s = lax.axis_index("section")
    dp = lax.axis_index("dp")
    edges[0, :, 0] = edge[...].reshape(2, BT, D)
    for x in range(4):
        a, b = oq[0, x].astype(F32), oq[1, x].astype(F32)
        qkv[0, :, HX * x : HX * (x + 1)] = a[:, 0:256]
        qkv[0, :, D + HX * x : D + HX * x + 128] = a[:, 256:384]
        qkv[0, :, D + HX * x + 128 : D + HX * (x + 1)] = b[:, 0:128]
        qkv[0, :, 2 * D + HX * x : 2 * D + HX * (x + 1)] = b[:, 128:384]
        for h in range(2):
            out[0, :, HX * x + 128 * h : HX * x + 128 * (h + 1)] = oo[h, x].astype(F32)
    for h, ref in ((0, gate), (1, up)):
        for p in range(2):
            a = ogu[h, 2 * p].astype(F32)
            b = pltpu.roll(ogu[h, 2 * p + 1].astype(F32), 64, 1)
            c = 2 * FX * p
            ref[0, :, c : c + 640] = a[:, 0:640]
            ref[0, :, c + 640 : c + 768] = a[:, 640:768] + b[:, 0:128]
            ref[0, :, c + 768 : c + 2 * FX] = b[:, 128:768]
    for h in range(2):
        down[0, :, 512 * h : 512 * (h + 1)] = od[h].astype(F32)
    tile = gsum[:, pl.ds(pl.multiple_of(128 * lax.div(dp, 2), 128), 128)]
    tile = jnp.where(lax.rem(dp, 2) == 1, pltpu.roll(tile, 64, 1), tile)
    rows = jnp.where(s == 1, tile[2:4], tile[0:2])
    gg[0] = rows[:, 0:SH]


def run_kernel(lengths, ends, qkv_w, out_w, gate_w, up_w, down_w, gains, angles):
    V = pltpu.VMEM
    sh = jax.ShapeDtypeStruct
    any_ = pl.BlockSpec(memory_space=pl.ANY)
    vm = pl.BlockSpec(memory_space=pltpu.VMEM)
    out_shape = [
        sh((2, 4, SH, 384), BF), sh((2, 4, SH, 128), BF), sh((2, 4, SH, FP), BF), sh((2, DR, 512), BF),
        sh((2, 2, BH, D), BF), sh((8, D), F32), sh((GROUP_BYTES // 4096, 16, 128), BF),
    ]
    scratch = [
        V((2, 4, 4, SH, 768), BF), V((2, 4, 4, SH, D), BF), V((2, 4, 4, SH, 2 * FP), BF), V((2, FP, D), BF),
        V((4, 4, 2, 16, 128), BF),
        V((2, T, D), BF), V((T, D), BF), V((T, D), BF),
        V((2, T, D), BF), V((2, T, D), BF), V((2, T, D), BF), V((2, T, D), BF),
        V((2, T, D), F32), V((2, 3, T, HX), BF), V((2, 4, T, T), BF),
        V((2, 4, T, HX), BF), V((2, 4, T, HX), BF),
        V((2, 2, T, FP), F32), V((2, T, FP), BF), V((2, T, FP), BF),
        V((2, 2, T, FP), BF), V((2, T, FP), BF),
        V((2, T, 768), BF), V((2, T, 384), BF),
        V((2, T, D), BF), V((2, T, 128), BF), V((2, T, 512), BF), V((2, 2, BH, D), F32),
        V((2, TH, HX), F32), V((2, 2, BH, D), BF),
        V((6, 2, 4, BH, D), BF), V((6, 2, 3, BH, D), BF),
        V((2, 4, 4, SH, 384), BF), V((2, 4, 4, SH, 128), BF), V((1, 4, 4, SH, FP), BF), V((2, FP, 512), BF),
        V((2, 3, 4, SH, 384), BF), V((2, 3, 4, SH, 128), BF), V((2, 3, 4, SH, FP), BF), V((2, 3, DR, 512), BF),
        V((2, 3, SH, 384), BF), V((2, 3, SH, 128), BF), V((2, 3, SH, FP), BF), V((2, 3, DR, 512), BF),
        V((2, 4, SH, 384), BF), V((2, 4, SH, 128), BF), V((2, 4, SH, FP), BF), V((2, DR, 512), BF),
        V((2, 4, SH, 384), BF), V((2, 4, SH, 128), BF), V((2, 4, SH, FP), BF), V((2, DR, 512), BF),
        V((SH, 384), BF), V((SH, 128), BF), V((SH, FP), BF), V((DR, 512), BF),
        V((5, 8, D), F32), V((4, 3, 8, D), F32), V((2, 4, BH, D), BF), V((2, 2, BH, D), BF),
        V((3, T, 128), F32), V((SH, 384), BF), V((SH, FP), BF), V((SH, 512), BF), V((DR, 512), BF),
        V((16, 128), BF), V((16, 128), F32),
        pltpu.SemaphoreType.DMA((N_SEND,)), pltpu.SemaphoreType.DMA((N_RECV,)), pltpu.SemaphoreType.DMA((N_LOC,)),
    ]
    return pl.pallas_call(
        kernel,
        out_shape=out_shape,
        in_specs=[pl.BlockSpec(memory_space=pltpu.SMEM)] + [any_] * 6 + [vm] * 2,
        out_specs=[any_] * 7,
        scratch_shapes=scratch,
        name="two_layers",
        compiler_params=pltpu.CompilerParams(
            collective_id=0, has_side_effects=True, vmem_limit_bytes=64 * 1024 * 1024 - 65536
        ),
    )(lengths, ends, qkv_w, out_w, gate_w, up_w, down_w, gains, angles)


def angle_table():
    pos = np.arange(T, dtype=np.float64)[:, None]
    freq = 10000.0 ** (-(np.arange(128) % 32) / 32.0)
    parts = []
    for v in (np.cos(pos * freq), np.sin(pos * freq)):
        high = v.astype(jnp.bfloat16)
        parts += [high, (v - high.astype(np.float64)).astype(jnp.bfloat16)]
    return np.concatenate(parts, axis=1)


def per_device(ends_in, lengths, qkv_w, out_w, gate_w, up_w, down_w, gains):
    oq, oo, ogu, od, edge, gsum, _ = run_kernel(
        lengths, ends_in, qkv_w, out_w, gate_w, up_w, down_w, gains, jnp.asarray(angle_table()))
    sh = jax.ShapeDtypeStruct
    return pl.pallas_call(
        epilogue,
        out_shape=[
            sh((1, 2, 1, BT, D), BF), sh((1, SH, 3 * D), F32), sh((1, SH, D), F32), sh((1, SH, FF), F32),
            sh((1, SH, FF), F32), sh((1, DR, D), F32), sh((1, 2, SH), F32),
        ],
        in_specs=[pl.BlockSpec(memory_space=pl.ANY)] * 6,
        out_specs=[pl.BlockSpec(memory_space=pltpu.VMEM)] * 7,
        scratch_shapes=[pltpu.VMEM(v.shape, v.dtype) for v in (oq, oo, ogu, od, edge, gsum)]
        + [pltpu.SemaphoreType.DMA((6,))],
        name="place_outputs",
        compiler_params=pltpu.CompilerParams(vmem_limit_bytes=63 * 1024 * 1024),
    )(oq, oo, ogu, od, edge, gsum)


def solution(mesh):
    in_specs = (
        P("section", None, "dp", "ctx", None),
        P(None, "dp", None),
        P("section", "dp", None),
        P("section", "dp", None),
        P("section", "dp", None),
        P("section", "dp", None),
        P("section", "dp", None),
        P("section", None, "dp"),
    )
    out_specs = (
        P("section", None, "dp", "ctx", None),
        P("section", "dp", None),
        P("section", "dp", None),
        P("section", "dp", None),
        P("section", "dp", None),
        P("section", "dp", None),
        P("section", None, "dp"),
    )
    return jax.shard_map(per_device, mesh=mesh, in_specs=in_specs, out_specs=out_specs, check_vma=False)
```

```python
import jax
import jax.numpy as jnp
import numpy as np
from jax import lax
from jax.experimental import pallas as pl
from jax.experimental.pallas import tpu as pltpu
from jax.sharding import PartitionSpec as P

T = 256
D = 1024
FF = 2816
FX = FF // 4
FP = 768
HX = 256
SH = 64
DR = 176
BT = 64
TH = 128
BH = 32
EPS = 1e-5
MESH = pl.DeviceIdType.MESH
BF = jnp.bfloat16
F32 = jnp.float32


def dot(a, b):
    return jnp.dot(a, b, preferred_element_type=F32)


def dot_nt(a, b):
    return lax.dot_general(a, b, (((1,), (1,)), ((), ())), preferred_element_type=F32)


def dot_tn(a, b):
    return lax.dot_general(a, b, (((0,), (0,)), ((), ())), preferred_element_type=F32)


N_SEND = 73
N_RECV = 207
N_LOC = 17
GROUP_BYTES = 4 * 1024 * 1024


def kernel(
    lengths, ends, q_w, o_w, gate_w, up_w, d_w, gains, angles,
    oq_hbm, oo_hbm, ogu_hbm, od_hbm, edge_hbm, gsum_hbm, dummy,
    Wq, Wo, Wgu, Wd, Gn,
    E, X1, DY0, N1, N1s, N2, N2s, H, QKV, PR, O, Os, GU, M, Ms, DGU, DGUs, DP, DPs, DHB, DHBs, DYs, DH, KV0, ED,
    PS, PRV,
    Gq, Go, Ggu, Gd, R1q, R1o, R1gu, R1d, R2q, R2o, R2gu, R2d, Sq, So, Sgu, Sd, OUTq, OUTo, OUTgu, OUTd,
    FSq, FSo, FSgu, FSd, GS, GR, TT, EO,
    CS, QT, GT, OT, DT, NT, gain_in,
    ssem, rsem, lsem,
):
    s = lax.axis_index("section")
    dp = lax.axis_index("dp")
    c = lax.axis_index("ctx")
    xh = lax.div(c, 2)
    k = lax.rem(c, 2)
    x = xh * 2 + s
    z = lax.div(dp, 4)
    y = lax.rem(dp, 4)

    def dev(x_, y_, z_, k_):
        return (lax.rem(x_, 2), z_ * 4 + y_, lax.div(x_, 2) * 2 + k_)

    def ring(v):
        return [lax.rem(v + 1, 4), lax.rem(v + 3, 4), lax.rem(v + 2, 4)]

    X3, Y3, Z3 = ring(x), ring(y), ring(z)
    PX = [dev(v, y, z, k) for v in X3]
    PY = [dev(x, v, z, k) for v in Y3]
    PZ = [dev(x, y, v, k) for v in Z3]
    SIB = dev(x, y, z, 1 - k)

    bar = pltpu.get_barrier_semaphore()
    partners = PX + PY + PZ + [SIB]
    for p in partners:
        pl.semaphore_signal(bar, inc=1, device_id=p, device_id_type=MESH)

    counter = [0, 0, 0]
    sent = []
    groups = []

    def size(ref):
        n = 2 if ref.dtype == BF else 4
        for v in ref.shape:
            n *= v
        return n

    def new_recv():
        counter[0] += 1
        return counter[0] - 1

    def rc(src, dst, to, recv=None, cond=None):
        recv = new_recv() if recv is None else recv
        if cond is None:
            if not groups or groups[-1][2] or groups[-1][1] + size(src) > GROUP_BYTES:
                groups.append([counter[2], 0, False])
                counter[2] += 1
            groups[-1][1] += size(src)
            i = groups[-1][0]
        else:
            i = counter[2]
            counter[2] += 1
        desc = pltpu.make_async_remote_copy(
            src_ref=src, dst_ref=dst, send_sem=ssem.at[i], recv_sem=rsem.at[recv],
            device_id=to, device_id_type=MESH,
        )
        if cond is not None:
            sent.append((cond, desc))
        return desc

    def push(src, dst, to, recv=None):
        desc = rc(src, dst, to, recv)
        desc.start()
        return desc

    def push3(srcs, dsts, to):
        return [push(a, b, t) for a, b, t in zip(srcs, dsts, to)]

    def wait_recv(descs):
        for desc in descs:
            desc.wait_recv()

    def wait_bytes(ref, recv):
        pltpu.make_async_remote_copy(
            src_ref=ref, dst_ref=ref, send_sem=ssem.at[0], recv_sem=rsem.at[recv], device_id=SIB, device_id_type=MESH,
        ).wait_recv()

    def close():
        if groups:
            groups[-1][2] = True
        return len(groups)

    def flush(first, last):
        for i, total, _ in groups[first:last]:
            ref = dummy.at[pl.ds(0, total // 4096)]
            pltpu.make_async_copy(ref, ref, ssem.at[i]).wait()

    def flush_conditional():
        for cond, desc in sent:
            @pl.when(cond)
            def _(desc=desc):
                desc.wait_send()

    class Gather:
        def __init__(self, ring, blk, some, direct=False):
            (self.p, self.m, self.o), self.me, self.to = ring
            self.blk, self.some, self.direct = blk, some, direct

        def a(self):
            self.r = [new_recv() for _ in range(1 if self.direct else 3)]
            if self.direct:
                for to in self.to:
                    push(self.blk(self.me, None), self.blk(self.me, None), to, self.r[0])
                return self
            h0, h1 = self.blk(self.me, 0), self.blk(self.me, 1)
            push(h0, h0, self.to[0], self.r[0])
            push(h1, h1, self.to[1], self.r[1])
            push(h1, h1, self.to[0], self.r[2])
            push(h0, h0, self.to[1], self.r[2])
            return self

        def b(self):
            if not self.direct:
                left, right = self.blk(self.m, 0), self.blk(self.p, 1)
                wait_bytes(left, self.r[0])
                push(left, left, self.to[0], self.r[2])
                wait_bytes(right, self.r[1])
                push(right, right, self.to[1], self.r[2])
            return self

        def c(self):
            if self.direct:
                wait_bytes(self.some(3), self.r[0])
            else:
                wait_bytes(self.some(2), self.r[2])

    class Reduce:
        def __init__(self, ring, part, buf, some, direct=False):
            (self.p, self.m, self.o), self.me, self.to = ring
            self.part, self.buf, self.some, self.direct = part, buf, some, direct
            self.terms = (0, 1, 2) if direct else (1, 2)

        def a(self):
            self.r = [new_recv() for _ in range(1 if self.direct else 3)]
            part, buf = self.part, self.buf
            if self.direct:
                for i, (j, to) in enumerate(zip((self.p, self.m, self.o), self.to)):
                    push(part(j, None), buf(i, None), to, self.r[0])
                return self
            push(part(self.o, 0), buf(0, 0), self.to[0], self.r[0])
            push(part(self.o, 1), buf(0, 1), self.to[1], self.r[1])
            push(part(self.p, 1), buf(1, 1), self.to[0], self.r[2])
            push(part(self.m, 0), buf(2, 0), self.to[1], self.r[2])
            return self

        def b(self):
            if self.direct:
                return self
            part, buf = self.part, self.buf
            for h, j, to in ((0, self.p, self.to[0]), (1, self.m, self.to[1])):
                ref, got = part(j, h), buf(0, h)
                wait_bytes(got, self.r[h])
                ref[...] = (ref[...].astype(F32) + got[...].astype(F32)).astype(BF)
                push(ref, buf(1 + h, h), to, self.r[2])
            return self

        def c(self):
            if self.direct:
                wait_bytes(self.some(0, 3), self.r[0])
            else:
                wait_bytes(self.some(1, 2), self.r[2])

        def total(self):
            value = self.part(self.me, None)[...].astype(F32)
            for i in self.terms:
                value = value + self.buf(i, None)[...].astype(F32)
            return value

    RX, RY, RZ = (X3, x, PX), (Y3, y, PY), (Z3, z, PZ)

    def path_rows(path, paths, h):
        n = 64 // len(paths)
        base = n * paths.index(path)
        return pl.ds(base, n) if h is None else pl.ds(base + h * (n // 2), n // 2)

    def sub(base, width, h):
        return pl.ds(base, width) if h is None else pl.ds(base + h * (width // 2), width // 2)

    def local(src, dst):
        i = counter[1]
        counter[1] += 1
        return pltpu.make_async_copy(src, dst, lsem.at[i])

    def half(width):
        return pl.ds(pl.multiple_of(k * (width // 2), 128), width // 2)

    def other_half(width):
        return pl.ds(pl.multiple_of((1 - k) * (width // 2), 128), width // 2)

    tx = lax.rem(x + 3 - 2 * k, 4)
    TO = dev(tx, y, z, k)
    REG = {"q": (Wq, 768), "o": (Wo, 1024), "gu": (Wgu, 2 * FP)}
    pre = {}
    down_rows = pl.ds(pl.multiple_of(y * DR, 16), DR)
    slices = (x, tx)
    q_in = GU.at[1, 0, pl.ds(128, 128), pl.ds(0, 384)]
    gu_in = GU.at[1, 0, pl.ds(0, 128), :]
    d_in = GU.at[1, 1, pl.ds(0, DR), pl.ds(0, 512)]
    o_in = GU.at[1, 1, pl.ds(192, SH), pl.ds(0, 512)]
    q_cp = []
    for j in range(2):
        for i in range(3):
            piece = 3 * k + i
            col = D * lax.div(piece, 2) + HX * slices[j] + 128 * lax.rem(piece, 2)
            q_cp.append(local(q_w.at[0, :, pl.ds(pl.multiple_of(col, 128), 128)],
                              GU.at[1, 0, pl.ds(128 + SH * j, SH), pl.ds(128 * i, 128)]))
    o_cp = local(o_w.at[0, :, half(D)], o_in)
    d_cp = local(d_w.at[0, :, half(D)], d_in)
    gu_cp = []
    for w in (gate_w, up_w):
        pair = []
        for j in range(2):
            col = 2 * FX * lax.div(slices[j], 2) + (FX - 64) * lax.rem(slices[j], 2)
            pair.append((w.at[0, :, pl.ds(pl.multiple_of(col, 128), FP)], GU.at[1, 0, pl.ds(SH * j, SH), :]))
        gu_cp.append(pair)
    gu_cp = [[local(*c) for c in gu_cp[0]], None, gu_cp[1]]
    gu_cp[1] = [pltpu.make_async_copy(*c, lsem.at[counter[1] - 2 + j]) for j, c in enumerate(gu_cp.pop())]
    for cp in q_cp:
        cp.start()
    for kk in range(2):
        @pl.when(k == kk)
        def _(kk=kk):
            for cp in gu_cp[kk]:
                cp.start()
    o_cp.start()
    d_cp.start()

    odd = lax.rem(dp, 2) == 1
    gz = jnp.zeros((2, SH), F32)
    gv = gains[0].astype(F32)
    NT[...] = jnp.zeros((16, 128), BF)
    gain_in[...] = jnp.zeros((16, 128), F32)
    gain_in[0:2, :] = jnp.where(odd, jnp.concatenate([gz, gv], axis=1), jnp.concatenate([gv, gz], axis=1))
    NT[...] = gain_in[...].astype(BF)
    Gn[z, y, s] = NT[...]
    pl.semaphore_wait(bar, len(partners))
    pre["g"] = rc(NT, Gn.at[z, y, s], TO)
    pre["g"].start()

    for cp in q_cp:
        cp.wait()
    QT[...] = q_in[SH : 2 * SH, :].astype(BF)
    pre["q"] = rc(QT, Wq.at[s, z, y, :, half(768)], TO)
    pre["q"].start()
    Wq[s, z, y, :, half(768)] = q_in[0:SH, :].astype(BF)

    o_cp.wait()
    OT[...] = o_in[...].astype(BF)
    pre["o"] = rc(OT, Wo.at[s, z, y, :, half(D)], TO)
    pre["o"].start()
    Wo[s, z, y, :, half(D)] = OT[...]

    wide = lax.broadcasted_iota(jnp.int32, (SH, FP), 1)

    def hidden_slice(j):
        v = gu_in[SH * j : SH * (j + 1), :]
        v = jnp.where(lax.rem(slices[j], 2) == 1, pltpu.roll(v, FP - 64, 1), v)
        return jnp.where(wide < FX, v, 0.0).astype(BF)

    for cp in gu_cp[0]:
        cp.wait()
    GT[...] = hidden_slice(1)
    pre["gu"] = rc(GT, Wgu.at[s, z, y, :, half(2 * FP)], TO)
    pre["gu"].start()
    Wgu[s, z, y, :, half(2 * FP)] = hidden_slice(0)

    d_cp.wait()
    DT[...] = d_in[...].astype(BF)
    pre["d"] = rc(DT, Wd.at[s, down_rows, half(D)], TO, cond=(z == tx))

    @pl.when(z == tx)
    def _():
        pre["d"].start()

    @pl.when(z == x)
    def _():
        Wd[s, down_rows, half(D)] = DT[...]

    mine = pl.ds(pl.multiple_of(xh * 128 + k * 64, 64), 64)
    e_loc = local(ends.at[0, k, 0], E.at[s, mine])
    e_loc.start()
    e_sib = push(ends.at[0, 1 - k, 0], E.at[s, mine], SIB)

    ag = {}

    def ready(l, name):
        @pl.when(s != l)
        def _():
            pre[name].wait_recv()

    def quarter(h):
        return half(D) if h is None else pl.ds(pl.multiple_of(k * 512 + h * 256, 128), 256)

    is_src, is_p, is_m, is_f = z == x, z == X3[0], z == X3[1], z == X3[2]

    AG_PATHS = {(l, name): "AB" for l in range(2) for name in REG}
    AG_DIRECT = ((0, "q"),)

    def g1():
        for l in range(2):
            ready(l, "g")
        ref = Gn.at[z, y]
        ag["g"] = new_recv()
        for to in PY:
            push(ref, ref, to, ag["g"])

    def g2():
        wait_bytes(Gn.at[z, pl.ds(0, 3)], ag["g"])
        ref = Gn.at[z]
        ag["g"] = new_recv()
        for to in PZ:
            push(ref, ref, to, ag["g"])

    def g3():
        wait_bytes(Gn.at[pl.ds(0, 3)], ag["g"])

    def s1a(l, name):
        if name == "d":
            ref = Wd.at[l, down_rows, half(D)]
            idx = new_recv()
            up = rc(ref, ref, PZ[0], recv=idx, cond=is_src)
            dn = rc(ref, ref, PZ[1], recv=idx, cond=is_src)

            @pl.when(is_src)
            def _():
                ready(l, "d")
                up.start()
                dn.start()
            ag[l, "d", 1] = up, idx
            return
        ready(l, name)
        W, width = REG[name]
        cols = half(width)
        paths, direct = AG_PATHS[l, name], (l, name) in AG_DIRECT
        first = []
        for path in paths:
            rows = lambda h, path=path: path_rows(path, paths, h)
            if path == "A":
                g = Gather(RY, lambda j, h, rows=rows: W.at[l, z, j, rows(h), cols],
                           lambda n, rows=rows: W.at[l, z, pl.ds(0, n), rows(None), cols], direct)
            else:
                g = Gather(RZ, lambda j, h, rows=rows: W.at[l, j, y, rows(h), cols],
                           lambda n, rows=rows: W.at[l, pl.ds(0, n), y, rows(None), cols], direct)
            first.append(g.a())
        ag[l, name, 1] = first

    def s1b(l, name):
        first = ag[l, name, 1]
        if name == "d":
            got, idx = first
            h0, h1 = Wd.at[l, down_rows, quarter(0)], Wd.at[l, down_rows, quarter(1)]
            to_f = [rc(h0, h0, PZ[0], recv=idx, cond=is_p), rc(h1, h1, PZ[1], recv=idx, cond=is_m)]
            for cond, desc in zip((is_p, is_m), to_f):
                @pl.when(cond)
                def _(desc=desc):
                    got.wait_recv()
                    desc.start()
            return
        for g in first:
            g.b()

    def s2a(l, name):
        first = ag[l, name, 1]
        if name == "d":
            @pl.when(is_f)
            def _():
                first[0].wait_recv()

            def blk(j, h):
                return Wd.at[l, pl.ds(pl.multiple_of(j * DR, 16), DR), quarter(h)]
            ag[l, name, 2] = [Gather(RY, blk, lambda n: Wd.at[l, pl.ds(0, n * DR), half(D)]).a()]
            return
        W, width = REG[name]
        cols = half(width)
        paths, direct = AG_PATHS[l, name], (l, name) in AG_DIRECT
        second = []
        for path, g in zip(paths, first):
            rows = lambda h, path=path: path_rows(path, paths, h)
            g.c()
            if path == "A":
                g = Gather(RZ, lambda j, h, rows=rows: W.at[l, j, :, rows(h), cols],
                           lambda n, rows=rows: W.at[l, pl.ds(0, n), :, rows(None), cols], direct)
            else:
                g = Gather(RY, lambda j, h, rows=rows: W.at[l, :, j, rows(h), cols],
                           lambda n, rows=rows: W.at[l, :, pl.ds(0, n), rows(None), cols], direct)
            second.append(g.a())
        ag[l, name, 2] = second

    def s2b(l, name):
        for g in ag[l, name, 2]:
            g.b()

    def s3(l, name):
        for g in ag[l, name, 2]:
            g.c()
        if name == "d":
            ref = Wd.at[l, pl.ds(0, FX), half(D)]
        else:
            W, width = REG[name]
            ref = W.at[l, :, :, :, half(width)]
        ag[l, name, 3] = push(ref, ref, SIB)

    def ag_done(l, name):
        wait_recv([ag[l, name, 3]])

    class Share:
        def __init__(self, ref, three):
            self.r, self.three = new_recv(), three
            for to in PX:
                push(ref, ref, to, self.r)

        def c(self):
            wait_bytes(self.three, self.r)

    class Meet:
        def __init__(self, i, a, part):
            self.i, self.a, self.r = i, a, new_recv()
            for j in range(4):
                PS[i, a, j] = part[BH * j : BH * (j + 1)]
            for n, (j, to) in enumerate(zip(X3, PX)):
                push(PS.at[i, a, j], PRV.at[i, a, n], to, self.r)

        def c(self):
            wait_bytes(PRV.at[self.i, self.a], self.r)
            total = PS[self.i, self.a, x].astype(F32)
            for n in range(3):
                total = total + PRV[self.i, self.a, n].astype(F32)
            return total

    def rows_of(a):
        return pl.ds(TH * a, TH)

    def own(a):
        return pl.ds(pl.multiple_of(TH * a + BH * x, BH), BH)

    def share_rows(ref, a):
        return Share(ref.at[own(a)], ref.at[pl.ds(0, 3 * BH)])

    GRAD = {"q": (Gq, R1q, R2q, Sq, OUTq, FSq, 384), "o": (Go, R1o, R2o, So, OUTo, FSo, 128),
            "gu": (Ggu, R1gu, R2gu, Sgu, OUTgu, FSgu, FP)}
    rs = {}

    def grad_ref(name, l):
        if name == "gu" and l == 0:
            return Wgu.at[1, :, :, :, pl.ds(0, FP)]
        return GRAD[name][0].at[0 if name == "gu" else l]

    RS_PATHS = {(l, name): "AB" for l in range(2) for name in GRAD}
    RS_DIRECT = ((0, "q"), (0, "o"), (1, "q"), (1, "o"))

    def r1a(l, name):
        if name == "d":
            def part(j, h):
                return Gd.at[l, pl.ds(pl.multiple_of(j * DR, 16), DR), sub(0, 512, h)]
            rs[l, name, 1] = [Reduce(RY, part, lambda n, h: R1d.at[l, n, :, sub(0, 512, h)],
                                     lambda i0, n: R1d.at[l, pl.ds(i0, n)]).a()]
            return
        _, R1, R2, S, OUT, FS, width = GRAD[name]
        G = grad_ref(name, l)
        paths, direct = RS_PATHS[l, name], (l, name) in RS_DIRECT
        first = []
        for path in paths:
            rows = lambda h, path=path: path_rows(path, paths, h)
            buf = lambda n, h, rows=rows: R1.at[l, n, :, rows(h)]
            some = lambda i0, n, rows=rows: R1.at[l, pl.ds(i0, n), :, rows(None)]
            if path == "A":
                r = Reduce(RZ, lambda j, h, rows=rows: G.at[j, :, rows(h)], buf, some, direct)
            else:
                r = Reduce(RY, lambda j, h, rows=rows: G.at[:, j, rows(h)], buf, some, direct)
            first.append(r.a())
        rs[l, name, 1] = first

    def r1b(l, name):
        for r in rs[l, name, 1]:
            r.b()

    def r2a(l, name):
        first = rs[l, name, 1]
        if name == "d":
            first[0].c()
            Sd[l] = first[0].total().astype(BF)
            idx = new_recv()
            to = [rc(Sd.at[l, :, pl.ds(0, 256)], R2d.at[l, 0, :, pl.ds(0, 256)], PZ[1], recv=idx, cond=is_f),
                  rc(Sd.at[l, :, pl.ds(256, 256)], R2d.at[l, 0, :, pl.ds(256, 256)], PZ[0], recv=idx, cond=is_f)]

            @pl.when(is_f)
            def _():
                to[0].start()
                to[1].start()
            rs[l, name, 2] = to
            return
        _, R1, R2, S, OUT, FS, width = GRAD[name]
        paths, direct = RS_PATHS[l, name], (l, name) in RS_DIRECT
        second = []
        for path, r in zip(paths, first):
            rows = lambda h, path=path: path_rows(path, paths, h)
            r.c()
            S[l, :, rows(None)] = r.total().astype(BF)
            r = Reduce(RY if path == "A" else RZ, lambda j, h, rows=rows: S.at[l, j, rows(h)],
                       lambda n, h, rows=rows: R2.at[l, n, rows(h)],
                       lambda i0, n, rows=rows: R2.at[l, pl.ds(i0, n), rows(None)], direct)
            second.append(r.a())
        rs[l, name, 2] = second

    def r2b(l, name):
        second = rs[l, name, 2]
        if name == "d":
            idx = [new_recv(), new_recv()]
            fin = [rc(Sd.at[l], R2d.at[l, 1], PZ[1], recv=idx[0], cond=is_p),
                   rc(Sd.at[l], R2d.at[l, 2], PZ[0], recv=idx[1], cond=is_m)]
            for cond, got, h, desc in ((is_p, second[0], 0, fin[0]), (is_m, second[1], 1, fin[1])):
                @pl.when(cond)
                def _(got=got, h=h, desc=desc):
                    got.wait_recv()
                    cols = pl.ds(256 * h, 256)
                    Sd[l, :, cols] = (Sd[l, :, cols].astype(F32) + R2d[l, 0, :, cols].astype(F32)).astype(BF)
                    desc.start()
            rs[l, name, 3] = fin
            return
        for r in second:
            r.b()

    def rs3(l, name):
        idx = new_recv()
        if name == "d":
            fin = rs[l, name, 3]
            far = rc(OUTd.at[k], OUTd.at[k], PX[2], recv=idx, cond=is_src & (s == l))
            near = [rc(FSd, OUTd.at[k], PX[j], recv=idx, cond=is_src & (s != l)) for j in range(2)]

            @pl.when(is_src)
            def _():
                wait_recv(fin)
                total = (Sd[l].astype(F32) + R2d[l, 1].astype(F32) + R2d[l, 2].astype(F32)).astype(BF)

                @pl.when(s == l)
                def _():
                    OUTd[k] = total
                    far.start()

                @pl.when(s != l)
                def _():
                    FSd[...] = total
                    for desc in near:
                        desc.start()
            rs[l, name, 4] = far
            return
        _, R1, R2, S, OUT, FS, width = GRAD[name]
        paths = RS_PATHS[l, name]
        second = rs[l, name, 2]
        for r in second:
            r.c()
        sums = [(path_rows(path, paths, None), r.total().astype(BF)) for path, r in zip(paths, second)]
        slot = OUT.at[k, x]
        far = rc(slot, slot, PX[2], recv=idx, cond=(s == l))
        near = [rc(FS, slot, PX[j], recv=idx, cond=(s != l)) for j in range(2)]

        @pl.when(s == l)
        def _():
            for rows, value in sums:
                OUT[k, x, rows] = value
            far.start()

        @pl.when(s != l)
        def _():
            for rows, value in sums:
                FS[rows] = value
            for desc in near:
                desc.start()
        rs[l, name, 4] = idx

    def rs4(l, name):
        got = rs[l, name, 4]
        ref = OUTd.at[k] if name == "d" else GRAD[name][4].at[k]
        fin = rc(ref, ref, SIB, cond=(s == l))

        @pl.when(s == l)
        def _():
            if name == "d":
                @pl.when(z != x)
                def _():
                    got.wait_recv()
            else:
                wait_bytes(GRAD[name][4].at[k, pl.ds(0, 3)], got)
            fin.start()
        rs[l, name, 5] = fin

    def rs5(l, name):
        @pl.when(s == l)
        def _():
            rs[l, name, 5].wait_recv()

    landed = {}

    def edge(l, a, value):
        if l not in landed:
            landed[l] = new_recv()
        goal = 2 * a + l
        ED[l, a] = value

        @pl.when(x == goal)
        def _():
            TT[l, x] = value

        for j in range(3):
            desc = rc(ED.at[l, a], TT.at[l, x], PX[j], recv=landed[l], cond=(X3[j] == goal))

            @pl.when(X3[j] == goal)
            def _(desc=desc):
                desc.start()

    swaps = {}

    def edge_swap(l):
        swaps[l] = rc(TT.at[l, pl.ds(2 * (1 - k), 2)], EO.at[k], SIB, cond=(s == l))

        @pl.when(s == l)
        def _():
            wait_bytes(TT.at[l, pl.ds(0, 3)], landed[l])
            swaps[l].start()
            EO[k] = TT[l, pl.ds(2 * k, 2)]

    def edge_done(l):
        @pl.when(s == l)
        def _():
            swaps[l].wait_recv()

    e0 = lengths[k, 0, 0]
    e1 = e0 + lengths[k, 0, 1]
    def doc(i):
        return jnp.where(i >= e0, 1, 0) + jnp.where(i >= e1, 1, 0)

    def keys(a):
        return TH * (a + 1)

    def allowed(a):
        qi = lax.broadcasted_iota(jnp.int32, (TH, keys(a)), 0) + TH * a
        ki = lax.broadcasted_iota(jnp.int32, (TH, keys(a)), 1)
        return (doc(qi) == doc(ki)) & (ki <= qi)

    def head(value, hh):
        lane = lax.broadcasted_iota(jnp.int32, value.shape, 1)
        return jnp.where((lane < 64) if hh == 0 else (lane >= 64), value, jnp.zeros_like(value))

    def make_angles():
        row = lax.broadcasted_iota(jnp.int32, (T, T), 0)
        ki = lax.broadcasted_iota(jnp.int32, (T, T), 1)
        lane = lax.broadcasted_iota(jnp.int32, (T, 128), 1)
        start = jnp.where(row >= e1, e1, jnp.where(row >= e0, e0, 0))
        pick = jnp.where(ki == row - start, 1.0, 0.0).astype(BF)
        cos = dot(pick, angles[:, 0:128]) + dot(pick, angles[:, 128:256])
        sin = dot(pick, angles[:, 256:384]) + dot(pick, angles[:, 384:512])
        first = (lane < 32) | ((lane >= 64) & (lane < 96))
        CS[0] = cos
        CS[1] = jnp.where(first, -sin, 0.0)
        CS[2] = jnp.where(first, 0.0, sin)

    def turn(v, sign, a):
        r = rows_of(a)
        tiles = []
        for t in range(2):
            u = v[:, 128 * t : 128 * (t + 1)]
            rot = pltpu.roll(u, 96, 1) * CS[1, r] + pltpu.roll(u, 32, 1) * CS[2, r]
            tiles.append(u * CS[0, r] + rot if sign > 0 else u * CS[0, r] - rot)
        return jnp.concatenate(tiles, axis=1)

    def gain(l, i):
        tiles = []
        for t in range(8):
            a = Gn[t // 2, 2 * (t % 2), l].astype(F32) + Gn[t // 2, 2 * (t % 2) + 1, l].astype(F32)
            tiles.append(a[i : i + 1])
        return jnp.concatenate(tiles, axis=1)

    def norm_rows(ref, out, g, a):
        for b in range(2):
            r = pl.ds(TH * a + 64 * b, 64)
            v = ref[r, :].astype(F32)
            inv = lax.rsqrt(jnp.mean(v * v, axis=-1, keepdims=True) + EPS)
            out[r, :] = (v * inv * g).astype(BF)

    def wq(l):
        return Wq[l].reshape(D, 768)

    def project(l, XR, a):
        r = rows_of(a)
        norm_rows(XR, N1.at[l], gain(l, 0), a)
        n = N1[l, r]
        w = wq(l)
        QKV[l, 0, r] = turn(dot(n, w[:, 0:256]), 1, a).astype(BF)
        QKV[l, 1, r] = turn(dot(n, w[:, 256:512]), 1, a).astype(BF)
        v = dot(n, w[:, 512:768])
        if l == 1:
            v = 0.5 * v + 0.5 * QKV[0, 2, r].astype(F32)
        QKV[l, 2, r] = v.astype(BF)

    def attend(l, a):
        ok = allowed(a)
        r, nk = rows_of(a), keys(a)
        for t in range(2):
            cols = pl.ds(128 * t, 128)
            qt, kt, vt = QKV[l, 0, r, cols], QKV[l, 1, 0:nk, cols], QKV[l, 2, 0:nk, cols]
            acc = jnp.zeros((TH, 128), F32)
            for hh in range(2):
                sc = jnp.where(ok, dot_nt(head(qt, hh), kt) * 0.125, -1e30)
                ex = jnp.exp(sc - jnp.max(sc, axis=-1, keepdims=True))
                pr = (ex / jnp.sum(ex, axis=-1, keepdims=True)).astype(BF)
                PR[l, 2 * t + hh, r, 0:nk] = pr
                acc = acc + dot(pr, head(vt, hh))
            O[l, x, r, cols] = acc.astype(BF)
        return Share(O.at[l, x, r], O.at[l, pl.ds(0, 3), r])

    def feed(l, XR, got, i, a):
        r = rows_of(a)
        got.c()
        o = jnp.concatenate([O[l, b, r] for b in range(4)], axis=1)
        H[l, r] = XR[r, :].astype(F32) + dot(o, Wo[l].reshape(D, D))
        norm_rows(H.at[l], N2.at[l], gain(l, 1), a)
        if a == 0:
            ag_done(l, "gu")
        n = N2[l, r]
        GU[l, 0, r] = dot(n, Wgu[l, :, :, :, 0:FP].reshape(D, FP))
        GU[l, 1, r] = dot(n, Wgu[l, :, :, :, FP : 2 * FP].reshape(D, FP))
        for b in range(2):
            q = pl.ds(TH * a + 64 * b, 64)
            ga, up = GU[l, 0, q, :], GU[l, 1, q, :]
            M[l, q, :] = (ga * jax.nn.sigmoid(ga) * up).astype(BF)
        if a == 0:
            ag_done(l, "d")
        return Meet(i, a, dot(M[l, r], Wd[l]).astype(BF))

    def gain_grad(i, row, ref):
        total = jnp.zeros((1, D), F32)
        for a in range(2):
            for j in range(4):
                v = ref[pl.ds(TH * a + BH * j, BH), :].astype(F32)
                inv = lax.rsqrt(jnp.mean(v * v, axis=-1, keepdims=True) + EPS)
                total = total + jnp.sum(PS[i, a, j].astype(F32) * (v * inv), axis=0, keepdims=True)
        GS[0, row : row + 1] = total

    def back_ff(l, DY, i, a):
        r = rows_of(a)
        dm = dot_nt(DY[r, :], Wd[l])
        ga, up = GU[l, 0, r], GU[l, 1, r]
        sg = jax.nn.sigmoid(ga)
        DGU[l, 0, r] = (dm * up * sg * (1.0 + ga * (1.0 - sg))).astype(BF)
        DGU[l, 1, r] = (dm * ga * sg).astype(BF)
        part = (dot_nt(DGU[l, 0, r], Wgu[l, :, :, :, 0:FP].reshape(D, FP))
                + dot_nt(DGU[l, 1, r], Wgu[l, :, :, :, FP : 2 * FP].reshape(D, FP))).astype(BF)
        return Meet(i, a, part)

    def grads_d(l, DY, msib, dysib):
        wait_recv([msib, dysib])
        Gd[l] = (dot_tn(M[l], DY[:, half(D)]) + dot_tn(Ms[l], DYs[l])).astype(BF)
        r1a(l, "d")

    def grads_gu(l, nsib, gsib):
        wait_recv([nsib, gsib])
        grad_ref("gu", l)[...] = (dot_tn(N2[l], DGU[l, k]) + dot_tn(N2s[l], DGUs[l])).astype(BF).reshape(4, 4, SH, FP)
        r1a(l, "gu")

    def back_hidden(l, DY, got, a):
        dn = got.c()
        hf = H[l, own(a), :]
        inv = lax.rsqrt(jnp.mean(hf * hf, axis=-1, keepdims=True) + EPS)
        e = dn * gain(l, 1)
        dh = DY[own(a), :].astype(F32) + inv * e - hf * (inv * inv * inv) * jnp.mean(e * hf, axis=-1, keepdims=True)
        DH[l, a] = dh
        DHB[l, own(a), :] = dh.astype(BF)
        return share_rows(DHB.at[l], a)

    def back_attend(l, got, i, a):
        r, nk = rows_of(a), keys(a)
        got.c()
        do = dot_nt(DHB[l, r], Wo[l, x].reshape(HX, D)).astype(BF)
        dqs, dks, dvs = [], [], []
        for t in range(2):
            cols = pl.ds(128 * t, 128)
            qt, kt, vt = QKV[l, 0, r, cols], QKV[l, 1, 0:nk, cols], QKV[l, 2, 0:nk, cols]
            dot_ = do[:, 128 * t : 128 * (t + 1)]
            dq = jnp.zeros((TH, 128), F32)
            dk = dv = jnp.zeros((nk, 128), F32)
            for hh in range(2):
                pr = PR[l, 2 * t + hh, r, 0:nk]
                pf = pr.astype(F32)
                dom = head(dot_, hh)
                dpp = dot_nt(dom, vt)
                ds = (pf * (dpp - jnp.sum(pf * dpp, axis=-1, keepdims=True))).astype(BF)
                dq = dq + dot(ds, head(kt, hh))
                dk = dk + dot_tn(ds, head(qt, hh))
                dv = dv + dot_tn(pr, dom)
            dqs.append(dq)
            dks.append(dk)
            dvs.append(dv)
        dq, dk, dv = (jnp.concatenate(v, axis=1) for v in (dqs, dks, dvs))
        if a == 1:
            KV0[0] = dk[0:TH]
            KV0[1] = dv[0:TH]
            dk, dv = dk[TH:], dv[TH:]
        else:
            dk, dv = dk + KV0[0], dv + KV0[1]
        DP[l, r, 0:256] = turn((dq * 0.125).astype(BF).astype(F32), -1, a).astype(BF)
        DP[l, r, 256:512] = turn((dk * 0.125).astype(BF).astype(F32), -1, a).astype(BF)
        if l == 1:
            DP[l, r, 512:768] = (0.5 * dv.astype(BF).astype(F32)).astype(BF)
        else:
            DP[l, r, 512:768] = (dv + DP[1, r, 512:768].astype(F32)).astype(BF)
        return Meet(i, a, dot_nt(DP[l, r], wq(l)).astype(BF))

    def grads_q(l, n1sib, psib):
        wait_recv([n1sib, psib])
        Gq[l] = (dot_tn(N1[l], DP[l, :, half(768)]) + dot_tn(N1s[l], DPs[l])).astype(BF).reshape(4, 4, SH, 384)
        r1a(l, "q")

    def push_heads(l):
        hs = pl.ds(pl.multiple_of(x * HX + (1 - k) * 128, 128), 128)
        return push(DHB.at[l, :, hs], DHBs.at[l], SIB)

    def grads_o(l, osib, hsib):
        wait_recv([osib, hsib])
        hs = pl.ds(pl.multiple_of(x * HX + k * 128, 128), 128)
        for b in range(4):
            Go[l, b] = (dot_tn(O[l, b], DHB[l, :, hs]) + dot_tn(Os[l, b], DHBs[l])).astype(BF).reshape(4, SH, 128)
        r1a(l, "o")

    def back_input(l, XR, got, a):
        dn = got.c()
        xf = XR[own(a), :].astype(F32)
        inv = lax.rsqrt(jnp.mean(xf * xf, axis=-1, keepdims=True) + EPS)
        e = dn * gain(l, 0)
        dx = DH[l, a] + inv * e - xf * (inv * inv * inv) * jnp.mean(e * xf, axis=-1, keepdims=True)
        return dx.astype(BF)

    def gsum_a(i, to):
        idx = new_recv()
        for j, t in enumerate(to):
            push(GS.at[i], GR.at[i, j], t, idx)
        return i, len(to), idx

    def gsum_b(sent_to):
        i, n, idx = sent_to
        wait_bytes(GR.at[i, pl.ds(0, n)], idx)
        total = GS[i]
        for j in range(n):
            total = total + GR[i, j]
        GS[i + 1] = total

    X0 = E.at[0]
    DY1 = E.at[1]
    GS[0] = jnp.zeros((8, D), F32)
    for l in range(2):
        Wd[l, FX:FP, :] = jnp.zeros((FP - FX, D), BF)
    s1a(0, "q")
    g1()
    s1a(0, "o")
    e_loc.wait()
    e_sib.wait_recv()
    mine2 = pl.ds(pl.multiple_of(xh * 128, 128), 128)
    e_got = push3([E.at[s, mine2]] * 3, [E.at[s, mine2]] * 3, PX)
    s2a(0, "q")
    s1a(0, "gu")
    s1a(0, "d")
    g2()
    s1b(0, "o")
    make_angles()
    s1b(0, "gu")
    s3(0, "q")
    s2a(0, "o")
    s2a(0, "gu")
    s1b(0, "d")
    s1a(1, "q")
    g3()
    wait_recv(e_got)
    s1a(1, "o")
    s1a(1, "gu")
    s1a(1, "d")
    s2a(0, "d")
    ag_done(0, "q")
    n1sib, osib, nsib, msib = [None, None], [None, None], [None, None], [None, None]
    project(0, X0, 0)
    g0 = attend(0, 0)
    s2b(0, "o")
    s2b(0, "gu")
    project(0, X0, 1)
    n1sib[0] = push(N1.at[0], N1s.at[0], SIB)
    g1 = attend(0, 1)
    dysib = [None, push(DY1.at[:, other_half(D)], DYs.at[1], SIB)]
    s3(0, "o")
    s2b(0, "d")
    for name in ("q", "o", "gu"):
        s1b(1, name)
    s3(0, "gu")
    s2a(1, "q")
    s1b(1, "d")
    s3(0, "d")
    s2a(1, "o")
    s2a(1, "gu")
    ag_done(0, "o")
    m0 = feed(0, X0, g0, 0, 0)
    s2b(1, "q")
    m1 = feed(0, X0, g1, 0, 1)
    osib[0] = push(O.at[0], Os.at[0], SIB)
    nsib[0] = push(N2.at[0], N2s.at[0], SIB)
    msib[0] = push(M.at[0], Ms.at[0], SIB)
    s2a(1, "d")
    s2b(1, "o")
    X1[own(0), :] = (m0.c() + H[0, own(0), :]).astype(BF)
    g0 = share_rows(X1, 0)
    s2b(1, "gu")
    X1[own(1), :] = (m1.c() + H[0, own(1), :]).astype(BF)
    g1 = share_rows(X1, 1)
    s3(1, "q")
    s2b(1, "d")
    s3(1, "o")
    g0.c()
    ag_done(1, "q")
    project(1, X1, 0)
    g0 = attend(1, 0)
    s3(1, "gu")
    s3(1, "d")
    early = close()
    g1.c()
    project(1, X1, 1)
    n1sib[1] = push(N1.at[1], N1s.at[1], SIB)
    g1 = attend(1, 1)
    ag_done(1, "o")
    y0 = feed(1, X1, g0, 1, 0)
    y1 = feed(1, X1, g1, 1, 1)
    osib[1] = push(O.at[1], Os.at[1], SIB)
    nsib[1] = push(N2.at[1], N2s.at[1], SIB)
    msib[1] = push(M.at[1], Ms.at[1], SIB)

    m1 = back_ff(1, DY1, 2, 1)
    m0 = back_ff(1, DY1, 2, 0)
    gsib = push(DGU.at[1, 1 - k], DGUs.at[1], SIB)
    grads_d(1, DY1, msib[1], dysib[1])
    g1 = back_hidden(1, DY1, m1, 1)
    g0 = back_hidden(1, DY1, m0, 0)
    grads_gu(1, nsib[1], gsib)
    r1b(1, "d")
    m1 = back_attend(1, g1, 3, 1)
    m0 = back_attend(1, g0, 3, 0)
    hsib = push_heads(1)
    psib = push(DP.at[1, :, other_half(768)], DPs.at[1], SIB)
    r1b(1, "gu")
    edge(1, 0, (y0.c() + H[1, own(0), :]).astype(BF))
    edge(1, 1, (y1.c() + H[1, own(1), :]).astype(BF))
    grads_q(1, n1sib[1], psib)
    DY0[own(1), :] = back_input(1, X1, m1, 1)
    g1 = share_rows(DY0, 1)
    DY0[own(0), :] = back_input(1, X1, m0, 0)
    g0 = share_rows(DY0, 0)
    r2a(1, "d")
    grads_o(1, osib[1], hsib)
    r2a(1, "gu")

    g1.c()
    m1 = back_ff(0, DY0, 4, 1)
    g0.c()
    m0 = back_ff(0, DY0, 4, 0)
    gsib = push(DGU.at[0, 1 - k], DGUs.at[0], SIB)
    dysib[0] = push(DY0.at[:, other_half(D)], DYs.at[0], SIB)
    r2b(1, "d")
    r1b(1, "q")
    flush(0, early)
    grads_d(0, DY0, msib[0], dysib[0])
    g1 = back_hidden(0, DY0, m1, 1)
    grads_gu(0, nsib[0], gsib)
    g0 = back_hidden(0, DY0, m0, 0)
    r1b(1, "o")
    r2b(1, "gu")
    m1 = back_attend(0, g1, 5, 1)
    m0 = back_attend(0, g0, 5, 0)
    hsib = push_heads(0)
    psib = push(DP.at[0, :, other_half(768)], DPs.at[0], SIB)
    r1b(0, "d")
    gain_grad(5, 0, X0)
    gain_grad(4, 1, H.at[0])
    gain_grad(3, 2, X1)
    gain_grad(2, 3, H.at[1])
    g = gsum_a(0, PX)
    r1b(0, "gu")
    grads_q(0, n1sib[0], psib)
    grads_o(0, osib[0], hsib)
    r2a(1, "q")
    r2a(1, "o")
    edge(0, 1, back_input(0, X0, m1, 1))
    edge(0, 0, back_input(0, X0, m0, 0))
    rs3(1, "d")
    r2a(0, "d")
    gsum_b(g)
    g = gsum_a(1, PY)
    r2a(0, "gu")
    r2a(0, "q")
    r2a(0, "o")
    edge_swap(0)
    r2b(0, "d")
    rs3(1, "gu")
    gsum_b(g)
    g = gsum_a(2, PZ)
    r2b(1, "q")
    r2b(1, "o")
    r2b(0, "gu")
    edge_swap(1)
    rs4(1, "d")
    rs3(0, "q")
    rs3(0, "o")
    rs3(0, "d")
    gsum_b(g)
    g = gsum_a(3, [SIB])
    rs3(1, "q")
    rs3(1, "o")
    rs3(0, "gu")
    rs4(1, "gu")
    rs4(0, "q")
    rs4(0, "o")
    rs4(0, "d")
    rs4(1, "q")
    rs4(1, "o")
    gsum_b(g)
    edge_done(0)
    edge_done(1)
    rs4(0, "gu")
    outs = []

    def put(a, b):
        outs.append(local(a, b))
        outs[-1].start()
    put(EO, edge_hbm)
    put(GS.at[4], gsum_hbm)
    for name, a, b in (("d", OUTd, od_hbm), ("q", OUTq, oq_hbm), ("o", OUTo, oo_hbm), ("gu", OUTgu, ogu_hbm)):
        rs5(1, name)
        rs5(0, name)
        put(a, b)
    flush(early, len(groups))
    flush_conditional()
    for o in outs:
        o.wait()
    assert counter[0] <= N_RECV and counter[1] <= N_LOC and counter[2] <= N_SEND, counter


def epilogue(*refs):
    given, (edges, qkv, out, gate, up, down, gg), held, sem = refs[:6], refs[6:13], refs[13:19], refs[19]
    copies = [pltpu.make_async_copy(a, b, sem.at[i]) for i, (a, b) in enumerate(zip(given, held))]
    for cp in copies:
        cp.start()
    for cp in copies:
        cp.wait()
    oq, oo, ogu, od, edge, gsum = held
    s = lax.axis_index("section")
    dp = lax.axis_index("dp")
    edges[0, :, 0] = edge[...].reshape(2, BT, D)
    for x in range(4):
        a, b = oq[0, x].astype(F32), oq[1, x].astype(F32)
        qkv[0, :, HX * x : HX * (x + 1)] = a[:, 0:256]
        qkv[0, :, D + HX * x : D + HX * x + 128] = a[:, 256:384]
        qkv[0, :, D + HX * x + 128 : D + HX * (x + 1)] = b[:, 0:128]
        qkv[0, :, 2 * D + HX * x : 2 * D + HX * (x + 1)] = b[:, 128:384]
        for h in range(2):
            out[0, :, HX * x + 128 * h : HX * x + 128 * (h + 1)] = oo[h, x].astype(F32)
    for h, ref in ((0, gate), (1, up)):
        for p in range(2):
            a = ogu[h, 2 * p].astype(F32)
            b = pltpu.roll(ogu[h, 2 * p + 1].astype(F32), 64, 1)
            c = 2 * FX * p
            ref[0, :, c : c + 640] = a[:, 0:640]
            ref[0, :, c + 640 : c + 768] = a[:, 640:768] + b[:, 0:128]
            ref[0, :, c + 768 : c + 2 * FX] = b[:, 128:768]
    for h in range(2):
        down[0, :, 512 * h : 512 * (h + 1)] = od[h].astype(F32)
    tile = gsum[:, pl.ds(pl.multiple_of(128 * lax.div(dp, 2), 128), 128)]
    tile = jnp.where(lax.rem(dp, 2) == 1, pltpu.roll(tile, 64, 1), tile)
    rows = jnp.where(s == 1, tile[2:4], tile[0:2])
    gg[0] = rows[:, 0:SH]


def run_kernel(lengths, ends, qkv_w, out_w, gate_w, up_w, down_w, gains, angles):
    V = pltpu.VMEM
    sh = jax.ShapeDtypeStruct
    any_ = pl.BlockSpec(memory_space=pl.ANY)
    vm = pl.BlockSpec(memory_space=pltpu.VMEM)
    out_shape = [
        sh((2, 4, SH, 384), BF), sh((2, 4, SH, 128), BF), sh((2, 4, SH, FP), BF), sh((2, DR, 512), BF),
        sh((2, 2, BH, D), BF), sh((8, D), F32), sh((GROUP_BYTES // 4096, 16, 128), BF),
    ]
    scratch = [
        V((2, 4, 4, SH, 768), BF), V((2, 4, 4, SH, D), BF), V((2, 4, 4, SH, 2 * FP), BF), V((2, FP, D), BF),
        V((4, 4, 2, 16, 128), BF),
        V((2, T, D), BF), V((T, D), BF), V((T, D), BF),
        V((2, T, D), BF), V((2, T, D), BF), V((2, T, D), BF), V((2, T, D), BF),
        V((2, T, D), F32), V((2, 3, T, HX), BF), V((2, 4, T, T), BF),
        V((2, 4, T, HX), BF), V((2, 4, T, HX), BF),
        V((2, 2, T, FP), F32), V((2, T, FP), BF), V((2, T, FP), BF),
        V((2, 2, T, FP), BF), V((2, T, FP), BF),
        V((2, T, 768), BF), V((2, T, 384), BF),
        V((2, T, D), BF), V((2, T, 128), BF), V((2, T, 512), BF), V((2, 2, BH, D), F32),
        V((2, TH, HX), F32), V((2, 2, BH, D), BF),
        V((6, 2, 4, BH, D), BF), V((6, 2, 3, BH, D), BF),
        V((2, 4, 4, SH, 384), BF), V((2, 4, 4, SH, 128), BF), V((1, 4, 4, SH, FP), BF), V((2, FP, 512), BF),
        V((2, 3, 4, SH, 384), BF), V((2, 3, 4, SH, 128), BF), V((2, 3, 4, SH, FP), BF), V((2, 3, DR, 512), BF),
        V((2, 3, SH, 384), BF), V((2, 3, SH, 128), BF), V((2, 3, SH, FP), BF), V((2, 3, DR, 512), BF),
        V((2, 4, SH, 384), BF), V((2, 4, SH, 128), BF), V((2, 4, SH, FP), BF), V((2, DR, 512), BF),
        V((2, 4, SH, 384), BF), V((2, 4, SH, 128), BF), V((2, 4, SH, FP), BF), V((2, DR, 512), BF),
        V((SH, 384), BF), V((SH, 128), BF), V((SH, FP), BF), V((DR, 512), BF),
        V((5, 8, D), F32), V((4, 3, 8, D), F32), V((2, 4, BH, D), BF), V((2, 2, BH, D), BF),
        V((3, T, 128), F32), V((SH, 384), BF), V((SH, FP), BF), V((SH, 512), BF), V((DR, 512), BF),
        V((16, 128), BF), V((16, 128), F32),
        pltpu.SemaphoreType.DMA((N_SEND,)), pltpu.SemaphoreType.DMA((N_RECV,)), pltpu.SemaphoreType.DMA((N_LOC,)),
    ]
    return pl.pallas_call(
        kernel,
        out_shape=out_shape,
        in_specs=[pl.BlockSpec(memory_space=pltpu.SMEM)] + [any_] * 6 + [vm] * 2,
        out_specs=[any_] * 7,
        scratch_shapes=scratch,
        name="two_layers",
        compiler_params=pltpu.CompilerParams(
            collective_id=0, has_side_effects=True, vmem_limit_bytes=64 * 1024 * 1024 - 65536
        ),
    )(lengths, ends, qkv_w, out_w, gate_w, up_w, down_w, gains, angles)


def angle_table():
    pos = np.arange(T, dtype=np.float64)[:, None]
    freq = 10000.0 ** (-(np.arange(128) % 32) / 32.0)
    parts = []
    for v in (np.cos(pos * freq), np.sin(pos * freq)):
        high = v.astype(jnp.bfloat16)
        parts += [high, (v - high.astype(np.float64)).astype(jnp.bfloat16)]
    return np.concatenate(parts, axis=1)


def per_device(ends_in, lengths, qkv_w, out_w, gate_w, up_w, down_w, gains):
    oq, oo, ogu, od, edge, gsum, _ = run_kernel(
        lengths, ends_in, qkv_w, out_w, gate_w, up_w, down_w, gains, jnp.asarray(angle_table()))
    sh = jax.ShapeDtypeStruct
    return pl.pallas_call(
        epilogue,
        out_shape=[
            sh((1, 2, 1, BT, D), BF), sh((1, SH, 3 * D), F32), sh((1, SH, D), F32), sh((1, SH, FF), F32),
            sh((1, SH, FF), F32), sh((1, DR, D), F32), sh((1, 2, SH), F32),
        ],
        in_specs=[pl.BlockSpec(memory_space=pl.ANY)] * 6,
        out_specs=[pl.BlockSpec(memory_space=pltpu.VMEM)] * 7,
        scratch_shapes=[pltpu.VMEM(v.shape, v.dtype) for v in (oq, oo, ogu, od, edge, gsum)]
        + [pltpu.SemaphoreType.DMA((6,))],
        name="place_outputs",
        compiler_params=pltpu.CompilerParams(vmem_limit_bytes=63 * 1024 * 1024),
    )(oq, oo, ogu, od, edge, gsum)


def solution(mesh):
    in_specs = (
        P("section", None, "dp", "ctx", None),
        P(None, "dp", None),
        P("section", "dp", None),
        P("section", "dp", None),
        P("section", "dp", None),
        P("section", "dp", None),
        P("section", "dp", None),
        P("section", None, "dp"),
    )
    out_specs = (
        P("section", None, "dp", "ctx", None),
        P("section", "dp", None),
        P("section", "dp", None),
        P("section", "dp", None),
        P("section", "dp", None),
        P("section", "dp", None),
        P("section", None, "dp"),
    )
    return jax.shard_map(per_device, mesh=mesh, in_specs=in_specs, out_specs=out_specs, check_vma=False)
```
